128 devices in a mesh: row: 8 (over x, core), col: 16 (over y, z).
Axes of the slice: x: 4, y: 4, z: 4, core: 2. Of those that a mesh axis runs over, the one named last changes fastest.
Arguments:
- grad: float32 [16384, 1024], P('col', 'row'), may hold values from -6 to 6
- moment: float32 [16384, 1024], P('col', 'row'), may hold values from -6 to 6
- second: float32 [16384, 1024], P(('row', 'col')), may hold values from 1 to 10
- left_basis: float32 [16384, 16384], P('col', 'row'), as said below
- right_basis: float32 [1024, 1024], replicated, may hold values from -0.1875 to 0.1875
Outputs:
- update: float32 [16384, 1024], P('col', 'row')
- moment_new: float32 [16384, 1024], P('col', 'row')
- second_new: float32 [16384, 1024], P(('row', 'col'))
The draws below stay inside these ranges and needn't reach their ends.
Inputs may be any that keep to these rules, and one draw needn't show every extreme that they name: left_basis is a dense real matrix whose columns have length close to one.
All inputs are finite; a program needn't handle non-finite values.
Results may differ from the reference program's by a relative error of at most 0.00007.
Values sent between devices are 32-bit elements; how exact they have to be, the bound alone decides.
No kernel may reach another device: no remote copies, remote signals or barrier semaphores. Data moves between devices by JAX's collectives and lax.ppermute only.
A program may use at most 128 MiB of HBM per device.

```python
import math
import jax
import jax.numpy as jnp
from jax import lax

M = 16384
N = 1024


def draw_left_basis(key, part):
    key = jax.random.fold_in(key, 7)
    base = jnp.clip(jax.random.normal(key, (M, M), jnp.float32), -6.0, 6.0)
    return (base / jnp.sqrt(jnp.float32(M))).astype(jnp.float32)


def block_levels(rng, extent, cuts, least, top_value):
    level, own = 1.0, jax.random.fold_in(rng, 6)
    for position, shards_of in cuts:
        draws = jnp.exp(jax.random.uniform(jax.random.fold_in(own, position), (shards_of,), jnp.float32, least / len(cuts), top_value / len(cuts)))
        level = level * jnp.repeat(draws, extent[position] // shards_of).reshape([-1 if axis == position else 1 for axis in range(len(extent))])
    return level


def gaussian(stream_key, dims, spread, bound, split=(), held_as=jnp.bfloat16):
    factor_of = block_levels(stream_key, dims, split, -0.22, 0.18) if split else 1.0
    result = jax.random.normal(stream_key, dims, jnp.float32) * spread * factor_of
    return jnp.minimum(jnp.maximum(result, -bound), bound).astype(held_as)


def setup_inputs(seed: int = 0) -> dict:
    key_of = jax.random.split(jax.random.key(seed), 6)
    grad = gaussian(key_of[0], (M, N), 1.0, 6.0, ((0, 16), (1, 8)), jnp.float32)
    moment = gaussian(key_of[1], (M, N), 1.0, 6.0, ((0, 16), (1, 8)), jnp.float32)
    second = jnp.clip(jnp.exp(math.log(10.0) - 2.3025851 * jax.random.uniform(key_of[2], (M, N), jnp.float32) ** block_levels(key_of[2], (M, N), ((0, 128),), -0.2, 0.2)), 1.0, 10.0)
    left_basis = draw_left_basis(jax.random.fold_in(key_of[5], 71), 0)
    right_basis = gaussian(key_of[4], (N, N), N ** -0.5, 0.1875, (), jnp.float32)
    return dict(grad=grad, moment=moment, second=second, left_basis=left_basis, right_basis=right_basis)


first_decay = 0.9
second_decay = 0.95
epsilon = 1e-08
clip_share = 0.25

def reference(grad, moment, second, left_basis, right_basis):
    highest = lax.Precision.HIGHEST
    moment_new = first_decay * moment + (1.0 - first_decay) * grad
    grad_rot = jnp.dot(jnp.dot(left_basis.T, grad, precision=highest), right_basis, precision=highest)
    mom_rot = jnp.dot(jnp.dot(left_basis.T, moment_new, precision=highest), right_basis, precision=highest)
    second_new = second_decay * second + (1.0 - second_decay) * grad_rot * grad_rot
    rotated = mom_rot / (jnp.sqrt(second_new) + epsilon)
    total = jnp.sum(rotated * rotated)
    factor = jnp.minimum(1.0, clip_share * jnp.sqrt(jnp.float32(M * N)) / (jnp.sqrt(total) + 1e-06))
    back = jnp.dot(rotated, right_basis.T, precision=highest)
    update = factor * jnp.dot(left_basis, back, precision=highest)
    return (update, moment_new, second_new)
```

```python
import jax
import jax.numpy as jnp
from jax import lax
from jax.sharding import PartitionSpec as P

M = 16384
N = 1024


first_decay = 0.9
second_decay = 0.95
epsilon = 1e-08
clip_share = 0.25


def total_over_devices(value):
    for axis, size in (("row", 8), ("col", 16)):
        bit = 1
        while bit < size:
            value = value + lax.ppermute(value, axis, [(i, i ^ bit) for i in range(size)])
            bit *= 2
    return value


def local(grad, moment, second, left_basis, right_basis):
    high = lax.Precision.HIGH
    moment_new = first_decay * moment + (1.0 - first_decay) * grad
    stacked = jnp.stack([grad, moment_new], axis=0)
    partial_sums = jnp.einsum(
        "ki,skw->siw",
        left_basis,
        lax.all_gather(stacked, "row", axis=2, tiled=True),
        precision=high,
    )
    shares = lax.psum_scatter(partial_sums, "col", scatter_dimension=1, tiled=True)
    shares = jnp.einsum("sij,jn->sin", shares, right_basis, precision=high)
    grad_rot = shares[0]
    mom_rot = shares[1]
    second_new = second_decay * second + (1.0 - second_decay) * grad_rot * grad_rot
    rotated = mom_rot / (jnp.sqrt(second_new) + epsilon)
    back = lax.dot_general(rotated, right_basis, (((1,), (1,)), ((), ())), precision=high)
    block_rows = lax.all_gather(back, "col", axis=0, tiled=True)
    squares = jnp.sum((rotated * rotated).reshape(16, 8, 8, 128), axis=(0, 2))
    total = jnp.sum(total_over_devices(squares))
    factor = jnp.minimum(1.0, clip_share * jnp.sqrt(jnp.float32(M * N)) / (jnp.sqrt(total) + 1e-06))
    flipped = lax.psum_scatter(
        lax.dot_general(block_rows, left_basis, (((0,), (1,)), ((), ())), precision=high),
        "row",
        scatter_dimension=0,
        tiled=True,
    )
    update = flipped.T * factor
    return (update, moment_new, second_new)


def solution(mesh):
    return jax.shard_map(
        local,
        mesh=mesh,
        in_specs=(P("col", "row"), P("col", "row"), P(("row", "col"), None), P("col", "row"), P()),
        out_specs=(P("col", "row"), P("col", "row"), P(("row", "col"), None)),
        check_vma=False,
    )
```

```python
import functools

import jax
import jax.numpy as jnp
from jax import lax
from jax.experimental import pallas as pl
from jax.experimental.pallas import tpu as pltpu
from jax.sharding import PartitionSpec as P

M = 16384
N = 1024

first_decay = 0.9
second_decay = 0.95
epsilon = 1e-08
clip_share = 0.25

f32, bf16 = jnp.float32, jnp.bfloat16
BOTH = ("row", "col")
VMEM_LIMIT = 40 * 1024 * 1024


def call(kernel, grid, in_specs, out_specs, out_shape, scratch=(), flops=0, moved=0, aliases=None, prefetch=0, name=None):
    return pl.pallas_call(
        kernel,
        grid_spec=pltpu.PrefetchScalarGridSpec(
            num_scalar_prefetch=prefetch, grid=grid, in_specs=in_specs, out_specs=out_specs, scratch_shapes=list(scratch)
        ),
        out_shape=out_shape,
        input_output_aliases=aliases or {},
        compiler_params=pltpu.CompilerParams(vmem_limit_bytes=VMEM_LIMIT, dimension_semantics=("arbitrary",) * len(grid)),
        cost_estimate=pl.CostEstimate(flops=flops, bytes_accessed=moved, transcendentals=0),
        name=name,
    )


def shape(rows, columns, dtype=f32):
    return jax.ShapeDtypeStruct((rows, columns), dtype)


def split(value):
    high = value.astype(bf16)
    return high, (value - high.astype(f32)).astype(bf16)


def dot3(a_high, a_low, b_high, b_low, dims=(((1,), (0,)), ((), ()))):
    d = functools.partial(lax.dot_general, dimension_numbers=dims, preferred_element_type=f32)
    return d(a_high, b_high) + (d(a_high, b_low) + d(a_low, b_high))


def move(value, step):
    pairs = []
    for x in range(4):
        for c in range(2):
            for y in range(4):
                for z in range(4):
                    tx, tc, ty, tz = step(x, c, y, z)
                    pairs.append(((2 * x + c) * 16 + 4 * y + z, (2 * (tx % 4) + tc) * 16 + 4 * (ty % 4) + tz % 4))
    return lax.ppermute(value, BOTH, pairs)


def swap(value):
    return move(value, lambda x, c, y, z: (x, 1 - c, y, z))


def along_x(value, d):
    return move(value, lambda x, c, y, z: (x + d, c, y, z))


def first(value, d):
    return move(value, lambda x, c, y, z: (x, c, y + d, z) if c == 0 else (x, c, y, z + d))


def second_axis(value, d):
    return move(value, lambda x, c, y, z: (x, c, y, z + d) if c == 0 else (x, c, y + d, z))


def start(core, grad, moment):
    def kernel(core_ref, grad_ref, moment_ref, new_ref, keep_ref, give_ref):
        g = grad_ref[...]
        new = first_decay * moment_ref[...] + (1.0 - first_decay) * g
        new_ref[...] = new
        g, new = g.T, new.T
        zero = core_ref[0] == 0
        keep_ref[...] = jnp.where(zero, g, new)
        give_ref[...] = jnp.where(zero, new, g)

    block = pl.BlockSpec((256, 128), lambda t, c: (t, 0))
    turned = pl.BlockSpec((128, 256), lambda t, c: (0, t))
    return call(
        kernel, (4,), [block, block], [block, turned, turned], [shape(1024, 128), shape(128, 1024), shape(128, 1024)],
        moved=3 * 2**20, flops=10**6, prefetch=1, name="start",
    )(core, grad, moment)


def order_left(order, left, half, held=None):
    def kernel(order_ref, left_ref, *refs):
        high_ref, low_ref = refs[-2:]
        high, low = split(left_ref[...])
        high_ref[...] = high
        low_ref[...] = low

    out = pl.BlockSpec((1024, 128), lambda a, b, o: (0, a * 8 + half * 4 + b))
    anywhere = pl.BlockSpec(memory_space=pl.ANY)
    more = [] if held is None else list(held)
    return call(
        kernel, (4, 4), [pl.BlockSpec((1024, 128), lambda a, b, o: (0, o[a * 4 + b]))] + [anywhere] * len(more),
        [out, out], [shape(1024, 4096, bf16)] * 2, moved=16 * 2**20, flops=10**7,
        aliases={2: 0, 3: 1} if more else None, prefetch=1, name="order_left",
    )(order, left, *more)


def order_right(order, right):
    def kernel(order_ref, right_ref, high_ref, low_ref):
        high, low = split(right_ref[...])
        high_ref[...] = high
        low_ref[...] = low

    out = pl.BlockSpec((128, 1024), lambda a, o: (a, 0))
    return call(
        kernel, (8,), [pl.BlockSpec((128, 1024), lambda a, o: (o[a], 0))], [out, out], [shape(1024, 1024, bf16)] * 2,
        moved=8 * 2**20, flops=10**6, prefetch=1, name="order_right",
    )(order, right)


def project(blocks, left, d, more=None, side=0, halves=False):
    rows = sum(b.shape[0] for b in blocks)
    n = len(blocks)

    def kernel(*refs):
        g_refs, (lh, ll) = refs[:n], refs[n : n + 2]
        gh, gl = refs[-2:]
        outs = refs[n + 2 + (more is not None) : -2]
        t = pl.program_id(0)

        @pl.when(t == 0)
        def _():
            at = 0
            for g in g_refs:
                size = g.shape[0]
                gh[at : at + size, :], gl[at : at + size, :] = split(g[...])
                at += size

        value = dot3(gh[...], gl[...], lh[...], ll[...])
        if halves:

            @pl.when(t < 2)
            def _():
                outs[0][...] = value

            @pl.when(t >= 2)
            def _():
                outs[1][...] = value

        elif more is not None:
            here = t < 2 if side == 0 else t >= 2

            @pl.when(here)
            def _():
                outs[0][...] = value + refs[n + 2][...]

            @pl.when(jnp.logical_not(here))
            def _():
                outs[0][...] = value

        else:
            outs[0][...] = value

    column = pl.BlockSpec((1024, 256), lambda t: (0, d * 4 + t))
    in_specs = [pl.BlockSpec(b.shape, lambda t: (0, 0)) for b in blocks] + [column, column]
    args = list(blocks) + list(left)
    low = pl.BlockSpec((rows, 256), lambda t: (0, jnp.minimum(t, 1)))
    high = pl.BlockSpec((rows, 256), lambda t: (0, jnp.maximum(t - 2, 0)))
    if more is not None:
        in_specs.append(high if side else low)
        args.append(more)
    if halves:
        out_specs, out_shape = [low, high], [shape(rows, 512)] * 2
    else:
        out_specs, out_shape = pl.BlockSpec((rows, 256), lambda t: (0, t)), shape(rows, 1024)
    return call(
        kernel, (4,), in_specs, out_specs, out_shape, [pltpu.VMEM((rows, 1024), bf16)] * 2,
        flops=6 * rows * 2**20, moved=4 * 2**20 + rows * 8192, name=f"project{d}",
    )(*args)


def settle(own, one, two):
    rows = own.shape[0]

    def kernel(a, b, c, *outs):
        value = a[...] + b[...] + c[...]
        for d, out in enumerate(outs):
            out[:, :128] = value[:, d * 128 : d * 128 + 128]
            out[:, 128:] = value[:, 512 + d * 128 : 640 + d * 128]

    block = pl.BlockSpec((128, 1024), lambda t: (t, 0))
    return call(
        kernel, (rows // 128,), [block] * 3, [pl.BlockSpec((128, 256), lambda t: (t, 0))] * 4, [shape(rows, 256)] * 4,
        flops=2 * rows * 1024, moved=rows * 16384, name="settle",
    )(own, one, two)


def rotate(parts, right, chips, before=None):
    rows = parts[0].shape[0]
    last = before is not None

    def kernel(*refs):
        p, (rh, rl) = refs[:4], refs[4:6]
        th, tl = refs[-2:]
        t = pl.program_id(0)

        @pl.when(t == 0)
        def _():
            total = (p[0][...] + p[1][...]) + (p[2][...] + p[3][...])
            th[...], tl[...] = split(total.T)

        def pick(r):
            return jnp.concatenate([r[h * 512 + d * 128 : h * 512 + d * 128 + 128, :] for d in chips for h in range(2)], axis=0)

        value = dot3(th[...], tl[...], pick(rh), pick(rl))
        if last:
            value = value + refs[6][...]
            refs[7][...] = value[:128]
            refs[8][...] = value[128:]
        else:
            refs[6][...] = value

    part = pl.BlockSpec((rows, 256), lambda t: (0, 0))
    column = pl.BlockSpec((1024, 256), lambda t: (0, t))
    tall = pl.BlockSpec((256, 256), lambda t: (0, t))
    flat = pl.BlockSpec((128, 256), lambda t: (0, t))
    return call(
        kernel, (4,), [part] * 4 + [column] * 2 + ([tall] if last else []),
        [flat, flat] if last else tall, [shape(128, 1024)] * 2 if last else shape(256, 1024),
        [pltpu.VMEM((256, rows), bf16)] * 2, flops=6 * 256 * rows * 1024, moved=8 * 2**20, name="rotate",
    )(*parts, *right, *([before] if last else []))


def turn(core, own, other, second, right):
    def kernel(core_ref, own_ref, other_ref, second_ref, rh, rl, new_ref, keep_ref, give_ref, sum_ref, th, tl):
        t = pl.program_id(0)

        @pl.when(t == 0)
        def _():
            zero = core_ref[0] == 0
            a, b = own_ref[...], other_ref[...]
            g, m = jnp.where(zero, a, b), jnp.where(zero, b, a)
            new = second_decay * second_ref[...] + (1.0 - second_decay) * g * g
            new_ref[...] = new
            rotated = m / (jnp.sqrt(new) + epsilon)
            th[...], tl[...] = split(rotated)
            squares = rotated * rotated
            total = squares[0:8, :]
            for i in range(1, 16):
                total = total + squares[i * 8 : i * 8 + 8, :]
            narrow = total[:, 0:128]
            for i in range(1, 8):
                narrow = narrow + total[:, i * 128 : i * 128 + 128]
            sum_ref[...] = narrow

        value = dot3(th[...], tl[...], rh[...], rl[...], (((1,), (1,)), ((), ())))

        @pl.when(t < 2)
        def _():
            keep_ref[...] = value

        @pl.when(t >= 2)
        def _():
            give_ref[...] = value

    whole = pl.BlockSpec((128, 1024), lambda t, c: (0, 0))
    rows = pl.BlockSpec((256, 1024), lambda t, c: (t, 0))
    return call(
        kernel, (4,), [whole, whole, whole, rows, rows],
        [
            whole,
            pl.BlockSpec((128, 256), lambda t, c: (0, jnp.minimum(t, 1))),
            pl.BlockSpec((128, 256), lambda t, c: (0, jnp.maximum(t - 2, 0))),
            pl.BlockSpec((8, 128), lambda t, c: (0, 0)),
        ],
        [shape(128, 1024), shape(128, 512), shape(128, 512), shape(8, 128)],
        [pltpu.VMEM((128, 1024), bf16)] * 2, flops=6 * 128 * 2**20, moved=7 * 2**20, prefetch=1, name="turn",
    )(core, own, other, second, *right)


def back_project(terms, left, before=None, cut=False):
    arrays = [a for _, group in terms for a in group]
    n, g = len(arrays), len(terms)

    def kernel(*refs):
        s_refs, l_refs = refs[:n], refs[n : n + 2 * g]
        sh, sl = refs[-2:]
        outs = refs[n + 2 * g + (before is not None) : -2]
        t = pl.program_id(0)

        @pl.when(t == 0)
        def _():
            at = 0
            for s in s_refs:
                size = s.shape[0]
                sh[at : at + size, :], sl[at : at + size, :] = split(s[...])
                at += size

        value = refs[n + 2 * g][...] if before is not None else None
        for i in range(g):
            rows = slice(i * 1024, i * 1024 + 1024)
            new = dot3(l_refs[2 * i][...], l_refs[2 * i + 1][...], sh[rows, :], sl[rows, :])
            value = new if value is None else value + new
        if cut:
            for d, out in enumerate(outs):
                out[...] = value[:, d * 128 : d * 128 + 128]
        else:
            outs[0][...] = value

    wide = pl.BlockSpec((256, 512), lambda t: (t, 0))
    in_specs = [pl.BlockSpec(a.shape, lambda t: (0, 0)) for a in arrays]
    args = list(arrays)
    for d, _ in terms:
        in_specs += [pl.BlockSpec((256, 1024), lambda t, d=d: (t, d))] * 2
        args += list(left)
    if before is not None:
        in_specs.append(wide)
        args.append(before)
    if cut:
        out_specs, out_shape = [pl.BlockSpec((256, 128), lambda t: (t, 0))] * 4, [shape(1024, 128)] * 4
    else:
        out_specs, out_shape = wide, shape(1024, 512)
    return call(
        kernel, (4,), in_specs, out_specs, out_shape, [pltpu.VMEM((1024 * g, 512), bf16)] * 2,
        flops=6 * g * 2**29, moved=(6 * g + 4) * 2**20, name="back_project",
    )(*args)


def scatter_sum(blocks, left):
    two_a, two_b = project(blocks, left, 2, halves=True)
    near = first(two_a, 1)
    far = first(two_b, -1)
    own = project(blocks, left, 0)
    up = first(project(blocks, left, 1, near, 0), 1)
    down = first(project(blocks, left, 3, far, 1), -1)
    q = settle(own, up, down)
    return [q[0], second_axis(q[1], 1), second_axis(q[3], -1), second_axis(q[2], 2)]


def local(grad, moment, second, left_basis, right_basis):
    row, col = lax.axis_index("row"), lax.axis_index("col")
    x, c, y, z = row // 2, row % 2, col // 4, col % 4
    core = c.reshape(1).astype(jnp.int32)
    a, b = jnp.arange(4)[:, None], jnp.arange(4)[None, :]
    u, v = jnp.where(c == 0, y, z), jnp.where(c == 0, z, y)
    u, v = (u + a) % 4, (v + b) % 4
    order = jnp.where(c == 0, u * 4 + v, v * 4 + u).reshape(16).astype(jnp.int32)
    halves, chips = jnp.arange(2)[:, None], jnp.arange(4)[None, :]
    order_r = (2 * ((x + chips) % 4) + (c + halves) % 2).reshape(8).astype(jnp.int32)

    moment_new, keep, give = start(core, grad, moment)
    mine = jnp.concatenate([keep, swap(give)], axis=0)
    left_other = swap(left_basis)
    plus = along_x(mine, -1)
    minus = along_x(mine, 1)
    left = order_left(order, left_basis, 0)
    right = order_right(order_r, right_basis)
    left = order_left(order, left_other, 1, left)
    far_a = along_x(plus[:128], -1)
    far_b = along_x(minus[128:], 1)

    z0 = scatter_sum([mine, plus], left)
    z1 = scatter_sum([minus, far_a, far_b], left)
    part = rotate(z0, right, (0, 1))
    own, other = rotate(z1, right, (3, 2), part)
    other = swap(other)

    second_new, keep, give, squares = turn(core, own, other, second, right)
    share = jnp.stack([keep, swap(give)], axis=0)
    for step in (
        lambda x, c, y, z: (x, 1 - c, y, z),
        lambda x, c, y, z: (x ^ 1, c, y, z),
        lambda x, c, y, z: (x ^ 2, c, y, z),
        lambda x, c, y, z: (x, c, y ^ 1, z),
        lambda x, c, y, z: (x, c, y ^ 2, z),
        lambda x, c, y, z: (x, c, y, z ^ 1),
        lambda x, c, y, z: (x, c, y, z ^ 2),
    ):
        squares = squares + move(squares, step)
    total = jnp.sum(squares)
    factor = jnp.minimum(1.0, clip_share * jnp.sqrt(jnp.float32(M * N)) / (jnp.sqrt(total) + 1e-06))

    shares = [share, second_axis(share, -1), second_axis(share, -2), second_axis(share, 1)]
    block = jnp.stack(shares, axis=1).reshape(1024, 512)
    plus = first(block, -1)
    minus = first(block, 1)
    far_a = first(plus[:512], -1)
    far_b = first(minus[512:], 1)
    sums = back_project([(0, [block])], left)
    sums = back_project([(1, [plus]), (3, [minus])], left, sums)
    u0, u1, u2, u3 = back_project([(2, [far_a, far_b])], left, sums, cut=True)
    update = ((u0 + along_x(u1, 1)) + (along_x(u3, -1) + along_x(u2, 2))) * factor
    return (update, moment_new, second_new)


def solution(mesh):
    return jax.shard_map(
        local,
        mesh=mesh,
        in_specs=(P("col", "row"), P("col", "row"), P(("row", "col"), None), P("col", "row"), P()),
        out_specs=(P("col", "row"), P("col", "row"), P(("row", "col"), None)),
        check_vma=False,
    )
```

```python
import functools

import jax
import jax.numpy as jnp
import numpy as np
from jax import lax
from jax.experimental import pallas as pl
from jax.experimental.pallas import tpu as pltpu
from jax.sharding import PartitionSpec as P

M = 16384
N = 1024

first_decay = 0.9
second_decay = 0.95
epsilon = 1e-08
clip_share = 0.25

f32, bf16 = jnp.float32, jnp.bfloat16
BOTH = ("row", "col")
VMEM_LIMIT = 50 * 1024 * 1024
SHRINK = 64
CHIPS = (1, 3, 2, 0)


def call(kernel, grid, in_specs, out_specs, out_shape, scratch=(), flops=0, moved=0, aliases=None, prefetch=0, name=None, after=()):
    at, k = prefetch + len(in_specs), len(after)

    def body(*refs):
        kernel(*refs[:at], *refs[at + k :])

    run = pl.pallas_call(
        body,
        grid_spec=pltpu.PrefetchScalarGridSpec(
            num_scalar_prefetch=prefetch, grid=grid, in_specs=list(in_specs) + [pl.BlockSpec(memory_space=pl.ANY)] * k,
            out_specs=out_specs, scratch_shapes=list(scratch),
        ),
        out_shape=out_shape,
        input_output_aliases=aliases or {},
        compiler_params=pltpu.CompilerParams(vmem_limit_bytes=VMEM_LIMIT, dimension_semantics=("arbitrary",) * len(grid)),
        cost_estimate=pl.CostEstimate(flops=flops // SHRINK, bytes_accessed=moved // SHRINK, transcendentals=0),
        name=name,
    )
    return lambda *args: run(*args, *after)


def shape(rows, columns, dtype=f32):
    return jax.ShapeDtypeStruct((rows, columns), dtype)


def split(value):
    high = value.astype(bf16)
    return high, (value - high.astype(f32)).astype(bf16)


def dot3(a_high, a_low, b_high, b_low, dims=(((1,), (0,)), ((), ()))):
    d = functools.partial(lax.dot_general, dimension_numbers=dims, preferred_element_type=f32)
    return d(a_high, b_high) + (d(a_high, b_low) + d(a_low, b_high))


def move(value, step):
    pairs = []
    for x in range(4):
        for c in range(2):
            for y in range(4):
                for z in range(4):
                    tx, tc, ty, tz = step(x, c, y, z)
                    pairs.append(((2 * x + c) * 16 + 4 * y + z, (2 * (tx % 4) + tc) * 16 + 4 * (ty % 4) + tz % 4))
    return lax.ppermute(value, BOTH, pairs)


def swap(value):
    return move(value, lambda x, c, y, z: (x, 1 - c, y, z))


def along_x(value, d):
    return move(value, lambda x, c, y, z: (x + d, c, y, z))


def first(value, d):
    return move(value, lambda x, c, y, z: (x, c, y + d, z) if c == 0 else (x, c, y, z + d))


def second_axis(value, d):
    return move(value, lambda x, c, y, z: (x, c, y, z + d) if c == 0 else (x, c, y + d, z))


def start(core, grad, moment):
    def kernel(core_ref, grad_ref, moment_ref, new_ref, keep_ref, give_ref):
        g = grad_ref[...]
        new = first_decay * moment_ref[...] + (1.0 - first_decay) * g
        new_ref[...] = new
        g, new = g.T, new.T
        zero = core_ref[0] == 0
        keep_ref[...] = jnp.where(zero, g, new)
        give_ref[...] = jnp.where(zero, new, g)

    block = pl.BlockSpec((256, 128), lambda t, c: (t, 0))
    turned = pl.BlockSpec((128, 256), lambda t, c: (0, t))
    return call(
        kernel, (4,), [block, block], [block, turned, turned], [shape(1024, 128), shape(128, 1024), shape(128, 1024)],
        moved=3 * 2**20, flops=10**6, prefetch=1, name="start",
    )(core, grad, moment)


def order_left(order, left, half, held=None):
    def kernel(order_ref, left_ref, *refs):
        high_ref, low_ref = refs[-2:]
        for a in range(4):
            for b in range(4):
                at = pl.multiple_of(order_ref[a * 4 + b] * 128, 128)
                high, low = split(left_ref[:, pl.ds(at, 128)])
                high_ref[a, 0, :, b * 128 : b * 128 + 128] = high
                low_ref[a, 0, :, b * 128 : b * 128 + 128] = low

    out = pl.BlockSpec((4, 1, 128, 512), lambda t, o: (0, half, t, 0))
    anywhere = pl.BlockSpec(memory_space=pl.ANY)
    more = [] if held is None else list(held)
    return call(
        kernel, (8,), [pl.BlockSpec((128, 2048), lambda t, o: (t, 0))] + [anywhere] * len(more),
        [out, out], [jax.ShapeDtypeStruct((4, 2, 1024, 512), bf16)] * 2, moved=16 * 2**20, flops=10**7,
        aliases={2: 0, 3: 1} if more else None, prefetch=1, name="order_left",
    )(order, left, *more)


def order_right(order, right):
    def kernel(order_ref, right_ref, high_ref, low_ref):
        high, low = split(right_ref[...])
        high_ref[...] = high
        low_ref[...] = low

    out = pl.BlockSpec((128, 1024), lambda a, o: (a, 0))
    return call(
        kernel, (8,), [pl.BlockSpec((128, 1024), lambda a, o: (o[a], 0))], [out, out], [shape(1024, 1024, bf16)] * 2,
        moved=8 * 2**20, flops=10**6, prefetch=1, name="order_right",
    )(order, right)


def fill(refs, high, low):
    at = 0
    for ref in refs:
        size = ref.shape[0]
        high[at : at + size, :], low[at : at + size, :] = split(ref[...])
        at += size


def project_far(blocks, left, after=()):
    rows = sum(b.shape[0] for b in blocks)
    n = len(blocks)

    def kernel(*refs):
        lh, ll, one, two, gh, gl = refs[n:]
        t = pl.program_id(0)

        @pl.when(t == 0)
        def _():
            fill(refs[:n], gh, gl)

        value = dot3(gh[...], gl[...], lh[0, 0], ll[0, 0])

        @pl.when(t == 0)
        def _():
            one[...] = value

        @pl.when(t == 1)
        def _():
            two[...] = value

    column = pl.BlockSpec((1, 1, 1024, 512), lambda t: (2, t, 0, 0))
    whole = pl.BlockSpec((rows, 512), lambda t: (0, 0))
    return call(
        kernel, (2,), [pl.BlockSpec(b.shape, lambda t: (0, 0)) for b in blocks] + [column, column],
        [whole, whole], [shape(rows, 512)] * 2, [pltpu.VMEM((rows, 1024), bf16)] * 2,
        flops=6 * rows * 2**20, moved=4 * 2**20 + rows * 8192, name="project_far", after=after,
    )(*blocks, *left)


def project_near(blocks, left, near, far, after=()):
    rows = sum(b.shape[0] for b in blocks)
    n = len(blocks)

    def kernel(*refs):
        lh, ll, near_ref, far_ref, up, down, gh, gl = refs[n:]
        t = pl.program_id(0)

        @pl.when(t == 0)
        def _():
            fill(refs[:n], gh, gl)

        value = dot3(gh[...], gl[...], lh[0, 0], ll[0, 0])

        @pl.when(t == 0)
        def _():
            up[...] = value + near_ref[...]

        @pl.when(t == 1)
        def _():
            up[...] = value

        @pl.when(t == 2)
        def _():
            down[...] = value

        @pl.when(t == 3)
        def _():
            down[...] = value + far_ref[...]

    column = pl.BlockSpec((1, 1, 1024, 512), lambda t: (t // 2 * 2 + 1, t % 2, 0, 0))
    whole = pl.BlockSpec((rows, 512), lambda t: (0, 0))
    return call(
        kernel, (4,), [pl.BlockSpec(b.shape, lambda t: (0, 0)) for b in blocks] + [column, column, whole, whole],
        [pl.BlockSpec((rows, 512), lambda t: (0, jnp.minimum(t, 1))), pl.BlockSpec((rows, 512), lambda t: (0, jnp.maximum(t - 2, 0)))],
        [shape(rows, 1024)] * 2, [pltpu.VMEM((rows, 1024), bf16)] * 2,
        flops=12 * rows * 2**20, moved=8 * 2**20 + rows * 16384, name="project_near", after=after,
    )(*blocks, *left, near, far)


def project_own(blocks, left, up, down, after=()):
    rows = sum(b.shape[0] for b in blocks)
    n = len(blocks)

    def kernel(*refs):
        lh, ll, up0, up1, down0, down1 = refs[n : n + 6]
        outs, (gh, gl) = refs[n + 6 : n + 10], refs[n + 10 :]
        t = pl.program_id(0)

        @pl.when(t == 0)
        def _():
            fill(refs[:n], gh, gl)

        high = jnp.concatenate([lh[0, 0], lh[0, 1]], axis=1)
        low = jnp.concatenate([ll[0, 0], ll[0, 1]], axis=1)
        value = dot3(gh[...], gl[...], high, low)
        value = value + jnp.concatenate([up0[...] + down0[...], up1[...] + down1[...]], axis=1)
        for d in range(4):

            @pl.when(t == d)
            def _(d=d):
                outs[d][...] = value

    column = pl.BlockSpec((1, 2, 1024, 128), lambda t: (0, 0, 0, t))
    one, two = pl.BlockSpec((rows, 128), lambda t: (0, t)), pl.BlockSpec((rows, 128), lambda t: (0, 4 + t))
    whole = pl.BlockSpec((rows, 256), lambda t: (0, 0))
    return call(
        kernel, (4,), [pl.BlockSpec(b.shape, lambda t: (0, 0)) for b in blocks] + [column, column, one, two, one, two],
        [whole] * 4, [shape(rows, 256)] * 4, [pltpu.VMEM((rows, 1024), bf16)] * 2,
        flops=6 * rows * 2**20, moved=4 * 2**20 + rows * 16384, name="project_own", after=after,
    )(*blocks, *left, up, up, down, down)


def rotate(parts, right, chips, before=None, last=False):
    rows = parts[0].shape[0]
    n = 6 + (before is not None)

    def kernel(*refs):
        p, (rh, rl) = refs[:4], refs[4:6]
        th, tl = refs[-2:]
        t = pl.program_id(0)

        @pl.when(t == 0)
        def _():
            total = (p[0][...] + p[1][...]) + (p[2][...] + p[3][...])
            th[...], tl[...] = split(total.T)

        def pick(r):
            places = [h * 512 + CHIPS.index(d) * 128 for d in chips for h in range(2)]
            return jnp.concatenate([r[p : p + 128, :] for p in places], axis=0)

        value = dot3(th[...], tl[...], pick(rh), pick(rl))
        if before is not None:
            value = value + refs[6][...]
        if last:
            refs[n][...] = value[:128]
            refs[n + 1][...] = value[128:]
        else:
            refs[n][...] = value

    part = pl.BlockSpec((rows, 256), lambda t: (0, 0))
    column = pl.BlockSpec((1024, 256), lambda t: (0, t))
    tall = pl.BlockSpec((256, 256), lambda t: (0, t))
    flat = pl.BlockSpec((128, 256), lambda t: (0, t))
    return call(
        kernel, (4,), [part] * 4 + [column] * 2 + [tall] * (n - 6),
        [flat, flat] if last else tall, [shape(128, 1024)] * 2 if last else shape(256, 1024),
        [pltpu.VMEM((256, rows), bf16)] * 2, flops=6 * 256 * rows * 1024, moved=8 * 2**20, name="rotate",
    )(*parts, *right, *([before] if n > 6 else []))


def turn(core, own, other, second, right):
    def kernel(core_ref, own_ref, other_ref, second_ref, rh, rl, new_ref, keep_ref, give_ref, th, tl, sum_ref):
        t = pl.program_id(0)

        @pl.when(t == 0)
        def _():
            zero = core_ref[0] == 0
            a, b = own_ref[...], other_ref[...]
            g, m = jnp.where(zero, a, b), jnp.where(zero, b, a)
            new = second_decay * second_ref[...] + (1.0 - second_decay) * g * g
            new_ref[...] = new
            rotated = m / (jnp.sqrt(new) + epsilon)
            th[...], tl[...] = split(rotated)
            squares = rotated * rotated
            total = squares[0:8, :]
            for i in range(1, 16):
                total = total + squares[i * 8 : i * 8 + 8, :]
            narrow = total[:, 0:128]
            for i in range(1, 8):
                narrow = narrow + total[:, i * 128 : i * 128 + 128]
            sum_ref[...] = narrow

        value = dot3(th[...], tl[...], rh[...], rl[...], (((1,), (1,)), ((), ())))
        first_lanes = jnp.where(t % 2 == 0, sum_ref[...], 0.0)
        extra = jnp.concatenate([first_lanes, jnp.zeros((8, 128), f32)], axis=1)

        @pl.when(t < 2)
        def _():
            keep_ref[0:128, :] = value
            keep_ref[128:136, :] = extra

        @pl.when(t >= 2)
        def _():
            give_ref[0:128, :] = value
            give_ref[128:136, :] = extra

    whole = pl.BlockSpec((128, 1024), lambda t, c: (0, 0))
    rows = pl.BlockSpec((256, 1024), lambda t, c: (t, 0))
    return call(
        kernel, (4,), [whole, whole, whole, rows, rows],
        [
            whole,
            pl.BlockSpec((136, 256), lambda t, c: (0, jnp.minimum(t, 1))),
            pl.BlockSpec((136, 256), lambda t, c: (0, jnp.maximum(t - 2, 0))),
        ],
        [shape(128, 1024), shape(136, 512), shape(136, 512)],
        [pltpu.VMEM((128, 1024), bf16)] * 2 + [pltpu.VMEM((8, 128), f32)],
        flops=6 * 128 * 2**20, moved=7 * 2**20, prefetch=1, name="turn",
    )(core, own, other, second, *right)


def back_project(terms, left, before=None, cut=False, after=()):
    arrays = [a for _, group in terms for a, _ in group]
    sizes = [size for _, group in terms for _, size in group]
    n, g = len(arrays), len(terms)

    def kernel(*refs):
        s_refs, l_refs = refs[:n], refs[n : n + 2 * g]
        sh, sl = refs[-2:]
        outs = refs[n + 2 * g + (before is not None) : -2]
        t = pl.program_id(0)

        @pl.when(t == 0)
        def _():
            fill(s_refs, sh, sl)

        value = refs[n + 2 * g][...] if before is not None else None
        for i in range(g):
            rows = slice(i * 1024, i * 1024 + 1024)
            high, low = l_refs[2 * i], l_refs[2 * i + 1]
            high = jnp.concatenate([high[0, 0], high[0, 1]], axis=1)
            low = jnp.concatenate([low[0, 0], low[0, 1]], axis=1)
            new = dot3(high, low, sh[rows, :], sl[rows, :])
            value = new if value is None else value + new
        if cut:
            outs[0][...] = value[:, :128]
            outs[1][...] = value[:, 128:]
        else:
            outs[0][...] = value

    wide = pl.BlockSpec((256, 256), lambda t: (t, 0))
    in_specs = [pl.BlockSpec((size, 256), lambda t: (0, 0)) for size in sizes]
    args = list(arrays)
    for d, _ in terms:
        in_specs += [pl.BlockSpec((1, 2, 256, 512), lambda t, d=d: (d, 0, t, 0))] * 2
        args += list(left)
    if before is not None:
        in_specs.append(wide)
        args.append(before)
    if cut:
        out_specs, out_shape = [pl.BlockSpec((256, 128), lambda t: (t, 0))] * 2, [shape(1024, 128)] * 2
    else:
        out_specs, out_shape = wide, shape(1024, 256)
    return call(
        kernel, (4,), in_specs, out_specs, out_shape, [pltpu.VMEM((1024 * g, 256), bf16)] * 2,
        flops=3 * g * 2**29, moved=(5 * g + 2) * 2**20, name="back_project", after=after,
    )(*args)


def lay(shares, half, after=()):
    def kernel(*refs):
        out = refs[-1]
        extra = jnp.zeros((8, 256), f32)
        for d in range(4):
            for h in range(2):
                out[(h * 4 + d) * 128 : (h * 4 + d) * 128 + 128, :] = refs[d][h, 0:128, :]
                extra = extra + refs[d][h, 128:136, :]
        out[1024:1032, :] = extra

    part = pl.BlockSpec((2, 136, 256), lambda t: (0, 0, half))
    return call(
        kernel, (1,), [part] * 4, pl.BlockSpec((1032, 256), lambda t: (0, 0)), shape(1032, 256),
        flops=2**14, moved=2**21, name="lay", after=after,
    )(*shares)


def tables():
    left = np.zeros((2, 16, 16), np.int32)
    right = np.zeros((8, 8), np.int32)
    for c in range(2):
        for y in range(4):
            for z in range(4):
                for a in range(4):
                    for b in range(4):
                        p, q = (y + a, z + b) if c == 0 else (y + b, z + a)
                        left[c, y * 4 + z, a * 4 + b] = p % 4 * 4 + q % 4
        for x in range(4):
            for h in range(2):
                for i, d in enumerate(CHIPS):
                    right[2 * x + c, h * 4 + i] = 2 * ((x + d) % 4) + (c + h) % 2
    return left, right


def local(grad, moment, second, left_basis, right_basis):
    row, col = lax.axis_index("row"), lax.axis_index("col")
    core = (row % 2).reshape(1).astype(jnp.int32)
    by_col, by_row = tables()
    order = jnp.asarray(by_col)[row % 2, col]
    order_r = jnp.asarray(by_row)[row]

    left_other = swap(left_basis)
    moment_new, keep, give = start(core, grad, moment)
    moved = swap(give)
    left = order_left(order, left_basis, 0)
    right = order_right(order_r, right_basis)
    mine = jnp.concatenate([keep, moved], axis=0)
    plus = along_x(mine, -1)
    minus = along_x(mine, 1)
    left = order_left(order, left_other, 1, left)
    far_a = along_x(plus[:128], -1)
    far_b = along_x(minus[128:], 1)

    chunks = [((0,), [mine]), ((1, 3), [plus, minus]), ((2,), [far_a, far_b])]
    far, near, parts = [None] * 3, [None] * 3, [None] * 3

    def step_far(i, after=()):
        one, two = project_far(chunks[i][1], left, after)
        far[i] = first(one, 1), first(two, -1)
        return (one,)

    def step_near(i, after=()):
        up, down = project_near(chunks[i][1], left, *far[i], after)
        near[i] = first(up, 1), first(down, -1)
        return (up,)

    def step_own(i, after=()):
        q = project_own(chunks[i][1], left, *near[i], after)
        parts[i] = [q[0], second_axis(q[1], 1), second_axis(q[3], -1), second_axis(q[2], 2)]
        return (q[0],)

    done = step_far(0)
    done = step_near(0, done)
    done = step_far(1, done)
    done = step_own(0, done)
    done = step_far(2, done)
    done = step_near(1, done)
    done = step_near(2, done)
    done = step_own(1, done)
    done = step_own(2, done)
    part = None
    for i, (chips, _) in enumerate(chunks):
        part = rotate(parts[i], right, chips, part, last=i == 2)
    own, other = part
    other = swap(other)

    second_new, keep, give = turn(core, own, other, second, right)
    share = jnp.stack([keep, swap(give)], axis=0)
    shares = [share, second_axis(share, -1), second_axis(share, -2), second_axis(share, 1)]

    block_a = lay(shares, 0)
    plus_a, minus_a = first(block_a, -1), first(block_a, 1)
    sums = back_project([(0, [(block_a, 1024)])], left)
    far_a, far_b = first(plus_a[:512], -1), first(minus_a[512:], 1)
    block_b = lay(shares, 1, (plus_a, minus_a))
    plus_b, minus_b = first(block_b, -1), first(block_b, 1)
    sums = back_project([(1, [(plus_a, 1024)]), (3, [(minus_a, 1024)])], left, sums, after=(block_b,))
    u1, u3 = back_project([(2, [(far_a, 512), (far_b, 512)])], left, sums, cut=True)
    got1, got3 = along_x(u1, 1), along_x(u3, -1)
    squares = (block_a[1024:, :128] + plus_a[1024:, :128]) + (minus_a[1024:, :128] + far_b[512:, :128])
    squares = squares + move(squares, lambda x, c, y, z: (x ^ 1, c, y, z))
    squares = squares + move(squares, lambda x, c, y, z: (x ^ 2, c, y, z))
    sums = back_project([(0, [(block_b, 1024)])], left, after=(u1,))
    far_a, far_b = first(plus_b[:512], -1), first(minus_b[512:1024], 1)
    sums = back_project([(1, [(plus_b, 1024)]), (3, [(minus_b, 1024)])], left, sums)
    u2, u0 = back_project([(2, [(far_a, 512), (far_b, 512)])], left, sums, cut=True, after=(squares,))
    total = jnp.sum(squares)
    factor = jnp.minimum(1.0, clip_share * jnp.sqrt(jnp.float32(M * N)) / (jnp.sqrt(total) + 1e-06))
    update = ((u0 + got1) + (got3 + along_x(u2, 2))) * factor
    return (update, moment_new, second_new)


def solution(mesh):
    return jax.shard_map(
        local,
        mesh=mesh,
        in_specs=(P("col", "row"), P("col", "row"), P(("row", "col"), None), P("col", "row"), P()),
        out_specs=(P("col", "row"), P("col", "row"), P(("row", "col"), None)),
        check_vma=False,
    )
```

```python
import functools

import jax
import jax.numpy as jnp
import numpy as np
from jax import lax
from jax.experimental import pallas as pl
from jax.experimental.pallas import tpu as pltpu
from jax.sharding import PartitionSpec as P

M = 16384
N = 1024

first_decay = 0.9
second_decay = 0.95
epsilon = 1e-08
clip_share = 0.25

f32, bf16 = jnp.float32, jnp.bfloat16
BOTH = ("row", "col")
VMEM_LIMIT = 16 * 1024 * 1024
CHIPS = (1, 3, 2, 0)
WHOLE = pl.BlockSpec(memory_space=pltpu.VMEM)
SCALARS = pl.BlockSpec(memory_space=pltpu.SMEM)
ANYWHERE = pl.BlockSpec(memory_space=pl.ANY)


def call(kernel, name, args, out_shape, specs=None, scratch=(), after=(), cost=1):
    n, k = len(args), len(after)

    def body(*refs):
        kernel(*refs[:n], *refs[n + k :])

    return pl.pallas_call(
        body,
        in_specs=(specs or [WHOLE] * n) + [ANYWHERE] * k,
        out_specs=[WHOLE] * len(out_shape),
        out_shape=out_shape,
        scratch_shapes=list(scratch),
        compiler_params=pltpu.CompilerParams(vmem_limit_bytes=VMEM_LIMIT),
        cost_estimate=pl.CostEstimate(flops=cost, bytes_accessed=cost, transcendentals=0),
        name=name,
    )(*args, *after)


def shape(rows, columns, dtype=f32):
    return jax.ShapeDtypeStruct((rows, columns), dtype)


def split(value):
    high = value.astype(bf16)
    return high, (value - high.astype(f32)).astype(bf16)


def dot3(a_high, a_low, b_high, b_low, dims=(((1,), (0,)), ((), ()))):
    d = functools.partial(lax.dot_general, dimension_numbers=dims, preferred_element_type=f32)
    return d(a_high, b_high) + (d(a_high, b_low) + d(a_low, b_high))


def move(value, step):
    pairs = []
    for x in range(4):
        for c in range(2):
            for y in range(4):
                for z in range(4):
                    tx, tc, ty, tz = step(x, c, y, z)
                    pairs.append(((2 * x + c) * 16 + 4 * y + z, (2 * (tx % 4) + tc) * 16 + 4 * (ty % 4) + tz % 4))
    return lax.ppermute(value, BOTH, pairs)


def swap(value):
    return move(value, lambda x, c, y, z: (x, 1 - c, y, z))


def along_x(value, d):
    return move(value, lambda x, c, y, z: (x + d, c, y, z))


def first(value, d):
    return move(value, lambda x, c, y, z: (x, c, y + d, z) if c == 0 else (x, c, y, z + d))


def second_axis(value, d):
    return move(value, lambda x, c, y, z: (x, c, y, z + d) if c == 0 else (x, c, y + d, z))


def start(core, grad, moment):
    def kernel(core_ref, grad_ref, moment_ref, new_ref, keep_ref, give_ref):
        g = grad_ref[...]
        new = first_decay * moment_ref[...] + (1.0 - first_decay) * g
        new_ref[...] = new
        g, new = g.T, new.T
        zero = core_ref[0] == 0
        keep_ref[...] = jnp.where(zero, g, new)
        give_ref[...] = jnp.where(zero, new, g)

    return call(
        kernel, "start", [core, grad, moment], [shape(1024, 128), shape(128, 1024), shape(128, 1024)], [SCALARS, WHOLE, WHOLE]
    )


def order_left(order, left, after=()):
    steps, slots = 8, 4

    def kernel(order_ref, left_ref, high_ref, low_ref, held, arrived):
        def copy(i):
            return pltpu.make_async_copy(left_ref.at[pl.ds(i * 128, 128), :], held.at[i % slots], arrived.at[i % slots])

        for i in range(slots):
            copy(i).start()
        for i in range(steps):
            copy(i).wait()
            rows = slice(i * 128, i * 128 + 128)
            for a in range(4):
                for b in range(4):
                    at = pl.multiple_of(order_ref[a * 4 + b] * 128, 128)
                    high, low = split(held[i % slots, :, pl.ds(at, 128)])
                    high_ref[a, rows, b * 128 : b * 128 + 128] = high
                    low_ref[a, rows, b * 128 : b * 128 + 128] = low
            if i + slots < steps:
                copy(i + slots).start()

    return call(
        kernel, "order_left", [order, left], [jax.ShapeDtypeStruct((4, 1024, 512), bf16)] * 2, [SCALARS, pl.BlockSpec(memory_space=pltpu.HBM)],
        [pltpu.VMEM((slots, 128, 2048), f32), pltpu.SemaphoreType.DMA((slots,))], after,
    )


def order_right(order, right):
    def kernel(order_ref, right_ref, high_ref, low_ref):
        for i in range(8):
            at = pl.multiple_of(order_ref[i] * 128, 128)
            rows = slice(i * 128, i * 128 + 128)
            high_ref[rows, :], low_ref[rows, :] = split(right_ref[pl.ds(at, 128), :])

    return call(kernel, "order_right", [order, right], [shape(1024, 1024, bf16)] * 2, [SCALARS, WHOLE])


def fill(refs, high, low):
    at = 0
    for ref in refs:
        size = ref.shape[0]
        high[at : at + size, :], low[at : at + size, :] = split(ref[...])
        at += size


def project_far(blocks, left, after=()):
    rows = sum(b.shape[0] for b in blocks)
    n = len(blocks)

    def kernel(*refs):
        l_refs, outs, (gh, gl) = refs[n : n + 4], refs[n + 4 : n + 6], refs[n + 6 :]
        fill(refs[:n], gh, gl)
        for h in range(2):
            for t in range(2):
                c = slice(t * 256, t * 256 + 256)
                outs[h][:, c] = dot3(gh[...], gl[...], l_refs[2 * h][2, :, c], l_refs[2 * h + 1][2, :, c])

    return call(
        kernel, "project_far", [*blocks, *left], [shape(rows, 512)] * 2, None, [pltpu.VMEM((rows, 1024), bf16)] * 2, after
    )


def project_near(blocks, left, near, far, after=()):
    rows = sum(b.shape[0] for b in blocks)
    n = len(blocks)

    def kernel(*refs):
        l_refs, more, outs, (gh, gl) = refs[n : n + 4], refs[n + 4 : n + 6], refs[n + 6 : n + 8], refs[n + 8 :]
        fill(refs[:n], gh, gl)
        for i, d in enumerate((1, 3)):
            for h in range(2):
                for t in range(2):
                    c = slice(t * 256, t * 256 + 256)
                    value = dot3(gh[...], gl[...], l_refs[2 * h][d, :, c], l_refs[2 * h + 1][d, :, c])
                    if h == i:
                        value = value + more[i][:, c]
                    outs[i][:, h * 512 + t * 256 : h * 512 + t * 256 + 256] = value

    return call(
        kernel, "project_near", [*blocks, *left, near, far], [shape(rows, 1024)] * 2, None,
        [pltpu.VMEM((rows, 1024), bf16)] * 2, after,
    )


def project_own(blocks, left, up, down, after=()):
    rows = sum(b.shape[0] for b in blocks)
    n = len(blocks)

    def kernel(*refs):
        l_refs, (up_ref, down_ref), outs, (gh, gl) = refs[n : n + 4], refs[n + 4 : n + 6], refs[n + 6 : n + 10], refs[n + 10 :]
        fill(refs[:n], gh, gl)
        for d in range(4):
            c = slice(d * 128, d * 128 + 128)
            high = jnp.concatenate([l_refs[0][0, :, c], l_refs[2][0, :, c]], axis=1)
            low = jnp.concatenate([l_refs[1][0, :, c], l_refs[3][0, :, c]], axis=1)
            value = dot3(gh[...], gl[...], high, low)
            for h in range(2):
                e = slice(h * 512 + d * 128, h * 512 + d * 128 + 128)
                outs[d][:, h * 128 : h * 128 + 128] = value[:, h * 128 : h * 128 + 128] + up_ref[:, e] + down_ref[:, e]

    return call(
        kernel, "project_own", [*blocks, *left, up, down], [shape(rows, 256)] * 4, None, [pltpu.VMEM((rows, 1024), bf16)] * 2, after
    )


def rotate(parts, right, chips, before=None, last=False):
    n = 6 + (before is not None)

    def kernel(*refs):
        p, (rh, rl) = refs[:4], refs[4:6]
        total = (p[0][...] + p[1][...]) + (p[2][...] + p[3][...])
        high, low = split(total.T)
        places = [h * 512 + CHIPS.index(d) * 128 for d in chips for h in range(2)]
        for t in range(4):
            c = slice(t * 256, t * 256 + 256)
            r_high = jnp.concatenate([rh[p : p + 128, c] for p in places], axis=0)
            r_low = jnp.concatenate([rl[p : p + 128, c] for p in places], axis=0)
            value = dot3(high, low, r_high, r_low)
            if before is not None:
                value = value + refs[6][:, c]
            if last:
                refs[n][:, c] = value[:128]
                refs[n + 1][:, c] = value[128:]
            else:
                refs[n][:, c] = value

    out = call(
        kernel, "rotate", [*parts, *right] + ([before] if n > 6 else []), [shape(128, 1024)] * 2 if last else [shape(256, 1024)]
    )
    return out if last else out[0]


def turn(core, own, other, second, right):
    def kernel(core_ref, own_ref, other_ref, second_ref, rh, rl, new_ref, keep_ref, give_ref):
        zero = core_ref[0] == 0
        a, b = own_ref[...], other_ref[...]
        g, m = jnp.where(zero, a, b), jnp.where(zero, b, a)
        new = second_decay * second_ref[...] + (1.0 - second_decay) * g * g
        new_ref[...] = new
        rotated = m / (jnp.sqrt(new) + epsilon)
        high, low = split(rotated)
        squares = rotated * rotated
        total = squares[0:8, :]
        for i in range(1, 16):
            total = total + squares[i * 8 : i * 8 + 8, :]
        narrow = total[:, 0:128]
        for i in range(1, 8):
            narrow = narrow + total[:, i * 128 : i * 128 + 128]
        for out, h in ((give_ref, 1), (keep_ref, 0)):
            for t in range(2):
                r = slice(h * 512 + t * 256, h * 512 + t * 256 + 256)
                out[0:128, t * 256 : t * 256 + 256] = dot3(high, low, rh[r, :], rl[r, :], (((1,), (1,)), ((), ())))
            out[128:136, :] = jnp.concatenate([narrow, jnp.zeros((8, 384), f32)], axis=1)

    return call(
        kernel, "turn", [core, own, other, second, *right], [shape(128, 1024), shape(136, 512), shape(136, 512)],
        [SCALARS] + [WHOLE] * 5,
    )


def back_project(terms, left, before=None, cut=False, after=()):
    arrays = [a for _, group in terms for a in group]
    n = len(arrays)

    def kernel(*refs):
        l_refs = refs[n : n + 4]
        sh, sl = refs[-2:]
        outs = refs[n + 4 + (before is not None) : -2]
        at, index = 0, 0
        for _, group in terms:
            size = 1024 // len(group)
            for _ in group:
                sh[at : at + size, :], sl[at : at + size, :] = split(refs[index][0:size, :])
                at, index = at + size, index + 1
        for t in range(4):
            r = slice(t * 256, t * 256 + 256)
            value = refs[n + 4][r, :] if before is not None else None
            for i, (d, _) in enumerate(terms):
                for h in range(2):
                    rows = slice(i * 1024 + h * 512, i * 1024 + h * 512 + 512)
                    new = dot3(l_refs[2 * h][d, r, :], l_refs[2 * h + 1][d, r, :], sh[rows, :], sl[rows, :])
                    value = new if value is None else value + new
            if cut:
                outs[0][r, :] = value[:, :128]
                outs[1][r, :] = value[:, 128:]
            else:
                outs[0][r, :] = value

    out = call(
        kernel, "back_project", [*arrays, *left] + ([] if before is None else [before]),
        [shape(1024, 128)] * 2 if cut else [shape(1024, 256)], None, [pltpu.VMEM((1024 * len(terms), 256), bf16)] * 2, after,
    )
    return out if cut else out[0]


def lay(shares, half, after=()):
    def kernel(*refs):
        out = refs[-1]
        c = slice(half * 256, half * 256 + 256)
        extra = jnp.zeros((8, 256), f32)
        for d in range(4):
            for h in range(2):
                out[(h * 4 + d) * 128 : (h * 4 + d) * 128 + 128, :] = refs[d][h, 0:128, c]
                extra = extra + refs[d][h, 128:136, c]
        out[1024:1032, :] = extra

    return call(kernel, "lay", list(shares), [shape(1032, 256)], after=after)[0]


def tables():
    left = np.zeros((2, 16, 16), np.int32)
    right = np.zeros((8, 8), np.int32)
    for c in range(2):
        for y in range(4):
            for z in range(4):
                for a in range(4):
                    for b in range(4):
                        p, q = (y + a, z + b) if c == 0 else (y + b, z + a)
                        left[c, y * 4 + z, a * 4 + b] = p % 4 * 4 + q % 4
        for x in range(4):
            for h in range(2):
                for i, d in enumerate(CHIPS):
                    right[2 * x + c, h * 4 + i] = 2 * ((x + d) % 4) + (c + h) % 2
    return left, right


def local(grad, moment, second, left_basis, right_basis):
    row, col = lax.axis_index("row"), lax.axis_index("col")
    core = (row % 2).reshape(1).astype(jnp.int32)
    by_col, by_row = tables()
    order = jnp.asarray(by_col)[row % 2, col]
    order_r = jnp.asarray(by_row)[row]

    left_other = swap(left_basis)
    moment_new, keep, give = start(core, grad, moment)
    plus_keep, minus_keep = along_x(keep, -1), along_x(keep, 1)
    moved = swap(give)
    left = order_left(order, left_basis)
    right = order_right(order_r, right_basis)
    plus_moved, minus_moved = along_x(moved, -1), along_x(moved, 1)
    far_keep, far_moved = along_x(plus_keep, -1), along_x(minus_moved, 1)
    left = [*left, *order_left(order, left_other, (plus_keep, minus_keep))]

    chunks = [
        ((0,), [keep, moved]),
        ((1, 3), [plus_keep, plus_moved, minus_keep, minus_moved]),
        ((2,), [far_keep, far_moved]),
    ]
    far, near, parts = [None] * 3, [None] * 3, [None] * 3

    def step_far(i, after=()):
        one, two = project_far(chunks[i][1], left, after)
        far[i] = first(one, 1), first(two, -1)
        return (one,)

    def step_near(i, after=()):
        up, down = project_near(chunks[i][1], left, *far[i], after)
        near[i] = first(up, 1), first(down, -1)
        return (up,)

    def step_own(i, after=()):
        q = project_own(chunks[i][1], left, *near[i], after)
        parts[i] = [q[0], second_axis(q[1], 1), second_axis(q[3], -1), second_axis(q[2], 2)]
        return (q[0],)

    done = step_far(0)
    done = step_near(0, done)
    done = step_far(1, done)
    done = step_own(0, done)
    done = step_near(1, done)
    done = step_far(2, done)
    done = step_own(1, done)
    done = step_near(2, done)
    done = step_own(2, done)
    part = None
    for i, (chips, _) in enumerate(chunks):
        part = rotate(parts[i], right, chips, part, last=i == 2)
    own, other = part
    other = swap(other)

    second_new, keep, give = turn(core, own, other, second, right)
    share = jnp.stack([keep, swap(give)], axis=0)
    shares = [share, second_axis(share, -1), second_axis(share, -2), second_axis(share, 1)]

    block_a = lay(shares, 0)
    plus_a, minus_a = first(block_a, -1), first(block_a, 1)
    sums = back_project([(0, [block_a])], left)
    far_a, far_b = first(plus_a[:512], -1), first(minus_a[512:], 1)
    block_b = lay(shares, 1, (plus_a, minus_a))
    plus_b, minus_b = first(block_b, -1), first(block_b, 1)
    sums = back_project([(1, [plus_a]), (3, [minus_a])], left, sums, after=(block_b,))
    u1, u3 = back_project([(2, [far_a, far_b])], left, sums, cut=True)
    got1, got3 = along_x(u1, 1), along_x(u3, -1)
    squares = (block_a[1024:, :128] + plus_a[1024:, :128]) + (minus_a[1024:, :128] + far_b[512:, :128])
    squares = squares + move(squares, lambda x, c, y, z: (x ^ 1, c, y, z))
    squares = squares + move(squares, lambda x, c, y, z: (x ^ 2, c, y, z))
    sums = back_project([(0, [block_b])], left, after=(u1,))
    far_a, far_b = first(plus_b[:512], -1), first(minus_b[512:1024], 1)
    sums = back_project([(1, [plus_b]), (3, [minus_b])], left, sums)
    u2, u0 = back_project([(2, [far_a, far_b])], left, sums, cut=True, after=(squares,))
    total = jnp.sum(squares)
    factor = jnp.minimum(1.0, clip_share * jnp.sqrt(jnp.float32(M * N)) / (jnp.sqrt(total) + 1e-06))
    update = ((u0 + got1) + (got3 + along_x(u2, 2))) * factor
    return (update, moment_new, second_new)


def solution(mesh):
    return jax.shard_map(
        local,
        mesh=mesh,
        in_specs=(P("col", "row"), P("col", "row"), P(("row", "col"), None), P("col", "row"), P()),
        out_specs=(P("col", "row"), P("col", "row"), P(("row", "col"), None)),
        check_vma=False,
    )
```

```python
import functools

import jax
import jax.numpy as jnp
import numpy as np
from jax import lax
from jax.experimental import pallas as pl
from jax.experimental.pallas import tpu as pltpu
from jax.sharding import PartitionSpec as P

M = 16384
N = 1024

first_decay = 0.9
second_decay = 0.95
epsilon = 1e-08
clip_share = 0.25

f32, bf16 = jnp.float32, jnp.bfloat16
BOTH = ("row", "col")
VMEM_LIMIT = 10 * 1024 * 1024
CHIPS = (1, 3, 2, 0)
WHOLE = pl.BlockSpec(memory_space=pltpu.VMEM)
SCALARS = pl.BlockSpec(memory_space=pltpu.SMEM)
ANYWHERE = pl.BlockSpec(memory_space=pl.ANY)


def call(kernel, name, args, out_shape, specs=None, scratch=(), after=(), cost=1):
    n, k = len(args), len(after)

    def body(*refs):
        kernel(*refs[:n], *refs[n + k :])

    return pl.pallas_call(
        body,
        in_specs=(specs or [WHOLE] * n) + [ANYWHERE] * k,
        out_specs=[WHOLE] * len(out_shape),
        out_shape=out_shape,
        scratch_shapes=list(scratch),
        compiler_params=pltpu.CompilerParams(vmem_limit_bytes=VMEM_LIMIT),
        cost_estimate=pl.CostEstimate(flops=cost, bytes_accessed=cost, transcendentals=0),
        name=name,
    )(*args, *after)


def shape(rows, columns, dtype=f32):
    return jax.ShapeDtypeStruct((rows, columns), dtype)


def split(value):
    high = value.astype(bf16)
    return high, (value - high.astype(f32)).astype(bf16)


def dot3(a_high, a_low, b_high, b_low, dims=(((1,), (0,)), ((), ()))):
    d = functools.partial(lax.dot_general, dimension_numbers=dims, preferred_element_type=f32)
    return d(a_high, b_high) + (d(a_high, b_low) + d(a_low, b_high))


def move(value, step):
    pairs = []
    for x in range(4):
        for c in range(2):
            for y in range(4):
                for z in range(4):
                    tx, tc, ty, tz = step(x, c, y, z)
                    pairs.append(((2 * x + c) * 16 + 4 * y + z, (2 * (tx % 4) + tc) * 16 + 4 * (ty % 4) + tz % 4))
    return lax.ppermute(value, BOTH, pairs)


def swap(value):
    return move(value, lambda x, c, y, z: (x, 1 - c, y, z))


def along_x(value, d):
    return move(value, lambda x, c, y, z: (x + d, c, y, z))


def first(value, d):
    return move(value, lambda x, c, y, z: (x, c, y + d, z) if c == 0 else (x, c, y, z + d))


def second_axis(value, d):
    return move(value, lambda x, c, y, z: (x, c, y, z + d) if c == 0 else (x, c, y + d, z))


def start(core, grad, moment):
    def kernel(core_ref, grad_ref, moment_ref, new_ref, keep_ref, give_ref):
        g = grad_ref[...]
        new = first_decay * moment_ref[...] + (1.0 - first_decay) * g
        new_ref[...] = new
        g, new = g.T, new.T
        zero = core_ref[0] == 0
        keep_ref[...] = jnp.where(zero, g, new)
        give_ref[...] = jnp.where(zero, new, g)

    return call(
        kernel, "start", [core, grad, moment], [shape(1024, 128), shape(128, 1024), shape(128, 1024)], [SCALARS, WHOLE, WHOLE]
    )


def order_left(order, left, after=()):
    steps, slots = 8, 4

    def kernel(order_ref, left_ref, high_ref, low_ref, held, arrived):
        def copy(i):
            return pltpu.make_async_copy(left_ref.at[pl.ds(i * 128, 128), :], held.at[i % slots], arrived.at[i % slots])

        for i in range(slots):
            copy(i).start()
        for i in range(steps):
            copy(i).wait()
            rows = slice(i * 128, i * 128 + 128)
            for a in range(4):
                for b in range(4):
                    at = pl.multiple_of(order_ref[a * 4 + b] * 128, 128)
                    high, low = split(held[i % slots, :, pl.ds(at, 128)])
                    high_ref[a, rows, b * 128 : b * 128 + 128] = high
                    low_ref[a, rows, b * 128 : b * 128 + 128] = low
            if i + slots < steps:
                copy(i + slots).start()

    return call(
        kernel, "order_left", [order, left], [jax.ShapeDtypeStruct((4, 1024, 512), bf16)] * 2, [SCALARS, pl.BlockSpec(memory_space=pltpu.HBM)],
        [pltpu.VMEM((slots, 128, 2048), f32), pltpu.SemaphoreType.DMA((slots,))], after,
    )


def order_right(order, right):
    def kernel(order_ref, right_ref, high_ref, low_ref):
        for i in range(8):
            at = pl.multiple_of(order_ref[i] * 128, 128)
            rows = slice(i * 128, i * 128 + 128)
            high_ref[rows, :], low_ref[rows, :] = split(right_ref[pl.ds(at, 128), :])

    return call(kernel, "order_right", [order, right], [shape(1024, 1024, bf16)] * 2, [SCALARS, WHOLE])


def fill(refs, high, low):
    at = 0
    for ref in refs:
        size = ref.shape[0]
        high[at : at + size, :], low[at : at + size, :] = split(ref[...])
        at += size


def project_far(blocks, left, after=()):
    rows = sum(b.shape[0] for b in blocks)
    n = len(blocks)

    def kernel(*refs):
        l_refs, outs, (gh, gl) = refs[n : n + 4], refs[n + 4 : n + 6], refs[n + 6 :]
        fill(refs[:n], gh, gl)
        for h in range(2):
            for t in range(2):
                c = slice(t * 256, t * 256 + 256)
                outs[h][:, c] = dot3(gh[...], gl[...], l_refs[2 * h][2, :, c], l_refs[2 * h + 1][2, :, c])

    return call(
        kernel, "project_far", [*blocks, *left], [shape(rows, 512)] * 2, None, [pltpu.VMEM((rows, 1024), bf16)] * 2, after
    )


def project_near(blocks, left, near, far, after=()):
    rows = sum(b.shape[0] for b in blocks)
    n = len(blocks)

    def kernel(*refs):
        l_refs, more, outs, (gh, gl) = refs[n : n + 4], refs[n + 4 : n + 6], refs[n + 6 : n + 8], refs[n + 8 :]
        fill(refs[:n], gh, gl)
        for i, d in enumerate((1, 3)):
            for h in range(2):
                for t in range(2):
                    c = slice(t * 256, t * 256 + 256)
                    value = dot3(gh[...], gl[...], l_refs[2 * h][d, :, c], l_refs[2 * h + 1][d, :, c])
                    if h == i:
                        value = value + more[i][:, c]
                    outs[i][:, h * 512 + t * 256 : h * 512 + t * 256 + 256] = value

    return call(
        kernel, "project_near", [*blocks, *left, near, far], [shape(rows, 1024)] * 2, None,
        [pltpu.VMEM((rows, 1024), bf16)] * 2, after,
    )


def project_own(blocks, left, up, down, after=()):
    rows = sum(b.shape[0] for b in blocks)
    n = len(blocks)

    def kernel(*refs):
        l_refs, (up_ref, down_ref), outs, (gh, gl) = refs[n : n + 4], refs[n + 4 : n + 6], refs[n + 6 : n + 10], refs[n + 10 :]
        fill(refs[:n], gh, gl)
        for d in range(4):
            c = slice(d * 128, d * 128 + 128)
            high = jnp.concatenate([l_refs[0][0, :, c], l_refs[2][0, :, c]], axis=1)
            low = jnp.concatenate([l_refs[1][0, :, c], l_refs[3][0, :, c]], axis=1)
            value = dot3(gh[...], gl[...], high, low)
            for h in range(2):
                e = slice(h * 512 + d * 128, h * 512 + d * 128 + 128)
                outs[d][:, h * 128 : h * 128 + 128] = value[:, h * 128 : h * 128 + 128] + up_ref[:, e] + down_ref[:, e]

    return call(
        kernel, "project_own", [*blocks, *left, up, down], [shape(rows, 256)] * 4, None, [pltpu.VMEM((rows, 1024), bf16)] * 2, after
    )


def rotate(parts, right, chips, before=None, last=False):
    n = 6 + (before is not None)

    def kernel(*refs):
        p, (rh, rl) = refs[:4], refs[4:6]
        total = (p[0][...] + p[1][...]) + (p[2][...] + p[3][...])
        high, low = split(total.T)
        places = [h * 512 + CHIPS.index(d) * 128 for d in chips for h in range(2)]
        for t in range(4):
            c = slice(t * 256, t * 256 + 256)
            r_high = jnp.concatenate([rh[p : p + 128, c] for p in places], axis=0)
            r_low = jnp.concatenate([rl[p : p + 128, c] for p in places], axis=0)
            value = dot3(high, low, r_high, r_low)
            if before is not None:
                value = value + refs[6][:, c]
            if last:
                refs[n][:, c] = value[:128]
                refs[n + 1][:, c] = value[128:]
            else:
                refs[n][:, c] = value

    out = call(
        kernel, "rotate", [*parts, *right] + ([before] if n > 6 else []), [shape(128, 1024)] * 2 if last else [shape(256, 1024)]
    )
    return out if last else out[0]


def turn(core, own, other, second, right):
    def kernel(core_ref, own_ref, other_ref, second_ref, rh, rl, new_ref, keep_ref, give_ref):
        zero = core_ref[0] == 0
        a, b = own_ref[...], other_ref[...]
        g, m = jnp.where(zero, a, b), jnp.where(zero, b, a)
        new = second_decay * second_ref[...] + (1.0 - second_decay) * g * g
        new_ref[...] = new
        rotated = m / (jnp.sqrt(new) + epsilon)
        high, low = split(rotated)
        squares = rotated * rotated
        total = squares[0:8, :]
        for i in range(1, 16):
            total = total + squares[i * 8 : i * 8 + 8, :]
        narrow = total[:, 0:128]
        for i in range(1, 8):
            narrow = narrow + total[:, i * 128 : i * 128 + 128]
        for out, h in ((give_ref, 1), (keep_ref, 0)):
            for t in range(2):
                r = slice(h * 512 + t * 256, h * 512 + t * 256 + 256)
                out[0:128, t * 256 : t * 256 + 256] = dot3(high, low, rh[r, :], rl[r, :], (((1,), (1,)), ((), ())))
            out[128:136, :] = jnp.concatenate([narrow, jnp.zeros((8, 384), f32)], axis=1)

    return call(
        kernel, "turn", [core, own, other, second, *right], [shape(128, 1024), shape(136, 512), shape(136, 512)],
        [SCALARS] + [WHOLE] * 5,
    )


def back_project(terms, left, before=None, cut=False, after=()):
    arrays = [a for _, group in terms for a in group]
    n = len(arrays)

    def kernel(*refs):
        l_refs = refs[n : n + 4]
        sh, sl = refs[-2:]
        outs = refs[n + 4 + (before is not None) : -2]
        at, index = 0, 0
        for _, group in terms:
            size = 1024 // len(group)
            for _ in group:
                sh[at : at + size, :], sl[at : at + size, :] = split(refs[index][0:size, :])
                at, index = at + size, index + 1
        for t in range(4):
            r = slice(t * 256, t * 256 + 256)
            value = refs[n + 4][r, :] if before is not None else None
            for i, (d, _) in enumerate(terms):
                for h in range(2):
                    rows = slice(i * 1024 + h * 512, i * 1024 + h * 512 + 512)
                    new = dot3(l_refs[2 * h][d, r, :], l_refs[2 * h + 1][d, r, :], sh[rows, :], sl[rows, :])
                    value = new if value is None else value + new
            if cut:
                outs[0][r, :] = value[:, :128]
                outs[1][r, :] = value[:, 128:]
            else:
                outs[0][r, :] = value

    out = call(
        kernel, "back_project", [*arrays, *left] + ([] if before is None else [before]),
        [shape(1024, 128)] * 2 if cut else [shape(1024, 256)], None, [pltpu.VMEM((1024 * len(terms), 256), bf16)] * 2, after,
    )
    return out if cut else out[0]


def lay(shares, half, after=()):
    def kernel(*refs):
        out = refs[-1]
        c = slice(half * 256, half * 256 + 256)
        extra = jnp.zeros((8, 256), f32)
        for d in range(4):
            for h in range(2):
                out[(h * 4 + d) * 128 : (h * 4 + d) * 128 + 128, :] = refs[d][h, 0:128, c]
                extra = extra + refs[d][h, 128:136, c]
        out[1024:1032, :] = extra

    return call(kernel, "lay", list(shares), [shape(1032, 256)], after=after)[0]


def forward(plus, minus, after):
    def kernel(plus_ref, minus_ref, one, two):
        one[...] = plus_ref[0:512, :]
        two[...] = minus_ref[512:1032, :]

    return call(kernel, "forward", [plus, minus], [shape(512, 256), shape(520, 256)], after=after)


def tables():
    left = np.zeros((2, 16, 16), np.int32)
    right = np.zeros((8, 8), np.int32)
    for c in range(2):
        for y in range(4):
            for z in range(4):
                for a in range(4):
                    for b in range(4):
                        p, q = (y + a, z + b) if c == 0 else (y + b, z + a)
                        left[c, y * 4 + z, a * 4 + b] = p % 4 * 4 + q % 4
        for x in range(4):
            for h in range(2):
                for i, d in enumerate(CHIPS):
                    right[2 * x + c, h * 4 + i] = 2 * ((x + d) % 4) + (c + h) % 2
    return left, right


def local(grad, moment, second, left_basis, right_basis):
    row, col = lax.axis_index("row"), lax.axis_index("col")
    core = (row % 2).reshape(1).astype(jnp.int32)
    by_col, by_row = tables()
    order = jnp.asarray(by_col)[row % 2, col]
    order_r = jnp.asarray(by_row)[row]

    left_other = swap(left_basis)
    moment_new, keep, give = start(core, grad, moment)
    plus_keep, minus_keep = along_x(keep, -1), along_x(keep, 1)
    moved = swap(give)
    left = order_left(order, left_basis)
    right = order_right(order_r, right_basis)
    plus_moved, minus_moved = along_x(moved, -1), along_x(moved, 1)
    far_keep, far_moved = along_x(plus_keep, -1), along_x(minus_moved, 1)
    left = [*left, *order_left(order, left_other, (right[0],))]

    chunks = [
        ((0,), [keep, moved]),
        ((1, 3), [plus_keep, plus_moved, minus_keep, minus_moved]),
        ((2,), [far_keep, far_moved]),
    ]
    far, near, parts = [None] * 3, [None] * 3, [None] * 3

    def step_far(i, after=()):
        one, two = project_far(chunks[i][1], left, after)
        far[i] = first(one, 1), first(two, -1)
        return (one,)

    def step_near(i, after=()):
        up, down = project_near(chunks[i][1], left, *far[i], after)
        near[i] = first(up, 1), first(down, -1)
        return (up,)

    def step_own(i, after=()):
        q = project_own(chunks[i][1], left, *near[i], after)
        parts[i] = [q[0], second_axis(q[1], 1), second_axis(q[3], -1), second_axis(q[2], 2)]
        return (q[0],)

    done = step_far(0, (plus_keep, minus_keep))
    done = step_near(0, done)
    done = step_far(1, done)
    done = step_own(0, done)
    done = step_far(2, done)
    done = step_near(1, done)
    part = rotate(parts[0], right, chunks[0][0])
    done = step_near(2, (*done, part))
    done = step_own(1, done)
    done = step_own(2, done)
    part = rotate(parts[1], right, chunks[1][0], part)
    part = rotate(parts[2], right, chunks[2][0], part, last=True)
    own, other = part
    other = swap(other)

    second_new, keep, give = turn(core, own, other, second, right)
    share = jnp.stack([keep, swap(give)], axis=0)
    shares = [share, second_axis(share, -1), second_axis(share, -2), second_axis(share, 1)]

    block_a = lay(shares, 0)
    plus_a, minus_a = first(block_a, -1), first(block_a, 1)
    sums = back_project([(0, [block_a])], left)
    far_a, far_b = forward(plus_a, minus_a, (sums,))
    block_b = lay(shares, 1, (far_a,))
    far_a, far_b = first(far_a, -1), first(far_b, 1)
    plus_b, minus_b = first(block_b, -1), first(block_b, 1)
    sums = back_project([(1, [plus_a]), (3, [minus_a])], left, sums, after=(block_b,))
    u1, u3 = back_project([(2, [far_a, far_b])], left, sums, cut=True)
    got1, got3 = along_x(u1, 1), along_x(u3, -1)
    squares = (block_a[1024:, :128] + plus_a[1024:, :128]) + (minus_a[1024:, :128] + far_b[512:, :128])
    squares = squares + move(squares, lambda x, c, y, z: (x ^ 1, c, y, z))
    squares = squares + move(squares, lambda x, c, y, z: (x ^ 2, c, y, z))
    sums = back_project([(0, [block_b])], left, after=(u1,))
    far_a, far_b = forward(plus_b, minus_b, (sums,))
    far_a, far_b = first(far_a, -1), first(far_b, 1)
    sums = back_project([(1, [plus_b]), (3, [minus_b])], left, sums)
    u2, u0 = back_project([(2, [far_a, far_b])], left, sums, cut=True, after=(squares, got1, got3))
    total = jnp.sum(squares)
    factor = jnp.minimum(1.0, clip_share * jnp.sqrt(jnp.float32(M * N)) / (jnp.sqrt(total) + 1e-06))
    update = ((u0 + got1) + (got3 + along_x(u2, 2))) * factor
    return (update, moment_new, second_new)


def solution(mesh):
    return jax.shard_map(
        local,
        mesh=mesh,
        in_specs=(P("col", "row"), P("col", "row"), P(("row", "col"), None), P("col", "row"), P()),
        out_specs=(P("col", "row"), P("col", "row"), P(("row", "col"), None)),
        check_vma=False,
    )
```

```python
import functools
import math

import jax
import jax.numpy as jnp
import numpy as np
from jax import lax
from jax.experimental import pallas as pl
from jax.experimental.pallas import tpu as pltpu
from jax.sharding import PartitionSpec as P

M = 16384
N = 1024

first_decay = 0.9
second_decay = 0.95
epsilon = 1e-08
clip_share = 0.25

f32, bf16 = jnp.float32, jnp.bfloat16
BOTH = ("row", "col")
VMEM_LIMIT = 10 * 1024 * 1024
CHIPS = (1, 3, 2, 0)
LONG = 10**11
WHOLE = pl.BlockSpec(memory_space=pltpu.VMEM)
SCALARS = pl.BlockSpec(memory_space=pltpu.SMEM)
ANYWHERE = pl.BlockSpec(memory_space=pl.ANY)


def call(kernel, name, args, out_shape, specs=None, scratch=(), after=(), hold=(), cost=1):
    n, k = len(args), len(after) + len(hold)

    def body(*refs):
        kernel(*refs[:n], *refs[n + k :])

    return pl.pallas_call(
        body,
        in_specs=(specs or [WHOLE] * n) + [ANYWHERE] * len(after) + [WHOLE] * len(hold),
        out_specs=[WHOLE] * len(out_shape),
        out_shape=out_shape,
        scratch_shapes=list(scratch),
        compiler_params=pltpu.CompilerParams(vmem_limit_bytes=VMEM_LIMIT),
        cost_estimate=pl.CostEstimate(flops=cost, bytes_accessed=cost, transcendentals=0),
        name=name,
    )(*args, *after, *hold)


def shape(rows, columns, dtype=f32):
    return jax.ShapeDtypeStruct((rows, columns), dtype)


def split(value):
    high = value.astype(bf16)
    return high, (value - high.astype(f32)).astype(bf16)


def dot3(a_high, a_low, b_high, b_low, dims=(((1,), (0,)), ((), ()))):
    d = functools.partial(lax.dot_general, dimension_numbers=dims, preferred_element_type=f32)
    return d(a_high, b_high) + (d(a_high, b_low) + d(a_low, b_high))


def move(value, step):
    pairs = []
    for x in range(4):
        for c in range(2):
            for y in range(4):
                for z in range(4):
                    tx, tc, ty, tz = step(x, c, y, z)
                    pairs.append(((2 * x + c) * 16 + 4 * y + z, (2 * (tx % 4) + tc) * 16 + 4 * (ty % 4) + tz % 4))
    return lax.ppermute(value, BOTH, pairs)


def swap(value):
    return move(value, lambda x, c, y, z: (x, 1 - c, y, z))


def along_x(value, d):
    return move(value, lambda x, c, y, z: (x + d, c, y, z))


def first(value, d):
    return move(value, lambda x, c, y, z: (x, c, y + d, z) if c == 0 else (x, c, y, z + d))


def second_axis(value, d):
    return move(value, lambda x, c, y, z: (x, c, y, z + d) if c == 0 else (x, c, y + d, z))


def start(core, grad, moment):
    def kernel(core_ref, grad_ref, moment_ref, new_ref, both_ref, give_ref):
        g = grad_ref[...]
        new = first_decay * moment_ref[...] + (1.0 - first_decay) * g
        new_ref[...] = new
        g, new = g.T, new.T
        zero = core_ref[0] == 0
        both_ref[0:128, :] = jnp.where(zero, g, new)
        give = jnp.where(zero, new, g)
        both_ref[128:256, :] = give
        give_ref[...] = give

    return call(
        kernel, "start", [core, grad, moment], [shape(1024, 128), shape(256, 1024), shape(128, 1024)], [SCALARS, WHOLE, WHOLE]
    )


def order_left(order, left, hold=()):
    steps, slots = 8, 2

    def kernel(order_ref, left_ref, high_ref, low_ref, held, arrived):
        def copy(i):
            return pltpu.make_async_copy(left_ref.at[pl.ds(i * 128, 128), :], held.at[i % slots], arrived.at[i % slots])

        for i in range(slots):
            copy(i).start()
        for i in range(steps):
            copy(i).wait()
            rows = slice(i * 128, i * 128 + 128)
            for a in range(4):
                for b in range(4):
                    at = pl.multiple_of(order_ref[a * 4 + b] * 128, 128)
                    high, low = split(held[i % slots, :, pl.ds(at, 128)])
                    high_ref[a, rows, b * 128 : b * 128 + 128] = high
                    low_ref[a, rows, b * 128 : b * 128 + 128] = low
            if i + slots < steps:
                copy(i + slots).start()

    return call(
        kernel, "order_left", [order, left], [jax.ShapeDtypeStruct((4, 1024, 512), bf16)] * 2, [SCALARS, pl.BlockSpec(memory_space=pltpu.HBM)],
        [pltpu.VMEM((slots, 128, 2048), f32), pltpu.SemaphoreType.DMA((slots,))], hold=hold,
    )


def order_right(order, right, after=()):
    def kernel(order_ref, right_ref, high_ref, low_ref):
        for i in range(8):
            at = pl.multiple_of(order_ref[i] * 128, 128)
            rows = slice(i * 128, i * 128 + 128)
            high_ref[rows, :], low_ref[rows, :] = split(right_ref[pl.ds(at, 128), :])

    return call(kernel, "order_right", [order, right], [shape(1024, 1024, bf16)] * 2, [SCALARS, WHOLE], after=after)


def fill(refs, blocks, high, low):
    at = 0
    for ref, (_, begin, size) in zip(refs, blocks):
        high[at : at + size, :], low[at : at + size, :] = split(ref[begin : begin + size, :])
        at += size


def project_far(blocks, left, after=()):
    rows = sum(size for _, _, size in blocks)
    n = len(blocks)

    def kernel(*refs):
        l_refs, outs, (gh, gl) = refs[n : n + 4], refs[n + 4 : n + 6], refs[n + 6 :]
        fill(refs[:n], blocks, gh, gl)
        for h in range(2):
            for t in range(2):
                c = slice(t * 256, t * 256 + 256)
                outs[h][:, c] = dot3(gh[...], gl[...], l_refs[2 * h][2, :, c], l_refs[2 * h + 1][2, :, c])

    return call(
        kernel, "project_far", [*[b[0] for b in blocks], *left], [shape(rows, 512)] * 2, None, [pltpu.VMEM((rows, 1024), bf16)] * 2, after
    )


def project_near(blocks, left, near, far, begin, after=(), cost=1):
    rows = sum(size for _, _, size in blocks)
    n = len(blocks)

    def kernel(*refs):
        l_refs, more, outs, (gh, gl) = refs[n : n + 4], refs[n + 4 : n + 6], refs[n + 6 : n + 8], refs[n + 8 :]
        fill(refs[:n], blocks, gh, gl)
        for i, d in enumerate((1, 3)):
            for h in range(2):
                for t in range(2):
                    c = slice(t * 256, t * 256 + 256)
                    value = dot3(gh[...], gl[...], l_refs[2 * h][d, :, c], l_refs[2 * h + 1][d, :, c])
                    if h == i:
                        value = value + more[i][begin : begin + rows, c]
                    outs[i][:, h * 512 + t * 256 : h * 512 + t * 256 + 256] = value

    return call(
        kernel, "project_near", [*[b[0] for b in blocks], *left, near, far], [shape(rows, 1024)] * 2, None,
        [pltpu.VMEM((rows, 1024), bf16)] * 2, after, cost=cost,
    )


def project_own(blocks, left, up, down, after=(), cost=1):
    rows = sum(size for _, _, size in blocks)
    n = len(blocks)

    def kernel(*refs):
        l_refs, (up_ref, down_ref), outs, (gh, gl) = refs[n : n + 4], refs[n + 4 : n + 6], refs[n + 6 : n + 10], refs[n + 10 :]
        fill(refs[:n], blocks, gh, gl)
        for d in range(4):
            c = slice(d * 128, d * 128 + 128)
            high = jnp.concatenate([l_refs[0][0, :, c], l_refs[2][0, :, c]], axis=1)
            low = jnp.concatenate([l_refs[1][0, :, c], l_refs[3][0, :, c]], axis=1)
            value = dot3(gh[...], gl[...], high, low)
            for h in range(2):
                e = slice(h * 512 + d * 128, h * 512 + d * 128 + 128)
                outs[d][:, h * 128 : h * 128 + 128] = value[:, h * 128 : h * 128 + 128] + up_ref[:, e] + down_ref[:, e]

    return call(
        kernel, "project_own", [*[b[0] for b in blocks], *left, up, down], [shape(rows, 256)] * 4, None, [pltpu.VMEM((rows, 1024), bf16)] * 2,
        after, cost=cost,
    )


def rotate(parts, right, chips, before=None, last=False):
    n = 6 + (before is not None)

    def kernel(*refs):
        p, (rh, rl) = refs[:4], refs[4:6]
        total = (p[0][...] + p[1][...]) + (p[2][...] + p[3][...])
        high, low = split(total.T)
        places = [h * 512 + CHIPS.index(d) * 128 for d in chips for h in range(2)]
        for t in range(4):
            c = slice(t * 256, t * 256 + 256)
            r_high = jnp.concatenate([rh[p : p + 128, c] for p in places], axis=0)
            r_low = jnp.concatenate([rl[p : p + 128, c] for p in places], axis=0)
            value = dot3(high, low, r_high, r_low)
            if before is not None:
                value = value + refs[6][:, c]
            if last:
                refs[n][:, c] = value[:128]
                refs[n + 1][:, c] = value[128:]
            else:
                refs[n][:, c] = value

    out = call(
        kernel, "rotate", [*parts, *right] + ([before] if n > 6 else []), [shape(128, 1024)] * 2 if last else [shape(256, 1024)]
    )
    return out if last else out[0]


def turn(core, own, other, second, right):
    def kernel(core_ref, own_ref, other_ref, second_ref, rh, rl, new_ref, keep_ref, give_ref):
        zero = core_ref[0] == 0
        a, b = own_ref[...], other_ref[...]
        g, m = jnp.where(zero, a, b), jnp.where(zero, b, a)
        new = second_decay * second_ref[...] + (1.0 - second_decay) * g * g
        new_ref[...] = new
        rotated = m / (jnp.sqrt(new) + epsilon)
        high, low = split(rotated)
        squares = rotated * rotated
        total = squares[0:8, :]
        for i in range(1, 16):
            total = total + squares[i * 8 : i * 8 + 8, :]
        narrow = total[:, 0:128]
        for i in range(1, 8):
            narrow = narrow + total[:, i * 128 : i * 128 + 128]
        zeros = jnp.zeros((8, 128), f32)
        for out, h in ((give_ref, 1), (keep_ref, 0)):
            for t in range(2):
                r = slice(h * 512 + t * 256, h * 512 + t * 256 + 256)
                out[0:128, t * 256 : t * 256 + 256] = dot3(high, low, rh[r, :], rl[r, :], (((1,), (1,)), ((), ())))
            out[128:136, :] = jnp.concatenate([narrow, zeros, narrow, zeros], axis=1)

    return call(
        kernel, "turn", [core, own, other, second, *right], [shape(128, 1024), shape(136, 512), shape(136, 512)],
        [SCALARS] + [WHOLE] * 5,
    )


def back_project(terms, left, before=None, cut=False, after=(), cost=1):
    arrays = [a for _, group in terms for a in group]
    n = len(arrays)

    def kernel(*refs):
        l_refs = refs[n : n + 4]
        sh, sl = refs[-2:]
        outs = refs[n + 4 + (before is not None) : -2]
        at, index = 0, 0
        extra = refs[n + 4][1024:1032, :] if before is not None else jnp.zeros((8, 256), f32)
        for _, group in terms:
            size = 1024 // len(group)
            for _ in group:
                sh[at : at + size, :], sl[at : at + size, :] = split(refs[index][0:size, :])
                if refs[index].shape[0] > size:
                    extra = extra + refs[index][size : size + 8, :]
                at, index = at + size, index + 1
        for t in range(4):
            r = slice(t * 256, t * 256 + 256)
            value = refs[n + 4][r, :] if before is not None else None
            for i, (d, _) in enumerate(terms):
                for h in range(2):
                    rows = slice(i * 1024 + h * 512, i * 1024 + h * 512 + 512)
                    new = dot3(l_refs[2 * h][d, r, :], l_refs[2 * h + 1][d, r, :], sh[rows, :], sl[rows, :])
                    value = new if value is None else value + new
            if cut:
                outs[0][r, :] = value[:, :128]
                outs[1][r, :] = value[:, 128:]
            else:
                outs[0][r, :] = value
        if cut:
            outs[0][1024:1032, :] = extra[:, :128]
            outs[1][1024:1032, :] = extra[:, :128]
        else:
            outs[0][1024:1032, :] = extra

    out = call(
        kernel, "back_project", [*arrays, *left] + ([] if before is None else [before]),
        [shape(1032, 128)] * 2 if cut else [shape(1032, 256)], None, [pltpu.VMEM((1024 * len(terms), 256), bf16)] * 2, after,
        cost=cost,
    )
    return out if cut else out[0]


def finish(parts):
    def kernel(a, b, c, d, out):
        rows = slice(1024, 1032)
        squares = (a[rows, :] + b[rows, :]) + (c[rows, :] + d[rows, :])
        total = jnp.sum(jnp.sum(squares, axis=0, keepdims=True), axis=1, keepdims=True)
        factor = jnp.minimum(1.0, clip_share * math.sqrt(M * N) / (jnp.sqrt(total) + 1e-06))
        rows = slice(0, 1024)
        out[...] = ((a[rows, :] + b[rows, :]) + (c[rows, :] + d[rows, :])) * factor

    return call(kernel, "finish", list(parts), [shape(1024, 128)])[0]


def lay(shares, half, after=()):
    def kernel(*refs):
        out = refs[-1]
        c = slice(half * 256, half * 256 + 256)
        extra = jnp.zeros((8, 256), f32)
        for d in range(4):
            for h in range(2):
                out[(h * 4 + d) * 128 : (h * 4 + d) * 128 + 128, :] = refs[d][h, 0:128, c]
                extra = extra + refs[d][h, 128:136, c]
        out[1024:1032, :] = extra

    return call(kernel, "lay", list(shares), [shape(1032, 256)], after=after)[0]


def forward(plus, minus, rows, others, after):
    def kernel(plus_ref, minus_ref, one, two):
        one[...] = plus_ref[rows[0] : rows[1], :]
        two[...] = minus_ref[others[0] : others[1], :]

    columns = plus.shape[1]
    outs = [shape(rows[1] - rows[0], columns), shape(others[1] - others[0], columns)]
    return call(kernel, "forward", [plus, minus], outs, after=after)


def tables():
    left = np.zeros((2, 16, 16), np.int32)
    right = np.zeros((8, 8), np.int32)
    for c in range(2):
        for y in range(4):
            for z in range(4):
                for a in range(4):
                    for b in range(4):
                        p, q = (y + a, z + b) if c == 0 else (y + b, z + a)
                        left[c, y * 4 + z, a * 4 + b] = p % 4 * 4 + q % 4
        for x in range(4):
            for h in range(2):
                for i, d in enumerate(CHIPS):
                    right[2 * x + c, h * 4 + i] = 2 * ((x + d) % 4) + (c + h) % 2
    return left, right


def local(grad, moment, second, left_basis, right_basis):
    row, col = lax.axis_index("row"), lax.axis_index("col")
    core = (row % 2).reshape(1).astype(jnp.int32)
    by_col, by_row = tables()
    order = jnp.asarray(by_col)[row % 2, col]
    order_r = jnp.asarray(by_row)[row]

    left_other = swap(left_basis)
    moment_new, both, give = start(core, grad, moment)
    plus, minus = along_x(both, -1), along_x(both, 1)
    moved = swap(give)
    right = order_right(order_r, right_basis, (both,))
    left = order_left(order, left_basis, right)
    left = [*left, *order_left(order, left_other, left)]

    one, two = project_far([(both, 0, 128), (moved, 0, 128)], left)
    far_keep, far_give = forward(plus, minus, (0, 128), (128, 256), (one,))
    far_keep, far_give = along_x(far_keep, -1), along_x(far_give, 1)
    plus_other, minus_other = swap(plus), swap(minus)
    far_moved = swap(far_give)

    chips = [(0,), (1, 3), (2,)]
    blocks = [
        [(both, 0, 128), (moved, 0, 128)],
        [(plus, 0, 128), (plus_other, 128, 128), (minus, 0, 128), (minus_other, 128, 128)],
        [(far_keep, 0, 128), (far_moved, 0, 128)],
    ]

    def own_step(i, near, after, cost=1):
        q = project_own(blocks[i], left, *near, after, cost)
        return [q[0], second_axis(q[1], 1), second_axis(q[3], -1), second_axis(q[2], 2)]

    one, two = first(one, 1), first(two, -1)
    up, down = project_near(blocks[0], left, one, two, 0, (far_keep, far_give), LONG)
    near = first(up, 1), first(down, -1)
    one, two = project_far(blocks[1] + blocks[2], left, (up,))
    more = first(one, 1), first(two, -1)
    parts = own_step(0, near, (one,), LONG)
    part = rotate(parts, right, chips[0])
    up1, down1 = project_near(blocks[1], left, *more, 0, (part,))
    up2, down2 = project_near(blocks[2], left, *more, 512, (up1,))
    near1 = first(up1, 1), first(down1, -1)
    near2 = first(up2, 1), first(down2, -1)
    parts1 = own_step(1, near1, (up2,))
    parts2 = own_step(2, near2, (parts1[0],))
    part = rotate(parts1, right, chips[1], part)
    part = rotate(parts2, right, chips[2], part, last=True)
    own, other = part
    other = swap(other)

    second_new, keep, give = turn(core, own, other, second, right)
    share = jnp.stack([keep, swap(give)], axis=0)
    shares = [share, second_axis(share, -1), second_axis(share, -2), second_axis(share, 1)]

    block_a = lay(shares, 0)
    plus_a, minus_a = first(block_a, -1), first(block_a, 1)
    sums_a = back_project([(0, [block_a])], left)
    far_a1, far_a3 = forward(plus_a, minus_a, (0, 512), (512, 1032), (sums_a,))
    block_b = lay(shares, 1, (far_a1,))
    far_a1, far_a3 = first(far_a1, -1), first(far_a3, 1)
    plus_b, minus_b = first(block_b, -1), first(block_b, 1)
    sums_a = back_project([(1, [plus_a]), (3, [minus_a])], left, sums_a, after=(block_b,))
    u1, u3 = back_project([(2, [far_a1, far_a3])], left, sums_a, cut=True)
    sums_b = back_project([(0, [block_b])], left, after=(u1,), cost=LONG)
    far_b1, far_b3 = forward(plus_b, minus_b, (0, 512), (512, 1032), (sums_b,))
    sums_b = back_project([(1, [plus_b]), (3, [minus_b])], left, sums_b, after=(far_b1,))
    far_b1, far_b3 = first(far_b1, -1), first(far_b3, 1)
    u2, u0 = back_project([(2, [far_b1, far_b3])], left, sums_b, cut=True)
    update = finish([u0, along_x(u1, 1), along_x(u3, -1), along_x(u2, 2)])
    return (update, moment_new, second_new)


def solution(mesh):
    return jax.shard_map(
        local,
        mesh=mesh,
        in_specs=(P("col", "row"), P("col", "row"), P(("row", "col"), None), P("col", "row"), P()),
        out_specs=(P("col", "row"), P("col", "row"), P(("row", "col"), None)),
        check_vma=False,
    )
```

```python
import functools
import math

import jax
import jax.numpy as jnp
import numpy as np
from jax import lax
from jax.experimental import pallas as pl
from jax.experimental.pallas import tpu as pltpu
from jax.sharding import PartitionSpec as P

M = 16384
N = 1024

first_decay = 0.9
second_decay = 0.95
epsilon = 1e-08
clip_share = 0.25

f32, bf16 = jnp.float32, jnp.bfloat16
BOTH = ("row", "col")
VMEM_LIMIT = 10 * 1024 * 1024
CHIPS = (1, 3, 2, 0)
LONG = 10**11
WHOLE = pl.BlockSpec(memory_space=pltpu.VMEM)
SCALARS = pl.BlockSpec(memory_space=pltpu.SMEM)
ANYWHERE = pl.BlockSpec(memory_space=pl.ANY)


def call(kernel, name, args, out_shape, specs=None, scratch=(), after=(), hold=(), cost=1):
    n, k = len(args), len(after) + len(hold)

    def body(*refs):
        kernel(*refs[:n], *refs[n + k :])

    return pl.pallas_call(
        body,
        in_specs=(specs or [WHOLE] * n) + [ANYWHERE] * len(after) + [WHOLE] * len(hold),
        out_specs=[WHOLE] * len(out_shape),
        out_shape=out_shape,
        scratch_shapes=list(scratch),
        compiler_params=pltpu.CompilerParams(vmem_limit_bytes=VMEM_LIMIT),
        cost_estimate=pl.CostEstimate(flops=cost, bytes_accessed=cost, transcendentals=0),
        name=name,
    )(*args, *after, *hold)


def shape(rows, columns, dtype=f32):
    return jax.ShapeDtypeStruct((rows, columns), dtype)


def split(value):
    high = value.astype(bf16)
    return high, (value - high.astype(f32)).astype(bf16)


def dot3(a_high, a_low, b_high, b_low, dims=(((1,), (0,)), ((), ()))):
    d = functools.partial(lax.dot_general, dimension_numbers=dims, preferred_element_type=f32)
    return d(a_high, b_high) + (d(a_high, b_low) + d(a_low, b_high))


def move(value, step):
    pairs = []
    for x in range(4):
        for c in range(2):
            for y in range(4):
                for z in range(4):
                    tx, tc, ty, tz = step(x, c, y, z)
                    pairs.append(((2 * x + c) * 16 + 4 * y + z, (2 * (tx % 4) + tc) * 16 + 4 * (ty % 4) + tz % 4))
    return lax.ppermute(value, BOTH, pairs)


def swap(value):
    return move(value, lambda x, c, y, z: (x, 1 - c, y, z))


def along_x(value, d):
    return move(value, lambda x, c, y, z: (x + d, c, y, z))


def first(value, d):
    return move(value, lambda x, c, y, z: (x, c, y + d, z) if c == 0 else (x, c, y, z + d))


def second_axis(value, d):
    return move(value, lambda x, c, y, z: (x, c, y, z + d) if c == 0 else (x, c, y + d, z))


def start(core, grad, moment):
    def kernel(core_ref, grad_ref, moment_ref, new_ref, both_ref, give_ref):
        g = grad_ref[...]
        new = first_decay * moment_ref[...] + (1.0 - first_decay) * g
        new_ref[...] = new
        g, new = g.T, new.T
        zero = core_ref[0] == 0
        both_ref[0:128, :] = jnp.where(zero, g, new)
        give = jnp.where(zero, new, g)
        both_ref[128:256, :] = give
        give_ref[...] = give

    return call(
        kernel, "start", [core, grad, moment], [shape(1024, 128), shape(256, 1024), shape(128, 1024)], [SCALARS, WHOLE, WHOLE]
    )


def order_left(order, left, hold=()):
    steps, slots = 8, 2

    def kernel(order_ref, left_ref, high_ref, low_ref, held, arrived):
        def copy(i):
            return pltpu.make_async_copy(left_ref.at[pl.ds(i * 128, 128), :], held.at[i % slots], arrived.at[i % slots])

        for i in range(slots):
            copy(i).start()
        for i in range(steps):
            copy(i).wait()
            rows = slice(i * 128, i * 128 + 128)
            for a in range(4):
                for b in range(4):
                    at = pl.multiple_of(order_ref[a * 4 + b] * 128, 128)
                    high, low = split(held[i % slots, :, pl.ds(at, 128)])
                    high_ref[a, rows, b * 128 : b * 128 + 128] = high
                    low_ref[a, rows, b * 128 : b * 128 + 128] = low
            if i + slots < steps:
                copy(i + slots).start()

    return call(
        kernel, "order_left", [order, left], [jax.ShapeDtypeStruct((4, 1024, 512), bf16)] * 2, [SCALARS, pl.BlockSpec(memory_space=pltpu.HBM)],
        [pltpu.VMEM((slots, 128, 2048), f32), pltpu.SemaphoreType.DMA((slots,))], hold=hold,
    )


def pick(order, right, places, columns):
    rows = [right[pl.ds(pl.multiple_of(order[p] * 128, 128), 128), columns] for p in places]
    return split(jnp.concatenate(rows, axis=0))


def fill(refs, blocks, high, low):
    at = 0
    for ref, (_, begin, size) in zip(refs, blocks):
        high[at : at + size, :], low[at : at + size, :] = split(ref[begin : begin + size, :])
        at += size


def project_far(blocks, left, after=()):
    rows = sum(size for _, _, size in blocks)
    n = len(blocks)

    def kernel(*refs):
        l_refs, outs, (gh, gl) = refs[n : n + 4], refs[n + 4 : n + 6], refs[n + 6 :]
        fill(refs[:n], blocks, gh, gl)
        for h in range(2):
            for t in range(2):
                c = slice(t * 256, t * 256 + 256)
                outs[h][:, c] = dot3(gh[...], gl[...], l_refs[2 * h][2, :, c], l_refs[2 * h + 1][2, :, c])

    return call(
        kernel, "project_far", [*[b[0] for b in blocks], *left], [shape(rows, 512)] * 2, None, [pltpu.VMEM((rows, 1024), bf16)] * 2, after
    )


def project_side(blocks, left, d, more=None, half=0, begin=0, after=(), cost=1):
    rows = sum(size for _, _, size in blocks)
    n = len(blocks)
    extra = [] if more is None else [more]

    def kernel(*refs):
        l_refs, out, (gh, gl) = refs[n : n + 4], refs[-3], refs[-2:]
        fill(refs[:n], blocks, gh, gl)
        for h in range(2):
            for t in range(2):
                c = slice(t * 256, t * 256 + 256)
                value = dot3(gh[...], gl[...], l_refs[2 * h][d, :, c], l_refs[2 * h + 1][d, :, c])
                if extra and h == half:
                    value = value + refs[n + 4][begin : begin + rows, c]
                out[:, h * 512 + t * 256 : h * 512 + t * 256 + 256] = value

    return call(
        kernel, "project_side", [*[b[0] for b in blocks], *left, *extra], [shape(rows, 1024)], None,
        [pltpu.VMEM((rows, 1024), bf16)] * 2, after, cost=cost,
    )[0]


def project_own(blocks, left, came, after=(), cost=1):
    rows = sum(size for _, _, size in blocks)
    n, m = len(blocks), len(came)

    def kernel(*refs):
        l_refs, came_refs = refs[n : n + 4], refs[n + 4 : n + 4 + m]
        outs, (gh, gl) = refs[n + 4 + m : n + 8 + m], refs[n + 8 + m :]
        fill(refs[:n], blocks, gh, gl)
        for d in range(4):
            c = slice(d * 128, d * 128 + 128)
            high = jnp.concatenate([l_refs[0][0, :, c], l_refs[2][0, :, c]], axis=1)
            low = jnp.concatenate([l_refs[1][0, :, c], l_refs[3][0, :, c]], axis=1)
            value = dot3(gh[...], gl[...], high, low)
            for h in range(2):
                e = slice(h * 512 + d * 128, h * 512 + d * 128 + 128)
                part = value[:, h * 128 : h * 128 + 128]
                for ref in came_refs:
                    part = part + ref[:, e]
                outs[d][:, h * 128 : h * 128 + 128] = part

    return call(
        kernel, "project_own", [*[b[0] for b in blocks], *left, *came], [shape(rows, 256)] * 4, None,
        [pltpu.VMEM((rows, 1024), bf16)] * 2, after, cost=cost,
    )


def add(parts, after=()):
    def kernel(a, b, c, d, out):
        out[...] = (a[...] + b[...]) + (c[...] + d[...])

    return call(kernel, "add", list(parts), [shape(*parts[0].shape)], after=after, cost=LONG)[0]


def rotate(groups, order, right, chips):
    parts = [p for group in groups for p in group]
    n = len(parts)

    def kernel(order_ref, *refs):
        right_ref, outs = refs[n], refs[n + 1 :]
        sums, at = [], 0
        for group in groups:
            total = refs[at][...]
            for i in range(1, len(group)):
                total = total + refs[at + i][...]
            sums.append(total.T)
            at += len(group)
        high, low = split(jnp.concatenate(sums, axis=1))
        places = [h * 4 + CHIPS.index(d) for d in chips for h in range(2)]
        for t in range(4):
            c = slice(t * 256, t * 256 + 256)
            value = dot3(high, low, *pick(order_ref, right_ref, places, c))
            outs[0][:, c] = value[:128]
            outs[1][:, c] = value[128:]

    return call(
        kernel, "rotate", [order, *parts, right], [shape(128, 1024)] * 2, [SCALARS] + [WHOLE] * (n + 1)
    )


def turn(core, order, own, other, second, right):
    def kernel(core_ref, order_ref, own_ref, other_ref, second_ref, right_ref, new_ref, keep_ref, give_ref):
        zero = core_ref[0] == 0
        a, b = own_ref[...], other_ref[...]
        g, m = jnp.where(zero, a, b), jnp.where(zero, b, a)
        new = second_decay * second_ref[...] + (1.0 - second_decay) * g * g
        new_ref[...] = new
        rotated = m / (jnp.sqrt(new) + epsilon)
        high, low = split(rotated)
        squares = rotated * rotated
        total = squares[0:8, :]
        for i in range(1, 16):
            total = total + squares[i * 8 : i * 8 + 8, :]
        narrow = total[:, 0:128]
        for i in range(1, 8):
            narrow = narrow + total[:, i * 128 : i * 128 + 128]
        zeros = jnp.zeros((8, 128), f32)
        for out, h in ((give_ref, 1), (keep_ref, 0)):
            for t in range(2):
                rows = pick(order_ref, right_ref, [h * 4 + t * 2, h * 4 + t * 2 + 1], slice(0, 1024))
                out[0:128, t * 256 : t * 256 + 256] = dot3(high, low, *rows, (((1,), (1,)), ((), ())))
            out[128:136, :] = jnp.concatenate([narrow, zeros, narrow, zeros], axis=1)

    return call(
        kernel, "turn", [core, order, own, other, second, right], [shape(128, 1024), shape(136, 512), shape(136, 512)],
        [SCALARS] * 2 + [WHOLE] * 4,
    )


def back_project(terms, left, before=None, cut=False, after=(), cost=1):
    arrays = [a for _, group in terms for a in group]
    n = len(arrays)

    def kernel(*refs):
        l_refs = refs[n : n + 4]
        sh, sl = refs[-2:]
        outs = refs[n + 4 + (before is not None) : -2]
        at, index = 0, 0
        extra = refs[n + 4][1024:1032, :] if before is not None else jnp.zeros((8, 256), f32)
        for _, group in terms:
            size = 1024 // len(group)
            for _ in group:
                sh[at : at + size, :], sl[at : at + size, :] = split(refs[index][0:size, :])
                if refs[index].shape[0] > size:
                    extra = extra + refs[index][size : size + 8, :]
                at, index = at + size, index + 1
        for t in range(4):
            r = slice(t * 256, t * 256 + 256)
            value = refs[n + 4][r, :] if before is not None else None
            for i, (d, _) in enumerate(terms):
                for h in range(2):
                    rows = slice(i * 1024 + h * 512, i * 1024 + h * 512 + 512)
                    new = dot3(l_refs[2 * h][d, r, :], l_refs[2 * h + 1][d, r, :], sh[rows, :], sl[rows, :])
                    value = new if value is None else value + new
            if cut:
                outs[0][r, :] = value[:, :128]
                outs[1][r, :] = value[:, 128:]
            else:
                outs[0][r, :] = value
        if cut:
            outs[0][1024:1032, :] = extra[:, :128]
            outs[1][1024:1032, :] = extra[:, :128]
        else:
            outs[0][1024:1032, :] = extra

    out = call(
        kernel, "back_project", [*arrays, *left] + ([] if before is None else [before]),
        [shape(1032, 128)] * 2 if cut else [shape(1032, 256)], None, [pltpu.VMEM((1024 * len(terms), 256), bf16)] * 2, after,
        cost=cost,
    )
    return out if cut else out[0]


def finish(parts):
    def kernel(a, b, c, d, out):
        rows = slice(1024, 1032)
        squares = (a[rows, :] + b[rows, :]) + (c[rows, :] + d[rows, :])
        total = jnp.sum(jnp.sum(squares, axis=0, keepdims=True), axis=1, keepdims=True)
        factor = jnp.minimum(1.0, clip_share * math.sqrt(M * N) / (jnp.sqrt(total) + 1e-06))
        rows = slice(0, 1024)
        out[...] = ((a[rows, :] + b[rows, :]) + (c[rows, :] + d[rows, :])) * factor

    return call(kernel, "finish", list(parts), [shape(1024, 128)])[0]


def lay(shares, half, after=()):
    def kernel(*refs):
        out = refs[-1]
        c = slice(half * 256, half * 256 + 256)
        extra = jnp.zeros((8, 256), f32)
        for d in range(4):
            for h in range(2):
                out[(h * 4 + d) * 128 : (h * 4 + d) * 128 + 128, :] = refs[d][h, 0:128, c]
                extra = extra + refs[d][h, 128:136, c]
        out[1024:1032, :] = extra

    return call(kernel, "lay", list(shares), [shape(1032, 256)], after=after)[0]


def gather(arrays, after):
    def kernel(*refs):
        for i in range(len(arrays)):
            refs[-1][i * 128 : i * 128 + 128, :] = refs[i][128:256, :]

    return call(kernel, "gather", list(arrays), [shape(128 * len(arrays), 1024)], after=after, cost=LONG)[0]


def forward(plus, minus, rows, others, after):
    def kernel(plus_ref, minus_ref, one, two):
        one[...] = plus_ref[rows[0] : rows[1], :]
        two[...] = minus_ref[others[0] : others[1], :]

    columns = plus.shape[1]
    outs = [shape(rows[1] - rows[0], columns), shape(others[1] - others[0], columns)]
    return call(kernel, "forward", [plus, minus], outs, after=after)


def tables():
    left = np.zeros((2, 16, 16), np.int32)
    right = np.zeros((8, 8), np.int32)
    for c in range(2):
        for y in range(4):
            for z in range(4):
                for a in range(4):
                    for b in range(4):
                        p, q = (y + a, z + b) if c == 0 else (y + b, z + a)
                        left[c, y * 4 + z, a * 4 + b] = p % 4 * 4 + q % 4
        for x in range(4):
            for h in range(2):
                for i, d in enumerate(CHIPS):
                    right[2 * x + c, h * 4 + i] = 2 * ((x + d) % 4) + (c + h) % 2
    return left, right


def local(grad, moment, second, left_basis, right_basis):
    row, col = lax.axis_index("row"), lax.axis_index("col")
    core = (row % 2).reshape(1).astype(jnp.int32)
    by_col, by_row = tables()
    order = jnp.asarray(by_col)[row % 2, col]
    order_r = jnp.asarray(by_row)[row]

    left_other = swap(left_basis)
    moment_new, both, give = start(core, grad, moment)
    plus, minus, opposite = along_x(both, -1), along_x(both, 1), along_x(both, 2)
    moved = swap(give)
    left = order_left(order, left_basis)
    left = [*left, *order_left(order, left_other, left)]

    mine = [(both, 0, 128), (moved, 0, 128)]
    cross = project_side(mine, left, 2)
    up0 = project_side(mine, left, 1, after=(cross,))
    down0 = project_side(mine, left, 3, after=(up0, plus, minus))
    came0 = [first(cross, 2), first(up0, 1), first(down0, -1)]
    others = swap(gather((plus, minus, opposite), (down0,)))
    rest = [
        (plus, 0, 128), (others, 0, 128), (minus, 0, 128), (others, 128, 128), (opposite, 0, 128), (others, 256, 128),
    ]

    def spread(q):
        return [q[0], second_axis(q[1], 1), second_axis(q[3], -1), second_axis(q[2], 2)]

    parts0 = spread(project_own(mine, left, came0, (down0,), LONG))
    cross = project_side(rest, left, 2, after=(parts0[0],))
    up1 = project_side(rest, left, 1, after=(cross,))
    down1 = project_side(rest, left, 3, after=(up1,))
    sum0 = add(parts0, (down1,))
    came1 = [first(cross, 2), first(up1, 1), first(down1, -1)]
    parts1 = spread(project_own(rest, left, came1, (sum0,)))
    part = rotate([[sum0], parts1], order_r, right_basis, (0, 1, 3, 2))
    own, other = part
    other = swap(other)

    second_new, keep, give = turn(core, order_r, own, other, second, right_basis)
    share = jnp.stack([keep, swap(give)], axis=0)
    shares = [share, second_axis(share, -1), second_axis(share, -2), second_axis(share, 1)]

    block_a = lay(shares, 0)
    plus_a, minus_a = first(block_a, -1), first(block_a, 1)
    sums_a = back_project([(0, [block_a])], left)
    far_a1, far_a3 = forward(plus_a, minus_a, (0, 512), (512, 1032), (sums_a,))
    block_b = lay(shares, 1, (far_a1,))
    far_a1, far_a3 = first(far_a1, -1), first(far_a3, 1)
    plus_b, minus_b = first(block_b, -1), first(block_b, 1)
    sums_a = back_project([(1, [plus_a]), (3, [minus_a])], left, sums_a, after=(block_b,))
    u1, u3 = back_project([(2, [far_a1, far_a3])], left, sums_a, cut=True)
    sums_b = back_project([(0, [block_b])], left, after=(u1,), cost=LONG)
    far_b1, far_b3 = forward(plus_b, minus_b, (0, 512), (512, 1032), (sums_b,))
    sums_b = back_project([(1, [plus_b]), (3, [minus_b])], left, sums_b, after=(far_b1,))
    far_b1, far_b3 = first(far_b1, -1), first(far_b3, 1)
    got1, got3 = along_x(u1, 1), along_x(u3, -1)
    u2, u0 = back_project([(2, [far_b1, far_b3])], left, sums_b, cut=True, after=(got1, got3))
    update = finish([u0, got1, got3, along_x(u2, 2)])
    return (update, moment_new, second_new)


def solution(mesh):
    return jax.shard_map(
        local,
        mesh=mesh,
        in_specs=(P("col", "row"), P("col", "row"), P(("row", "col"), None), P("col", "row"), P()),
        out_specs=(P("col", "row"), P("col", "row"), P(("row", "col"), None)),
        check_vma=False,
    )
```

```python
import functools
import math

import jax
import jax.numpy as jnp
import numpy as np
from jax import lax
from jax.experimental import pallas as pl
from jax.experimental.pallas import tpu as pltpu
from jax.sharding import PartitionSpec as P

M = 16384
N = 1024

first_decay = 0.9
second_decay = 0.95
epsilon = 1e-08
clip_share = 0.25

f32, bf16 = jnp.float32, jnp.bfloat16
BOTH = ("row", "col")
VMEM_LIMIT = 10 * 1024 * 1024
CHIPS = (1, 3, 2, 0)
LONG = 10**11
WHOLE = pl.BlockSpec(memory_space=pltpu.VMEM)
SCALARS = pl.BlockSpec(memory_space=pltpu.SMEM)
ANYWHERE = pl.BlockSpec(memory_space=pl.ANY)


def call(kernel, name, args, out_shape, specs=None, scratch=(), after=(), hold=(), cost=1):
    n, k = len(args), len(after) + len(hold)

    def body(*refs):
        kernel(*refs[:n], *refs[n + k :])

    return pl.pallas_call(
        body,
        in_specs=(specs or [WHOLE] * n) + [ANYWHERE] * len(after) + [WHOLE] * len(hold),
        out_specs=[WHOLE] * len(out_shape),
        out_shape=out_shape,
        scratch_shapes=list(scratch),
        compiler_params=pltpu.CompilerParams(vmem_limit_bytes=VMEM_LIMIT),
        cost_estimate=pl.CostEstimate(flops=cost, bytes_accessed=cost, transcendentals=0),
        name=name,
    )(*args, *after, *hold)


def shape(rows, columns, dtype=f32):
    return jax.ShapeDtypeStruct((rows, columns), dtype)


def split(value):
    high = value.astype(bf16)
    return high, (value - high.astype(f32)).astype(bf16)


def dot3(a_high, a_low, b_high, b_low, dims=(((1,), (0,)), ((), ()))):
    d = functools.partial(lax.dot_general, dimension_numbers=dims, preferred_element_type=f32)
    return d(a_high, b_high) + (d(a_high, b_low) + d(a_low, b_high))


def move(value, step):
    pairs = []
    for x in range(4):
        for c in range(2):
            for y in range(4):
                for z in range(4):
                    tx, tc, ty, tz = step(x, c, y, z)
                    pairs.append(((2 * x + c) * 16 + 4 * y + z, (2 * (tx % 4) + tc) * 16 + 4 * (ty % 4) + tz % 4))
    return lax.ppermute(value, BOTH, pairs)


def swap(value):
    return move(value, lambda x, c, y, z: (x, 1 - c, y, z))


def along_x(value, d):
    return move(value, lambda x, c, y, z: (x + d, c, y, z))


def first(value, d):
    return move(value, lambda x, c, y, z: (x, c, y + d, z) if c == 0 else (x, c, y, z + d))


def second_axis(value, d):
    return move(value, lambda x, c, y, z: (x, c, y, z + d) if c == 0 else (x, c, y + d, z))


def start(core, grad, moment):
    def kernel(core_ref, grad_ref, moment_ref, new_ref, both_ref, give_ref):
        g = grad_ref[...]
        new = first_decay * moment_ref[...] + (1.0 - first_decay) * g
        new_ref[...] = new
        g, new = g.T, new.T
        zero = core_ref[0] == 0
        both_ref[0:128, :] = jnp.where(zero, g, new)
        give = jnp.where(zero, new, g)
        both_ref[128:256, :] = give
        give_ref[...] = give

    return call(
        kernel, "start", [core, grad, moment], [shape(1024, 128), shape(256, 1024), shape(128, 1024)], [SCALARS, WHOLE, WHOLE]
    )


def order_left(order, left, hold=(), after=()):
    steps, slots = 8, 2

    def kernel(order_ref, left_ref, high_ref, low_ref, held, arrived):
        def copy(i):
            return pltpu.make_async_copy(left_ref.at[pl.ds(i * 128, 128), :], held.at[i % slots], arrived.at[i % slots])

        for i in range(slots):
            copy(i).start()
        for i in range(steps):
            copy(i).wait()
            rows = slice(i * 128, i * 128 + 128)
            for a in range(4):
                for b in range(4):
                    at = pl.multiple_of(order_ref[a * 4 + b] * 128, 128)
                    high, low = split(held[i % slots, :, pl.ds(at, 128)])
                    high_ref[a, rows, b * 128 : b * 128 + 128] = high
                    low_ref[a, rows, b * 128 : b * 128 + 128] = low
            if i + slots < steps:
                copy(i + slots).start()

    return call(
        kernel, "order_left", [order, left], [jax.ShapeDtypeStruct((4, 1024, 512), bf16)] * 2, [SCALARS, pl.BlockSpec(memory_space=pltpu.HBM)],
        [pltpu.VMEM((slots, 128, 2048), f32), pltpu.SemaphoreType.DMA((slots,))], after, hold,
    )


def order_right(order, right, after=()):
    def kernel(order_ref, right_ref, high_ref, low_ref):
        for i in range(8):
            at = pl.multiple_of(order_ref[i] * 128, 128)
            rows = slice(i * 128, i * 128 + 128)
            high_ref[rows, :], low_ref[rows, :] = split(right_ref[pl.ds(at, 128), :])

    return call(kernel, "order_right", [order, right], [shape(1024, 1024, bf16)] * 2, [SCALARS, WHOLE], after=after)


def fill(refs, blocks, high, low):
    at = 0
    for ref, (_, begin, size) in zip(refs, blocks):
        high[at : at + size, :], low[at : at + size, :] = split(ref[begin : begin + size, :])
        at += size


def project_far(blocks, left, after=()):
    rows = sum(size for _, _, size in blocks)
    n = len(blocks)

    def kernel(*refs):
        l_refs, outs, (gh, gl) = refs[n : n + 4], refs[n + 4 : n + 6], refs[n + 6 :]
        fill(refs[:n], blocks, gh, gl)
        for h in range(2):
            for t in range(2):
                c = slice(t * 256, t * 256 + 256)
                outs[h][:, c] = dot3(gh[...], gl[...], l_refs[2 * h][2, :, c], l_refs[2 * h + 1][2, :, c])

    return call(
        kernel, "project_far", [*[b[0] for b in blocks], *left], [shape(rows, 512)] * 2, None, [pltpu.VMEM((rows, 1024), bf16)] * 2, after
    )


def project_near(blocks, left, near, far, begin, after=(), cost=1):
    rows = sum(size for _, _, size in blocks)
    n = len(blocks)

    def kernel(*refs):
        l_refs, more, outs, (gh, gl) = refs[n : n + 4], refs[n + 4 : n + 6], refs[n + 6 : n + 8], refs[n + 8 :]
        fill(refs[:n], blocks, gh, gl)
        for i, d in enumerate((1, 3)):
            for h in range(2):
                for t in range(2):
                    c = slice(t * 256, t * 256 + 256)
                    value = dot3(gh[...], gl[...], l_refs[2 * h][d, :, c], l_refs[2 * h + 1][d, :, c])
                    if h == i:
                        value = value + more[i][begin : begin + rows, c]
                    outs[i][:, h * 512 + t * 256 : h * 512 + t * 256 + 256] = value

    return call(
        kernel, "project_near", [*[b[0] for b in blocks], *left, near, far], [shape(rows, 1024)] * 2, None,
        [pltpu.VMEM((rows, 1024), bf16)] * 2, after, cost=cost,
    )


def project_own(blocks, left, up, down, after=(), cost=1):
    rows = sum(size for _, _, size in blocks)
    n = len(blocks)

    def kernel(*refs):
        l_refs, (up_ref, down_ref), outs, (gh, gl) = refs[n : n + 4], refs[n + 4 : n + 6], refs[n + 6 : n + 10], refs[n + 10 :]
        fill(refs[:n], blocks, gh, gl)
        for d in range(4):
            c = slice(d * 128, d * 128 + 128)
            high = jnp.concatenate([l_refs[0][0, :, c], l_refs[2][0, :, c]], axis=1)
            low = jnp.concatenate([l_refs[1][0, :, c], l_refs[3][0, :, c]], axis=1)
            value = dot3(gh[...], gl[...], high, low)
            for h in range(2):
                e = slice(h * 512 + d * 128, h * 512 + d * 128 + 128)
                outs[d][:, h * 128 : h * 128 + 128] = value[:, h * 128 : h * 128 + 128] + up_ref[:, e] + down_ref[:, e]

    return call(
        kernel, "project_own", [*[b[0] for b in blocks], *left, up, down], [shape(rows, 256)] * 4, None, [pltpu.VMEM((rows, 1024), bf16)] * 2,
        after, cost=cost,
    )


def rotate(parts, right, chips, before=None, last=False):
    n = 6 + (before is not None)

    def kernel(*refs):
        p, (rh, rl) = refs[:4], refs[4:6]
        total = (p[0][...] + p[1][...]) + (p[2][...] + p[3][...])
        high, low = split(total.T)
        places = [h * 512 + CHIPS.index(d) * 128 for d in chips for h in range(2)]
        for t in range(4):
            c = slice(t * 256, t * 256 + 256)
            r_high = jnp.concatenate([rh[p : p + 128, c] for p in places], axis=0)
            r_low = jnp.concatenate([rl[p : p + 128, c] for p in places], axis=0)
            value = dot3(high, low, r_high, r_low)
            if before is not None:
                value = value + refs[6][:, c]
            if last:
                refs[n][:, c] = value[:128]
                refs[n + 1][:, c] = value[128:]
            else:
                refs[n][:, c] = value

    out = call(
        kernel, "rotate", [*parts, *right] + ([before] if n > 6 else []), [shape(128, 1024)] * 2 if last else [shape(256, 1024)]
    )
    return out if last else out[0]


def turn(core, own, other, second, right):
    def kernel(core_ref, own_ref, other_ref, second_ref, rh, rl, new_ref, keep_ref, give_ref):
        zero = core_ref[0] == 0
        a, b = own_ref[...], other_ref[...]
        g, m = jnp.where(zero, a, b), jnp.where(zero, b, a)
        new = second_decay * second_ref[...] + (1.0 - second_decay) * g * g
        new_ref[...] = new
        rotated = m / (jnp.sqrt(new) + epsilon)
        high, low = split(rotated)
        squares = rotated * rotated
        total = squares[0:8, :]
        for i in range(1, 16):
            total = total + squares[i * 8 : i * 8 + 8, :]
        narrow = total[:, 0:128]
        for i in range(1, 8):
            narrow = narrow + total[:, i * 128 : i * 128 + 128]
        zeros = jnp.zeros((8, 128), f32)
        for out, h in ((give_ref, 1), (keep_ref, 0)):
            for t in range(2):
                r = slice(h * 512 + t * 256, h * 512 + t * 256 + 256)
                out[0:128, t * 256 : t * 256 + 256] = dot3(high, low, rh[r, :], rl[r, :], (((1,), (1,)), ((), ())))
            out[128:136, :] = jnp.concatenate([narrow, zeros, narrow, zeros], axis=1)

    return call(
        kernel, "turn", [core, own, other, second, *right], [shape(128, 1024), shape(136, 512), shape(136, 512)],
        [SCALARS] + [WHOLE] * 5,
    )


def back_project(terms, left, before=None, cut=False, after=(), cost=1):
    arrays = [a for _, group in terms for a in group]
    n = len(arrays)

    def kernel(*refs):
        l_refs = refs[n : n + 4]
        sh, sl = refs[-2:]
        outs = refs[n + 4 + (before is not None) : -2]
        at, index = 0, 0
        extra = refs[n + 4][1024:1032, :] if before is not None else jnp.zeros((8, 256), f32)
        for _, group in terms:
            size = 1024 // len(group)
            for _ in group:
                sh[at : at + size, :], sl[at : at + size, :] = split(refs[index][0:size, :])
                if refs[index].shape[0] > size:
                    extra = extra + refs[index][size : size + 8, :]
                at, index = at + size, index + 1
        for t in range(4):
            r = slice(t * 256, t * 256 + 256)
            value = refs[n + 4][r, :] if before is not None else None
            for i, (d, _) in enumerate(terms):
                for h in range(2):
                    rows = slice(i * 1024 + h * 512, i * 1024 + h * 512 + 512)
                    new = dot3(l_refs[2 * h][d, r, :], l_refs[2 * h + 1][d, r, :], sh[rows, :], sl[rows, :])
                    value = new if value is None else value + new
            if cut:
                outs[0][r, :] = value[:, :128]
                outs[1][r, :] = value[:, 128:]
            else:
                outs[0][r, :] = value
        if cut:
            outs[0][1024:1032, :] = extra[:, :128]
            outs[1][1024:1032, :] = extra[:, :128]
        else:
            outs[0][1024:1032, :] = extra

    out = call(
        kernel, "back_project", [*arrays, *left] + ([] if before is None else [before]),
        [shape(1032, 128)] * 2 if cut else [shape(1032, 256)], None, [pltpu.VMEM((1024 * len(terms), 256), bf16)] * 2, after,
        cost=cost,
    )
    return out if cut else out[0]


def finish(parts):
    def kernel(a, b, c, d, out):
        rows = slice(1024, 1032)
        squares = (a[rows, :] + b[rows, :]) + (c[rows, :] + d[rows, :])
        total = jnp.sum(jnp.sum(squares, axis=0, keepdims=True), axis=1, keepdims=True)
        factor = jnp.minimum(1.0, clip_share * math.sqrt(M * N) / (jnp.sqrt(total) + 1e-06))
        rows = slice(0, 1024)
        out[...] = ((a[rows, :] + b[rows, :]) + (c[rows, :] + d[rows, :])) * factor

    return call(kernel, "finish", list(parts), [shape(1024, 128)])[0]


def lay(shares, half, after=()):
    def kernel(*refs):
        out = refs[-1]
        c = slice(half * 256, half * 256 + 256)
        extra = jnp.zeros((8, 256), f32)
        for d in range(4):
            for h in range(2):
                out[(h * 4 + d) * 128 : (h * 4 + d) * 128 + 128, :] = refs[d][h, 0:128, c]
                extra = extra + refs[d][h, 128:136, c]
        out[1024:1032, :] = extra

    return call(kernel, "lay", list(shares), [shape(1032, 256)], after=after)[0]


def forward(plus, minus, rows, others, after):
    def kernel(plus_ref, minus_ref, one, two):
        one[...] = plus_ref[rows[0] : rows[1], :]
        two[...] = minus_ref[others[0] : others[1], :]

    columns = plus.shape[1]
    outs = [shape(rows[1] - rows[0], columns), shape(others[1] - others[0], columns)]
    return call(kernel, "forward", [plus, minus], outs, after=after)


def tables():
    left = np.zeros((2, 16, 16), np.int32)
    right = np.zeros((8, 8), np.int32)
    for c in range(2):
        for y in range(4):
            for z in range(4):
                for a in range(4):
                    for b in range(4):
                        p, q = (y + a, z + b) if c == 0 else (y + b, z + a)
                        left[c, y * 4 + z, a * 4 + b] = p % 4 * 4 + q % 4
        for x in range(4):
            for h in range(2):
                for i, d in enumerate(CHIPS):
                    right[2 * x + c, h * 4 + i] = 2 * ((x + d) % 4) + (c + h) % 2
    return left, right


def local(grad, moment, second, left_basis, right_basis):
    row, col = lax.axis_index("row"), lax.axis_index("col")
    core = (row % 2).reshape(1).astype(jnp.int32)
    by_col, by_row = tables()
    order = jnp.asarray(by_col)[row % 2, col]
    order_r = jnp.asarray(by_row)[row]

    left_other = swap(left_basis)
    moment_new, both, give = start(core, grad, moment)
    plus, minus = along_x(both, -1), along_x(both, 1)
    moved = swap(give)
    right = order_right(order_r, right_basis, (both,))
    left = order_left(order, left_basis, (), right)
    left = [*left, *order_left(order, left_other, left)]

    one, two = project_far([(both, 0, 128), (moved, 0, 128)], left)
    far_keep, far_give = forward(plus, minus, (0, 128), (128, 256), (one,))
    far_keep, far_give = along_x(far_keep, -1), along_x(far_give, 1)
    plus_other, minus_other = swap(plus), swap(minus)
    far_moved = swap(far_give)

    chips = [(0,), (1, 3), (2,)]
    blocks = [
        [(both, 0, 128), (moved, 0, 128)],
        [(plus, 0, 128), (plus_other, 128, 128), (minus, 0, 128), (minus_other, 128, 128)],
        [(far_keep, 0, 128), (far_moved, 0, 128)],
    ]

    def own_step(i, near, after, cost=1):
        q = project_own(blocks[i], left, *near, after, cost)
        return [q[0], second_axis(q[1], 1), second_axis(q[3], -1), second_axis(q[2], 2)]

    one, two = first(one, 1), first(two, -1)
    up, down = project_near(blocks[0], left, one, two, 0, (), LONG)
    near = first(up, 1), first(down, -1)
    one, two = project_far(blocks[1] + blocks[2], left, (up,))
    more = first(one, 1), first(two, -1)
    parts = own_step(0, near, (one,), LONG)
    part = rotate(parts, right, chips[0])
    up1, down1 = project_near(blocks[1], left, *more, 0, (parts[0],))
    up2, down2 = project_near(blocks[2], left, *more, 512, (up1, part))
    near1 = first(up1, 1), first(down1, -1)
    near2 = first(up2, 1), first(down2, -1)
    parts1 = own_step(1, near1, (up2,))
    parts2 = own_step(2, near2, (parts1[0],))
    part = rotate(parts1, right, chips[1], part)
    part = rotate(parts2, right, chips[2], part, last=True)
    own, other = part
    other = swap(other)

    second_new, keep, give = turn(core, own, other, second, right)
    share = jnp.stack([keep, swap(give)], axis=0)
    shares = [share, second_axis(share, -1), second_axis(share, -2), second_axis(share, 1)]

    block_a = lay(shares, 0)
    plus_a, minus_a = first(block_a, -1), first(block_a, 1)
    sums_a = back_project([(0, [block_a])], left)
    far_a1, far_a3 = forward(plus_a, minus_a, (0, 512), (512, 1032), (sums_a,))
    block_b = lay(shares, 1, (far_a1,))
    far_a1, far_a3 = first(far_a1, -1), first(far_a3, 1)
    plus_b, minus_b = first(block_b, -1), first(block_b, 1)
    sums_a = back_project([(1, [plus_a]), (3, [minus_a])], left, sums_a, after=(block_b,))
    u1, u3 = back_project([(2, [far_a1, far_a3])], left, sums_a, cut=True)
    sums_b = back_project([(0, [block_b])], left, after=(u1,), cost=LONG)
    far_b1, far_b3 = forward(plus_b, minus_b, (0, 512), (512, 1032), (sums_b,))
    sums_b = back_project([(1, [plus_b]), (3, [minus_b])], left, sums_b, after=(far_b1,))
    far_b1, far_b3 = first(far_b1, -1), first(far_b3, 1)
    got1, got3 = along_x(u1, 1), along_x(u3, -1)
    u2, u0 = back_project([(2, [far_b1, far_b3])], left, sums_b, cut=True, after=(got1, got3))
    update = finish([u0, got1, got3, along_x(u2, 2)])
    return (update, moment_new, second_new)


def solution(mesh):
    return jax.shard_map(
        local,
        mesh=mesh,
        in_specs=(P("col", "row"), P("col", "row"), P(("row", "col"), None), P("col", "row"), P()),
        out_specs=(P("col", "row"), P("col", "row"), P(("row", "col"), None)),
        check_vma=False,
    )
```

```python
import functools
import math

import jax
import jax.numpy as jnp
import numpy as np
from jax import lax
from jax.experimental import pallas as pl
from jax.experimental.pallas import tpu as pltpu
from jax.sharding import PartitionSpec as P

M = 16384
N = 1024

first_decay = 0.9
second_decay = 0.95
epsilon = 1e-08
clip_share = 0.25

f32, bf16 = jnp.float32, jnp.bfloat16
BOTH = ("row", "col")
VMEM_LIMIT = 10 * 1024 * 1024
CHIPS = (1, 3, 2, 0)
LONG = 10**11
WHOLE = pl.BlockSpec(memory_space=pltpu.VMEM)
SCALARS = pl.BlockSpec(memory_space=pltpu.SMEM)
ANYWHERE = pl.BlockSpec(memory_space=pl.ANY)


def call(kernel, name, args, out_shape, specs=None, scratch=(), after=(), hold=(), cost=1):
    n, k = len(args), len(after) + len(hold)

    def body(*refs):
        kernel(*refs[:n], *refs[n + k :])

    return pl.pallas_call(
        body,
        in_specs=(specs or [WHOLE] * n) + [ANYWHERE] * len(after) + [WHOLE] * len(hold),
        out_specs=[WHOLE] * len(out_shape),
        out_shape=out_shape,
        scratch_shapes=list(scratch),
        compiler_params=pltpu.CompilerParams(vmem_limit_bytes=VMEM_LIMIT),
        cost_estimate=pl.CostEstimate(flops=cost, bytes_accessed=cost, transcendentals=0),
        name=name,
    )(*args, *after, *hold)


def shape(rows, columns, dtype=f32):
    return jax.ShapeDtypeStruct((rows, columns), dtype)


def split(value):
    high = value.astype(bf16)
    return high, (value - high.astype(f32)).astype(bf16)


def dot3(a_high, a_low, b_high, b_low, dims=(((1,), (0,)), ((), ()))):
    d = functools.partial(lax.dot_general, dimension_numbers=dims, preferred_element_type=f32)
    return d(a_high, b_high) + (d(a_high, b_low) + d(a_low, b_high))


def move(value, step):
    pairs = []
    for x in range(4):
        for c in range(2):
            for y in range(4):
                for z in range(4):
                    tx, tc, ty, tz = step(x, c, y, z)
                    pairs.append(((2 * x + c) * 16 + 4 * y + z, (2 * (tx % 4) + tc) * 16 + 4 * (ty % 4) + tz % 4))
    return lax.ppermute(value, BOTH, pairs)


def swap(value):
    return move(value, lambda x, c, y, z: (x, 1 - c, y, z))


def along_x(value, d):
    return move(value, lambda x, c, y, z: (x + d, c, y, z))


def first(value, d):
    return move(value, lambda x, c, y, z: (x, c, y + d, z) if c == 0 else (x, c, y, z + d))


def second_axis(value, d):
    return move(value, lambda x, c, y, z: (x, c, y, z + d) if c == 0 else (x, c, y + d, z))


def start(core, grad, moment):
    def kernel(core_ref, grad_ref, moment_ref, new_ref, both_ref, give_ref):
        g = grad_ref[...]
        new = first_decay * moment_ref[...] + (1.0 - first_decay) * g
        new_ref[...] = new
        g, new = g.T, new.T
        zero = core_ref[0] == 0
        both_ref[0:128, :] = jnp.where(zero, g, new)
        give = jnp.where(zero, new, g)
        both_ref[128:256, :] = give
        give_ref[...] = give

    return call(
        kernel, "start", [core, grad, moment], [shape(1024, 128), shape(256, 1024), shape(128, 1024)], [SCALARS, WHOLE, WHOLE]
    )


def order_left(order, left, hold=(), after=()):
    steps, slots = 8, 2

    def kernel(order_ref, left_ref, high_ref, low_ref, held, arrived):
        def copy(i):
            return pltpu.make_async_copy(left_ref.at[pl.ds(i * 128, 128), :], held.at[i % slots], arrived.at[i % slots])

        for i in range(slots):
            copy(i).start()
        for i in range(steps):
            copy(i).wait()
            rows = slice(i * 128, i * 128 + 128)
            for a in range(4):
                for b in range(4):
                    at = pl.multiple_of(order_ref[a * 4 + b] * 128, 128)
                    high, low = split(held[i % slots, :, pl.ds(at, 128)])
                    high_ref[a, rows, b * 128 : b * 128 + 128] = high
                    low_ref[a, rows, b * 128 : b * 128 + 128] = low
            if i + slots < steps:
                copy(i + slots).start()

    return call(
        kernel, "order_left", [order, left], [jax.ShapeDtypeStruct((4, 1024, 512), bf16)] * 2, [SCALARS, pl.BlockSpec(memory_space=pltpu.HBM)],
        [pltpu.VMEM((slots, 128, 2048), f32), pltpu.SemaphoreType.DMA((slots,))], after, hold,
    )


def order_right(order, right, after=()):
    def kernel(order_ref, right_ref, high_ref, low_ref):
        for i in range(8):
            at = pl.multiple_of(order_ref[i] * 128, 128)
            rows = slice(i * 128, i * 128 + 128)
            high_ref[rows, :], low_ref[rows, :] = split(right_ref[pl.ds(at, 128), :])

    return call(kernel, "order_right", [order, right], [shape(1024, 1024, bf16)] * 2, [SCALARS, WHOLE], after=after)


def fill(refs, blocks, high, low):
    at = 0
    for ref, (_, begin, size) in zip(refs, blocks):
        high[at : at + size, :], low[at : at + size, :] = split(ref[begin : begin + size, :])
        at += size


def project_far(blocks, left, after=()):
    rows = sum(size for _, _, size in blocks)
    n = len(blocks)

    def kernel(*refs):
        l_refs, outs, (gh, gl) = refs[n : n + 4], refs[n + 4 : n + 6], refs[n + 6 :]
        fill(refs[:n], blocks, gh, gl)
        for h in range(2):
            for t in range(2):
                c = slice(t * 256, t * 256 + 256)
                outs[h][:, c] = dot3(gh[...], gl[...], l_refs[2 * h][2, :, c], l_refs[2 * h + 1][2, :, c])

    return call(
        kernel, "project_far", [*[b[0] for b in blocks], *left], [shape(rows, 512)] * 2, None, [pltpu.VMEM((rows, 1024), bf16)] * 2, after
    )


def project_near(blocks, left, near, far, begin, after=(), cost=1):
    rows = sum(size for _, _, size in blocks)
    n = len(blocks)

    def kernel(*refs):
        l_refs, more, outs, (gh, gl) = refs[n : n + 4], refs[n + 4 : n + 6], refs[n + 6 : n + 8], refs[n + 8 :]
        fill(refs[:n], blocks, gh, gl)
        for i, d in enumerate((1, 3)):
            for h in range(2):
                for t in range(2):
                    c = slice(t * 256, t * 256 + 256)
                    value = dot3(gh[...], gl[...], l_refs[2 * h][d, :, c], l_refs[2 * h + 1][d, :, c])
                    if h == i:
                        value = value + more[i][begin : begin + rows, c]
                    outs[i][:, h * 512 + t * 256 : h * 512 + t * 256 + 256] = value

    return call(
        kernel, "project_near", [*[b[0] for b in blocks], *left, near, far], [shape(rows, 1024)] * 2, None,
        [pltpu.VMEM((rows, 1024), bf16)] * 2, after, cost=cost,
    )


def project_own(blocks, left, up, down, after=(), cost=1):
    rows = sum(size for _, _, size in blocks)
    n = len(blocks)

    def kernel(*refs):
        l_refs, (up_ref, down_ref), outs, (gh, gl) = refs[n : n + 4], refs[n + 4 : n + 6], refs[n + 6 : n + 10], refs[n + 10 :]
        fill(refs[:n], blocks, gh, gl)
        for d in range(4):
            c = slice(d * 128, d * 128 + 128)
            high = jnp.concatenate([l_refs[0][0, :, c], l_refs[2][0, :, c]], axis=1)
            low = jnp.concatenate([l_refs[1][0, :, c], l_refs[3][0, :, c]], axis=1)
            value = dot3(gh[...], gl[...], high, low)
            for h in range(2):
                e = slice(h * 512 + d * 128, h * 512 + d * 128 + 128)
                outs[d][:, h * 128 : h * 128 + 128] = value[:, h * 128 : h * 128 + 128] + up_ref[:, e] + down_ref[:, e]

    return call(
        kernel, "project_own", [*[b[0] for b in blocks], *left, up, down], [shape(rows, 256)] * 4, None, [pltpu.VMEM((rows, 1024), bf16)] * 2,
        after, cost=cost,
    )


def rotate(parts, right, chips, before=None, last=False, after=()):
    n = 6 + (before is not None)

    def kernel(*refs):
        p, (rh, rl) = refs[:4], refs[4:6]
        total = (p[0][...] + p[1][...]) + (p[2][...] + p[3][...])
        high, low = split(total.T)
        places = [h * 512 + CHIPS.index(d) * 128 for d in chips for h in range(2)]
        for t in range(4):
            c = slice(t * 256, t * 256 + 256)
            r_high = jnp.concatenate([rh[p : p + 128, c] for p in places], axis=0)
            r_low = jnp.concatenate([rl[p : p + 128, c] for p in places], axis=0)
            value = dot3(high, low, r_high, r_low)
            if before is not None:
                value = value + refs[6][:, c]
            if last:
                refs[n][:, c] = value[:128]
                refs[n + 1][:, c] = value[128:]
            else:
                refs[n][:, c] = value

    out = call(
        kernel, "rotate", [*parts, *right] + ([before] if n > 6 else []), [shape(128, 1024)] * 2 if last else [shape(256, 1024)],
        after=after,
    )
    return out if last else out[0]


def turn(core, own, other, second, right):
    def kernel(core_ref, own_ref, other_ref, second_ref, rh, rl, new_ref, keep_ref, give_ref):
        zero = core_ref[0] == 0
        a, b = own_ref[...], other_ref[...]
        g, m = jnp.where(zero, a, b), jnp.where(zero, b, a)
        new = second_decay * second_ref[...] + (1.0 - second_decay) * g * g
        new_ref[...] = new
        rotated = m / (jnp.sqrt(new) + epsilon)
        high, low = split(rotated)
        squares = rotated * rotated
        total = squares[0:8, :]
        for i in range(1, 16):
            total = total + squares[i * 8 : i * 8 + 8, :]
        narrow = total[:, 0:128]
        for i in range(1, 8):
            narrow = narrow + total[:, i * 128 : i * 128 + 128]
        zeros = jnp.zeros((8, 128), f32)
        for out, h in ((give_ref, 1), (keep_ref, 0)):
            for t in range(2):
                r = slice(h * 512 + t * 256, h * 512 + t * 256 + 256)
                out[0:128, t * 256 : t * 256 + 256] = dot3(high, low, rh[r, :], rl[r, :], (((1,), (1,)), ((), ())))
            out[128:136, :] = jnp.concatenate([narrow, zeros, narrow, zeros], axis=1)

    return call(
        kernel, "turn", [core, own, other, second, *right], [shape(128, 1024), shape(136, 512), shape(136, 512)],
        [SCALARS] + [WHOLE] * 5,
    )


def back_project(terms, left, before=None, cut=False, after=(), cost=1):
    arrays = [a for _, group in terms for a in group]
    n = len(arrays)

    def kernel(*refs):
        l_refs = refs[n : n + 4]
        sh, sl = refs[-2:]
        outs = refs[n + 4 + (before is not None) : -2]
        at, index = 0, 0
        extra = refs[n + 4][1024:1032, :] if before is not None else jnp.zeros((8, 256), f32)
        for _, group in terms:
            size = 1024 // len(group)
            for _ in group:
                sh[at : at + size, :], sl[at : at + size, :] = split(refs[index][0:size, :])
                if refs[index].shape[0] > size:
                    extra = extra + refs[index][size : size + 8, :]
                at, index = at + size, index + 1
        for t in range(4):
            r = slice(t * 256, t * 256 + 256)
            value = refs[n + 4][r, :] if before is not None else None
            for i, (d, _) in enumerate(terms):
                for h in range(2):
                    rows = slice(i * 1024 + h * 512, i * 1024 + h * 512 + 512)
                    new = dot3(l_refs[2 * h][d, r, :], l_refs[2 * h + 1][d, r, :], sh[rows, :], sl[rows, :])
                    value = new if value is None else value + new
            if cut:
                outs[0][r, :] = value[:, :128]
                outs[1][r, :] = value[:, 128:]
            else:
                outs[0][r, :] = value
        if cut:
            outs[0][1024:1032, :] = extra[:, :128]
            outs[1][1024:1032, :] = extra[:, :128]
        else:
            outs[0][1024:1032, :] = extra

    out = call(
        kernel, "back_project", [*arrays, *left] + ([] if before is None else [before]),
        [shape(1032, 128)] * 2 if cut else [shape(1032, 256)], None, [pltpu.VMEM((1024 * len(terms), 256), bf16)] * 2, after,
        cost=cost,
    )
    return out if cut else out[0]


def finish(parts):
    def kernel(a, b, c, d, out):
        rows = slice(1024, 1032)
        squares = (a[rows, :] + b[rows, :]) + (c[rows, :] + d[rows, :])
        total = jnp.sum(jnp.sum(squares, axis=0, keepdims=True), axis=1, keepdims=True)
        factor = jnp.minimum(1.0, clip_share * math.sqrt(M * N) / (jnp.sqrt(total) + 1e-06))
        rows = slice(0, 1024)
        out[...] = ((a[rows, :] + b[rows, :]) + (c[rows, :] + d[rows, :])) * factor

    return call(kernel, "finish", list(parts), [shape(1024, 128)])[0]


def lay(shares, half, after=()):
    def kernel(*refs):
        out = refs[-1]
        c = slice(half * 256, half * 256 + 256)
        extra = jnp.zeros((8, 256), f32)
        for d in range(4):
            for h in range(2):
                out[(h * 4 + d) * 128 : (h * 4 + d) * 128 + 128, :] = refs[d][h, 0:128, c]
                extra = extra + refs[d][h, 128:136, c]
        out[1024:1032, :] = extra

    return call(kernel, "lay", list(shares), [shape(1032, 256)], after=after)[0]


def forward(plus, minus, rows, others, after):
    def kernel(plus_ref, minus_ref, one, two):
        one[...] = plus_ref[rows[0] : rows[1], :]
        two[...] = minus_ref[others[0] : others[1], :]

    columns = plus.shape[1]
    outs = [shape(rows[1] - rows[0], columns), shape(others[1] - others[0], columns)]
    return call(kernel, "forward", [plus, minus], outs, after=after)


def sort(plus, minus, after):
    def kernel(plus_ref, minus_ref, keep, gives):
        keep[...] = plus_ref[0:128, :]
        gives[0:128, :] = plus_ref[128:256, :]
        gives[128:256, :] = minus_ref[128:256, :]

    return call(kernel, "sort", [plus, minus], [shape(128, 1024), shape(256, 1024)], after=after)


def tables():
    left = np.zeros((2, 16, 16), np.int32)
    right = np.zeros((8, 8), np.int32)
    for c in range(2):
        for y in range(4):
            for z in range(4):
                for a in range(4):
                    for b in range(4):
                        p, q = (y + a, z + b) if c == 0 else (y + b, z + a)
                        left[c, y * 4 + z, a * 4 + b] = p % 4 * 4 + q % 4
        for x in range(4):
            for h in range(2):
                for i, d in enumerate(CHIPS):
                    right[2 * x + c, h * 4 + i] = 2 * ((x + d) % 4) + (c + h) % 2
    return left, right


def local(grad, moment, second, left_basis, right_basis):
    row, col = lax.axis_index("row"), lax.axis_index("col")
    core = (row % 2).reshape(1).astype(jnp.int32)
    by_col, by_row = tables()
    order = jnp.asarray(by_col)[row % 2, col]
    order_r = jnp.asarray(by_row)[row]

    left_other = swap(left_basis)
    moment_new, both, give = start(core, grad, moment)
    plus, minus = along_x(both, -1), along_x(both, 1)
    moved = swap(give)
    right = order_right(order_r, right_basis, (both,))
    left = order_left(order, left_basis, (), right)
    left = [*left, *order_left(order, left_other, left)]

    one, two = project_far([(both, 0, 128), (moved, 0, 128)], left)
    keep, gives = sort(plus, minus, (one,))
    far_keep = along_x(keep, -1)
    others = swap(gives)
    far_moved = along_x(others[128:], 1)

    chips = [(0,), (1, 3), (2,)]
    blocks = [
        [(both, 0, 128), (moved, 0, 128)],
        [(plus, 0, 128), (others, 0, 128), (minus, 0, 128), (others, 128, 128)],
        [(far_keep, 0, 128), (far_moved, 0, 128)],
    ]

    def own_step(i, near, after, cost=1):
        q = project_own(blocks[i], left, *near, after, cost)
        return [q[0], second_axis(q[1], 1), second_axis(q[3], -1), second_axis(q[2], 2)]

    one, two = first(one, 1), first(two, -1)
    up, down = project_near(blocks[0], left, one, two, 0, (), LONG)
    near = first(up, 1), first(down, -1)
    one, two = project_far(blocks[1], left, (up,))
    more1 = first(one, 1), first(two, -1)
    parts = own_step(0, near, (one, far_keep, far_moved), LONG)
    one, two = project_far(blocks[2], left, (parts[0],))
    more2 = first(one, 1), first(two, -1)
    up1, down1 = project_near(blocks[1], left, *more1, 0, (one,))
    part = rotate(parts, right, chips[0], after=(up1,))
    up2, down2 = project_near(blocks[2], left, *more2, 0, (up1, part), LONG)
    near1 = first(up1, 1), first(down1, -1)
    near2 = first(up2, 1), first(down2, -1)
    parts1 = own_step(1, near1, (up2,))
    parts2 = own_step(2, near2, (parts1[0],))
    part = rotate(parts1, right, chips[1], part)
    part = rotate(parts2, right, chips[2], part, last=True)
    own, other = part
    other = swap(other)

    second_new, keep, give = turn(core, own, other, second, right)
    share = jnp.stack([keep, swap(give)], axis=0)
    shares = [share, second_axis(share, -1), second_axis(share, -2), second_axis(share, 1)]

    block_a = lay(shares, 0)
    plus_a, minus_a = first(block_a, -1), first(block_a, 1)
    sums_a = back_project([(0, [block_a])], left)
    far_a1, far_a3 = forward(plus_a, minus_a, (0, 512), (512, 1032), (sums_a,))
    block_b = lay(shares, 1, (far_a1,))
    far_a1, far_a3 = first(far_a1, -1), first(far_a3, 1)
    plus_b, minus_b = first(block_b, -1), first(block_b, 1)
    sums_a = back_project([(1, [plus_a]), (3, [minus_a])], left, sums_a, after=(block_b,))
    u1, u3 = back_project([(2, [far_a1, far_a3])], left, sums_a, cut=True)
    sums_b = back_project([(0, [block_b])], left, after=(u1,), cost=LONG)
    far_b1, far_b3 = forward(plus_b, minus_b, (0, 512), (512, 1032), (sums_b,))
    sums_b = back_project([(1, [plus_b]), (3, [minus_b])], left, sums_b, after=(far_b1,))
    far_b1, far_b3 = first(far_b1, -1), first(far_b3, 1)
    got1, got3 = along_x(u1, 1), along_x(u3, -1)
    u2, u0 = back_project([(2, [far_b1, far_b3])], left, sums_b, cut=True, after=(got1, got3))
    update = finish([u0, got1, got3, along_x(u2, 2)])
    return (update, moment_new, second_new)


def solution(mesh):
    return jax.shard_map(
        local,
        mesh=mesh,
        in_specs=(P("col", "row"), P("col", "row"), P(("row", "col"), None), P("col", "row"), P()),
        out_specs=(P("col", "row"), P("col", "row"), P(("row", "col"), None)),
        check_vma=False,
    )
```

```python
import functools
import math

import jax
import jax.numpy as jnp
import numpy as np
from jax import lax
from jax.experimental import pallas as pl
from jax.experimental.pallas import tpu as pltpu
from jax.sharding import PartitionSpec as P

M = 16384
N = 1024

first_decay = 0.9
second_decay = 0.95
epsilon = 1e-08
clip_share = 0.25

f32, bf16 = jnp.float32, jnp.bfloat16
BOTH = ("row", "col")
VMEM_LIMIT = 10 * 1024 * 1024
CHIPS = (1, 3, 2, 0)
LONG = 10**11
WHOLE = pl.BlockSpec(memory_space=pltpu.VMEM)
SCALARS = pl.BlockSpec(memory_space=pltpu.SMEM)
ANYWHERE = pl.BlockSpec(memory_space=pl.ANY)


def call(kernel, name, args, out_shape, specs=None, scratch=(), after=(), hold=(), cost=1):
    n, k = len(args), len(after) + len(hold)

    def body(*refs):
        kernel(*refs[:n], *refs[n + k :])

    return pl.pallas_call(
        body,
        in_specs=(specs or [WHOLE] * n) + [ANYWHERE] * len(after) + [WHOLE] * len(hold),
        out_specs=[WHOLE] * len(out_shape),
        out_shape=out_shape,
        scratch_shapes=list(scratch),
        compiler_params=pltpu.CompilerParams(vmem_limit_bytes=VMEM_LIMIT),
        cost_estimate=pl.CostEstimate(flops=cost, bytes_accessed=cost, transcendentals=0),
        name=name,
    )(*args, *after, *hold)


def shape(rows, columns, dtype=f32):
    return jax.ShapeDtypeStruct((rows, columns), dtype)


def split(value):
    high = value.astype(bf16)
    return high, (value - high.astype(f32)).astype(bf16)


def dot3(a_high, a_low, b_high, b_low, dims=(((1,), (0,)), ((), ()))):
    d = functools.partial(lax.dot_general, dimension_numbers=dims, preferred_element_type=f32)
    return d(a_high, b_high) + (d(a_high, b_low) + d(a_low, b_high))


def move(value, step):
    pairs = []
    for x in range(4):
        for c in range(2):
            for y in range(4):
                for z in range(4):
                    tx, tc, ty, tz = step(x, c, y, z)
                    pairs.append(((2 * x + c) * 16 + 4 * y + z, (2 * (tx % 4) + tc) * 16 + 4 * (ty % 4) + tz % 4))
    return lax.ppermute(value, BOTH, pairs)


def swap(value):
    return move(value, lambda x, c, y, z: (x, 1 - c, y, z))


def along_x(value, d):
    return move(value, lambda x, c, y, z: (x + d, c, y, z))


def first(value, d):
    return move(value, lambda x, c, y, z: (x, c, y + d, z) if c == 0 else (x, c, y, z + d))


def second_axis(value, d):
    return move(value, lambda x, c, y, z: (x, c, y, z + d) if c == 0 else (x, c, y + d, z))


def start(core, grad, moment):
    def kernel(core_ref, grad_ref, moment_ref, new_ref, both_ref, give_ref):
        g = grad_ref[...]
        new = first_decay * moment_ref[...] + (1.0 - first_decay) * g
        new_ref[...] = new
        g, new = g.T, new.T
        zero = core_ref[0] == 0
        both_ref[0:128, :] = jnp.where(zero, g, new)
        give = jnp.where(zero, new, g)
        both_ref[128:256, :] = give
        give_ref[...] = give

    return call(
        kernel, "start", [core, grad, moment], [shape(1024, 128), shape(256, 1024), shape(128, 1024)], [SCALARS, WHOLE, WHOLE]
    )


def order_left(order, left, hold=(), after=()):
    steps, slots = 8, 4

    def kernel(order_ref, left_ref, high_ref, low_ref, held, arrived):
        def copy(i):
            return pltpu.make_async_copy(left_ref.at[pl.ds(i * 128, 128), :], held.at[i % slots], arrived.at[i % slots])

        for i in range(slots):
            copy(i).start()
        for i in range(steps):
            copy(i).wait()
            rows = slice(i * 128, i * 128 + 128)
            for a in range(4):
                for b in range(4):
                    at = pl.multiple_of(order_ref[a * 4 + b] * 128, 128)
                    high, low = split(held[i % slots, :, pl.ds(at, 128)])
                    high_ref[a, rows, b * 128 : b * 128 + 128] = high
                    low_ref[a, rows, b * 128 : b * 128 + 128] = low
            if i + slots < steps:
                copy(i + slots).start()

    return call(
        kernel, "order_left", [order, left], [jax.ShapeDtypeStruct((4, 1024, 512), bf16)] * 2, [SCALARS, pl.BlockSpec(memory_space=pltpu.HBM)],
        [pltpu.VMEM((slots, 128, 2048), f32), pltpu.SemaphoreType.DMA((slots,))], after, hold,
    )


def order_right(order, right, after=()):
    def kernel(order_ref, right_ref, high_ref, low_ref, mark_ref):
        for i in range(8):
            at = pl.multiple_of(order_ref[i] * 128, 128)
            rows = slice(i * 128, i * 128 + 128)
            high_ref[rows, :], low_ref[rows, :] = split(right_ref[pl.ds(at, 128), :])
        mark_ref[...] = jnp.zeros((8, 128), f32)

    outs = [shape(1024, 1024, bf16), shape(1024, 1024, bf16), shape(8, 128)]
    *right, mark = call(kernel, "order_right", [order, right], outs, [SCALARS, WHOLE], after=after)
    return right, mark


def fill(refs, blocks, high, low):
    at = 0
    for ref, (_, begin, size) in zip(refs, blocks):
        high[at : at + size, :], low[at : at + size, :] = split(ref[begin : begin + size, :])
        at += size


def project_far(blocks, left, after=()):
    rows = sum(size for _, _, size in blocks)
    n = len(blocks)

    def kernel(*refs):
        l_refs, outs, (gh, gl) = refs[n : n + 4], refs[n + 4 : n + 6], refs[n + 6 :]
        fill(refs[:n], blocks, gh, gl)
        for h in range(2):
            for t in range(2):
                c = slice(t * 256, t * 256 + 256)
                outs[h][:, c] = dot3(gh[...], gl[...], l_refs[2 * h][2, :, c], l_refs[2 * h + 1][2, :, c])

    return call(
        kernel, "project_far", [*[b[0] for b in blocks], *left], [shape(rows, 512)] * 2, None, [pltpu.VMEM((rows, 1024), bf16)] * 2, after
    )


def project_near(blocks, left, near, far, begin, after=(), cost=1):
    rows = sum(size for _, _, size in blocks)
    n = len(blocks)

    def kernel(*refs):
        l_refs, more, outs, (gh, gl) = refs[n : n + 4], refs[n + 4 : n + 6], refs[n + 6 : n + 8], refs[n + 8 :]
        fill(refs[:n], blocks, gh, gl)
        for i, d in enumerate((1, 3)):
            for h in range(2):
                for t in range(2):
                    c = slice(t * 256, t * 256 + 256)
                    value = dot3(gh[...], gl[...], l_refs[2 * h][d, :, c], l_refs[2 * h + 1][d, :, c])
                    if h == i:
                        value = value + more[i][begin : begin + rows, c]
                    outs[i][:, h * 512 + t * 256 : h * 512 + t * 256 + 256] = value

    return call(
        kernel, "project_near", [*[b[0] for b in blocks], *left, near, far], [shape(rows, 1024)] * 2, None,
        [pltpu.VMEM((rows, 1024), bf16)] * 2, after, cost=cost,
    )


def project_own(blocks, left, up, down, after=(), cost=1):
    rows = sum(size for _, _, size in blocks)
    n = len(blocks)

    def kernel(*refs):
        l_refs, (up_ref, down_ref), outs, (gh, gl) = refs[n : n + 4], refs[n + 4 : n + 6], refs[n + 6 : n + 10], refs[n + 10 :]
        fill(refs[:n], blocks, gh, gl)
        for d in range(4):
            c = slice(d * 128, d * 128 + 128)
            high = jnp.concatenate([l_refs[0][0, :, c], l_refs[2][0, :, c]], axis=1)
            low = jnp.concatenate([l_refs[1][0, :, c], l_refs[3][0, :, c]], axis=1)
            value = dot3(gh[...], gl[...], high, low)
            for h in range(2):
                e = slice(h * 512 + d * 128, h * 512 + d * 128 + 128)
                outs[d][:, h * 128 : h * 128 + 128] = value[:, h * 128 : h * 128 + 128] + up_ref[:, e] + down_ref[:, e]

    return call(
        kernel, "project_own", [*[b[0] for b in blocks], *left, up, down], [shape(rows, 256)] * 4, None, [pltpu.VMEM((rows, 1024), bf16)] * 2,
        after, cost=cost,
    )


def rotate(parts, right, chips, before=None, last=False, after=()):
    n = 6 + (before is not None)

    def kernel(*refs):
        p, (rh, rl) = refs[:4], refs[4:6]
        total = (p[0][...] + p[1][...]) + (p[2][...] + p[3][...])
        high, low = split(total.T)
        places = [h * 512 + CHIPS.index(d) * 128 for d in chips for h in range(2)]
        for t in range(4):
            c = slice(t * 256, t * 256 + 256)
            r_high = jnp.concatenate([rh[p : p + 128, c] for p in places], axis=0)
            r_low = jnp.concatenate([rl[p : p + 128, c] for p in places], axis=0)
            value = dot3(high, low, r_high, r_low)
            if before is not None:
                value = value + refs[6][:, c]
            if last:
                refs[n][:, c] = value[:128]
                refs[n + 1][:, c] = value[128:]
            else:
                refs[n][:, c] = value

    out = call(
        kernel, "rotate", [*parts, *right] + ([before] if n > 6 else []), [shape(128, 1024)] * 2 if last else [shape(256, 1024)],
        after=after,
    )
    return out if last else out[0]


def turn(core, own, other, second, right):
    def kernel(core_ref, own_ref, other_ref, second_ref, rh, rl, new_ref, keep_ref, give_ref):
        zero = core_ref[0] == 0
        a, b = own_ref[...], other_ref[...]
        g, m = jnp.where(zero, a, b), jnp.where(zero, b, a)
        new = second_decay * second_ref[...] + (1.0 - second_decay) * g * g
        new_ref[...] = new
        rotated = m / (jnp.sqrt(new) + epsilon)
        high, low = split(rotated)
        squares = rotated * rotated
        total = squares[0:8, :]
        for i in range(1, 16):
            total = total + squares[i * 8 : i * 8 + 8, :]
        narrow = total[:, 0:128]
        for i in range(1, 8):
            narrow = narrow + total[:, i * 128 : i * 128 + 128]
        zeros = jnp.zeros((8, 128), f32)
        for out, h in ((give_ref, 1), (keep_ref, 0)):
            for t in range(2):
                r = slice(h * 512 + t * 256, h * 512 + t * 256 + 256)
                out[0:128, t * 256 : t * 256 + 256] = dot3(high, low, rh[r, :], rl[r, :], (((1,), (1,)), ((), ())))
            out[128:136, :] = jnp.concatenate([narrow, zeros, narrow, zeros], axis=1)

    return call(
        kernel, "turn", [core, own, other, second, *right], [shape(128, 1024), shape(136, 512), shape(136, 512)],
        [SCALARS] + [WHOLE] * 5,
    )


def back_project(terms, left, before=None, cut=False, after=(), cost=1):
    arrays = [a for _, group in terms for a in group]
    n = len(arrays)

    def kernel(*refs):
        l_refs = refs[n : n + 4]
        sh, sl = refs[-2:]
        outs = refs[n + 4 + (before is not None) : -2]
        at, index = 0, 0
        extra = refs[n + 4][1024:1032, :] if before is not None else jnp.zeros((8, 256), f32)
        for _, group in terms:
            size = 1024 // len(group)
            for _ in group:
                sh[at : at + size, :], sl[at : at + size, :] = split(refs[index][0:size, :])
                if refs[index].shape[0] > size:
                    extra = extra + refs[index][size : size + 8, :]
                at, index = at + size, index + 1
        for t in range(4):
            r = slice(t * 256, t * 256 + 256)
            value = refs[n + 4][r, :] if before is not None else None
            for i, (d, _) in enumerate(terms):
                for h in range(2):
                    rows = slice(i * 1024 + h * 512, i * 1024 + h * 512 + 512)
                    new = dot3(l_refs[2 * h][d, r, :], l_refs[2 * h + 1][d, r, :], sh[rows, :], sl[rows, :])
                    value = new if value is None else value + new
            if cut:
                outs[0][r, :] = value[:, :128]
                outs[1][r, :] = value[:, 128:]
            else:
                outs[0][r, :] = value
        if cut:
            outs[0][1024:1032, :] = extra[:, :128]
            outs[1][1024:1032, :] = extra[:, :128]
        else:
            outs[0][1024:1032, :] = extra

    out = call(
        kernel, "back_project", [*arrays, *left] + ([] if before is None else [before]),
        [shape(1032, 128)] * 2 if cut else [shape(1032, 256)], None, [pltpu.VMEM((1024 * len(terms), 256), bf16)] * 2, after,
        cost=cost,
    )
    return out if cut else out[0]


def finish(parts):
    def kernel(a, b, c, d, out):
        rows = slice(1024, 1032)
        squares = (a[rows, :] + b[rows, :]) + (c[rows, :] + d[rows, :])
        total = jnp.sum(jnp.sum(squares, axis=0, keepdims=True), axis=1, keepdims=True)
        factor = jnp.minimum(1.0, clip_share * math.sqrt(M * N) / (jnp.sqrt(total) + 1e-06))
        rows = slice(0, 1024)
        out[...] = ((a[rows, :] + b[rows, :]) + (c[rows, :] + d[rows, :])) * factor

    return call(kernel, "finish", list(parts), [shape(1024, 128)])[0]


def pack(keep, other):
    def kernel(keep_ref, other_ref, one, two):
        for out, c in ((one, slice(0, 256)), (two, slice(256, 512))):
            out[0, :, :] = keep_ref[:, c]
            out[1, :, :] = other_ref[:, c]

    return call(kernel, "pack", [keep, other], [jax.ShapeDtypeStruct((2, 136, 256), f32)] * 2)


def lay(shares, after=()):
    def kernel(*refs):
        out = refs[-1]
        extra = jnp.zeros((8, 256), f32)
        for d in range(4):
            for h in range(2):
                out[(h * 4 + d) * 128 : (h * 4 + d) * 128 + 128, :] = refs[d][h, 0:128, :]
                extra = extra + refs[d][h, 128:136, :]
        out[1024:1032, :] = extra

    return call(kernel, "lay", list(shares), [shape(1032, 256)], after=after)[0]


def forward(plus, minus, rows, others, after):
    def kernel(plus_ref, minus_ref, one, two):
        one[...] = plus_ref[rows[0] : rows[1], :]
        two[...] = minus_ref[others[0] : others[1], :]

    columns = plus.shape[1]
    outs = [shape(rows[1] - rows[0], columns), shape(others[1] - others[0], columns)]
    return call(kernel, "forward", [plus, minus], outs, after=after)


def sort(plus, minus, after):
    def kernel(plus_ref, minus_ref, keep, gives):
        keep[...] = plus_ref[0:128, :]
        gives[0:128, :] = plus_ref[128:256, :]
        gives[128:256, :] = minus_ref[128:256, :]

    return call(kernel, "sort", [plus, minus], [shape(128, 1024), shape(256, 1024)], after=after)


def tables():
    left = np.zeros((2, 16, 16), np.int32)
    right = np.zeros((8, 8), np.int32)
    for c in range(2):
        for y in range(4):
            for z in range(4):
                for a in range(4):
                    for b in range(4):
                        p, q = (y + a, z + b) if c == 0 else (y + b, z + a)
                        left[c, y * 4 + z, a * 4 + b] = p % 4 * 4 + q % 4
        for x in range(4):
            for h in range(2):
                for i, d in enumerate(CHIPS):
                    right[2 * x + c, h * 4 + i] = 2 * ((x + d) % 4) + (c + h) % 2
    return left, right


def local(grad, moment, second, left_basis, right_basis):
    row, col = lax.axis_index("row"), lax.axis_index("col")
    core = (row % 2).reshape(1).astype(jnp.int32)
    by_col, by_row = tables()
    order = jnp.asarray(by_col)[row % 2, col]
    order_r = jnp.asarray(by_row)[row]

    left_other = swap(left_basis)
    moment_new, both, give = start(core, grad, moment)
    plus, minus = along_x(both, -1), along_x(both, 1)
    moved = swap(give)
    right, mark = order_right(order_r, right_basis, (give,))
    left = order_left(order, left_basis, (), (mark,))
    left = [*left, *order_left(order, left_other, left)]

    one, two = project_far([(both, 0, 128), (moved, 0, 128)], left)
    keep, gives = sort(plus, minus, (one,))
    far_keep = along_x(keep, -1)
    others = swap(gives)
    far_moved = along_x(others[128:], 1)

    chips = [(0,), (1, 3), (2,)]
    blocks = [
        [(both, 0, 128), (moved, 0, 128)],
        [(plus, 0, 128), (others, 0, 128), (minus, 0, 128), (others, 128, 128)],
        [(far_keep, 0, 128), (far_moved, 0, 128)],
    ]

    def own_step(i, near, after, cost=1):
        q = project_own(blocks[i], left, *near, after, cost)
        return [q[0], second_axis(q[1], 1), second_axis(q[3], -1), second_axis(q[2], 2)]

    one, two = first(one, 1), first(two, -1)
    up, down = project_near(blocks[0], left, one, two, 0, (), LONG)
    near = first(up, 1), first(down, -1)
    one, two = project_far(blocks[1], left, (up,))
    more1 = first(one, 1), first(two, -1)
    parts = own_step(0, near, (one, far_keep, far_moved), LONG)
    one, two = project_far(blocks[2], left, (parts[0],))
    more2 = first(one, 1), first(two, -1)
    up1, down1 = project_near(blocks[1], left, *more1, 0, (one,))
    part = rotate(parts, right, chips[0], after=(up1,))
    up2, down2 = project_near(blocks[2], left, *more2, 0, (up1, part), LONG)
    near1 = first(up1, 1), first(down1, -1)
    near2 = first(up2, 1), first(down2, -1)
    parts1 = own_step(1, near1, (up2,))
    parts2 = own_step(2, near2, (parts1[0],))
    part = rotate(parts1, right, chips[1], part)
    part = rotate(parts2, right, chips[2], part, last=True)
    own, other = part
    other = swap(other)

    second_new, keep, give = turn(core, own, other, second, right)
    share_a, share_b = pack(keep, swap(give))

    def spread_share(share):
        return [share, second_axis(share, -1), second_axis(share, -2), second_axis(share, 1)]

    block_a = lay(spread_share(share_a))
    shares_b = spread_share(share_b)
    plus_a, minus_a = first(block_a, -1), first(block_a, 1)
    sums_a = back_project([(0, [block_a])], left, after=shares_b[1:])
    far_a1, far_a3 = forward(plus_a, minus_a, (0, 512), (512, 1032), (sums_a,))
    block_b = lay(shares_b, (far_a1,))
    far_a1, far_a3 = first(far_a1, -1), first(far_a3, 1)
    plus_b, minus_b = first(block_b, -1), first(block_b, 1)
    sums_a = back_project([(1, [plus_a]), (3, [minus_a])], left, sums_a, after=(block_b,))
    u1, u3 = back_project([(2, [far_a1, far_a3])], left, sums_a, cut=True)
    sums_b = back_project([(0, [block_b])], left, after=(u1,), cost=LONG)
    far_b1, far_b3 = forward(plus_b, minus_b, (0, 512), (512, 1032), (sums_b,))
    sums_b = back_project([(1, [plus_b]), (3, [minus_b])], left, sums_b, after=(far_b1,))
    far_b1, far_b3 = first(far_b1, -1), first(far_b3, 1)
    got1, got3 = along_x(u1, 1), along_x(u3, -1)
    u2, u0 = back_project([(2, [far_b1, far_b3])], left, sums_b, cut=True, after=(got1, got3))
    update = finish([u0, got1, got3, along_x(u2, 2)])
    return (update, moment_new, second_new)


def solution(mesh):
    return jax.shard_map(
        local,
        mesh=mesh,
        in_specs=(P("col", "row"), P("col", "row"), P(("row", "col"), None), P("col", "row"), P()),
        out_specs=(P("col", "row"), P("col", "row"), P(("row", "col"), None)),
        check_vma=False,
    )
```

```python
import functools
import math

import jax
import jax.numpy as jnp
import numpy as np
from jax import lax
from jax.experimental import pallas as pl
from jax.experimental.pallas import tpu as pltpu
from jax.sharding import PartitionSpec as P

M = 16384
N = 1024

first_decay = 0.9
second_decay = 0.95
epsilon = 1e-08
clip_share = 0.25

f32, bf16 = jnp.float32, jnp.bfloat16
BOTH = ("row", "col")
VMEM_LIMIT = 10 * 1024 * 1024
CHIPS = (1, 3, 2, 0)
LONG = 10**11
WHOLE = pl.BlockSpec(memory_space=pltpu.VMEM)
SCALARS = pl.BlockSpec(memory_space=pltpu.SMEM)
ANYWHERE = pl.BlockSpec(memory_space=pl.ANY)


def call(kernel, name, args, out_shape, specs=None, scratch=(), after=(), hold=(), cost=1):
    n, k = len(args), len(after) + len(hold)

    def body(*refs):
        kernel(*refs[:n], *refs[n + k :])

    return pl.pallas_call(
        body,
        in_specs=(specs or [WHOLE] * n) + [ANYWHERE] * len(after) + [WHOLE] * len(hold),
        out_specs=[WHOLE] * len(out_shape),
        out_shape=out_shape,
        scratch_shapes=list(scratch),
        compiler_params=pltpu.CompilerParams(vmem_limit_bytes=VMEM_LIMIT),
        cost_estimate=pl.CostEstimate(flops=cost, bytes_accessed=cost, transcendentals=0),
        name=name,
    )(*args, *after, *hold)


def shape(rows, columns, dtype=f32):
    return jax.ShapeDtypeStruct((rows, columns), dtype)


def split(value):
    high = value.astype(bf16)
    return high, (value - high.astype(f32)).astype(bf16)


def dot3(a_high, a_low, b_high, b_low, dims=(((1,), (0,)), ((), ()))):
    d = functools.partial(lax.dot_general, dimension_numbers=dims, preferred_element_type=f32)
    return d(a_high, b_high) + (d(a_high, b_low) + d(a_low, b_high))


def move(value, step):
    pairs = []
    for x in range(4):
        for c in range(2):
            for y in range(4):
                for z in range(4):
                    tx, tc, ty, tz = step(x, c, y, z)
                    pairs.append(((2 * x + c) * 16 + 4 * y + z, (2 * (tx % 4) + tc) * 16 + 4 * (ty % 4) + tz % 4))
    return lax.ppermute(value, BOTH, pairs)


def swap(value):
    return move(value, lambda x, c, y, z: (x, 1 - c, y, z))


def along_x(value, d):
    return move(value, lambda x, c, y, z: (x + d, c, y, z))


def first(value, d):
    return move(value, lambda x, c, y, z: (x, c, y + d, z) if c == 0 else (x, c, y, z + d))


def second_axis(value, d):
    return move(value, lambda x, c, y, z: (x, c, y, z + d) if c == 0 else (x, c, y + d, z))


def start(core, grad, moment):
    def kernel(core_ref, grad_ref, moment_ref, new_ref, both_ref, give_ref):
        g = grad_ref[...]
        new = first_decay * moment_ref[...] + (1.0 - first_decay) * g
        new_ref[...] = new
        g, new = g.T, new.T
        zero = core_ref[0] == 0
        both_ref[0:128, :] = jnp.where(zero, g, new)
        give = jnp.where(zero, new, g)
        both_ref[128:256, :] = give
        give_ref[...] = give

    return call(
        kernel, "start", [core, grad, moment], [shape(1024, 128), shape(256, 1024), shape(128, 1024)], [SCALARS, WHOLE, WHOLE]
    )


def order_left(order, left, hold=(), after=()):
    steps, slots = 8, 4

    def kernel(order_ref, left_ref, high_ref, low_ref, held, arrived):
        def copy(i):
            return pltpu.make_async_copy(left_ref.at[pl.ds(i * 128, 128), :], held.at[i % slots], arrived.at[i % slots])

        for i in range(slots):
            copy(i).start()
        for i in range(steps):
            copy(i).wait()
            rows = slice(i * 128, i * 128 + 128)
            for a in range(4):
                for b in range(4):
                    at = pl.multiple_of(order_ref[a * 4 + b] * 128, 128)
                    high, low = split(held[i % slots, :, pl.ds(at, 128)])
                    high_ref[a, rows, b * 128 : b * 128 + 128] = high
                    low_ref[a, rows, b * 128 : b * 128 + 128] = low
            if i + slots < steps:
                copy(i + slots).start()

    return call(
        kernel, "order_left", [order, left], [jax.ShapeDtypeStruct((4, 1024, 512), bf16)] * 2, [SCALARS, pl.BlockSpec(memory_space=pltpu.HBM)],
        [pltpu.VMEM((slots, 128, 2048), f32), pltpu.SemaphoreType.DMA((slots,))], after, hold,
    )


def order_right(order, right, after=()):
    def kernel(order_ref, right_ref, high_ref, low_ref, mark_ref):
        for i in range(8):
            at = pl.multiple_of(order_ref[i] * 128, 128)
            rows = slice(i * 128, i * 128 + 128)
            high_ref[rows, :], low_ref[rows, :] = split(right_ref[pl.ds(at, 128), :])
        mark_ref[...] = jnp.zeros((8, 128), f32)

    outs = [shape(1024, 1024, bf16), shape(1024, 1024, bf16), shape(8, 128)]
    *right, mark = call(kernel, "order_right", [order, right], outs, [SCALARS, WHOLE], after=after)
    return right, mark


def fill(refs, blocks, high, low):
    at = 0
    for ref, (_, begin, size) in zip(refs, blocks):
        high[at : at + size, :], low[at : at + size, :] = split(ref[begin : begin + size, :])
        at += size


def project_far(blocks, left, after=()):
    rows = sum(size for _, _, size in blocks)
    n = len(blocks)

    def kernel(*refs):
        l_refs, outs, gh, gl = refs[n : n + 4], refs[n + 4 : n + 6], refs[n + 6], refs[n + 7]
        fill(refs[:n], blocks, gh, gl)
        for h in range(2):
            for t in range(2):
                c = slice(t * 256, t * 256 + 256)
                outs[h][:, c] = dot3(gh[...], gl[...], l_refs[2 * h][2, :, c], l_refs[2 * h + 1][2, :, c])

    return call(
        kernel, "project_far", [*[b[0] for b in blocks], *left], [shape(rows, 512)] * 2 + [shape(rows, 1024, bf16)] * 2,
        after=after,
    )


def project_near(halves, left, near, far, begin, after=(), cost=1):
    rows = halves[0].shape[0]

    def kernel(*refs):
        (gh, gl), l_refs, more, outs = refs[:2], refs[2:6], refs[6:8], refs[8:]
        for i, d in enumerate((1, 3)):
            for h in range(2):
                for t in range(2):
                    c = slice(t * 256, t * 256 + 256)
                    value = dot3(gh[...], gl[...], l_refs[2 * h][d, :, c], l_refs[2 * h + 1][d, :, c])
                    if h == i:
                        value = value + more[i][begin : begin + rows, c]
                    outs[i][:, h * 512 + t * 256 : h * 512 + t * 256 + 256] = value

    return call(
        kernel, "project_near", [*halves, *left, near, far], [shape(rows, 1024)] * 2,
        after=after, cost=cost,
    )


def project_own(halves, left, up, down, after=(), cost=1):
    rows = halves[0].shape[0]

    def kernel(*refs):
        (gh, gl), l_refs, (up_ref, down_ref), outs = refs[:2], refs[2:6], refs[6:8], refs[8:]
        for d in range(4):
            c = slice(d * 128, d * 128 + 128)
            high = jnp.concatenate([l_refs[0][0, :, c], l_refs[2][0, :, c]], axis=1)
            low = jnp.concatenate([l_refs[1][0, :, c], l_refs[3][0, :, c]], axis=1)
            value = dot3(gh[...], gl[...], high, low)
            for h in range(2):
                e = slice(h * 512 + d * 128, h * 512 + d * 128 + 128)
                outs[d][:, h * 128 : h * 128 + 128] = value[:, h * 128 : h * 128 + 128] + up_ref[:, e] + down_ref[:, e]

    return call(
        kernel, "project_own", [*halves, *left, up, down], [shape(rows, 256)] * 4,
        after=after, cost=cost,
    )


def rotate(parts, right, chips, before=None, last=False, after=()):
    n = 6 + (before is not None)

    def kernel(*refs):
        p, (rh, rl) = refs[:4], refs[4:6]
        total = (p[0][...] + p[1][...]) + (p[2][...] + p[3][...])
        high, low = split(total.T)
        places = [h * 512 + CHIPS.index(d) * 128 for d in chips for h in range(2)]
        for t in range(4):
            c = slice(t * 256, t * 256 + 256)
            r_high = jnp.concatenate([rh[p : p + 128, c] for p in places], axis=0)
            r_low = jnp.concatenate([rl[p : p + 128, c] for p in places], axis=0)
            value = dot3(high, low, r_high, r_low)
            if before is not None:
                value = value + refs[6][:, c]
            if last:
                refs[n][:, c] = value[:128]
                refs[n + 1][:, c] = value[128:]
            else:
                refs[n][:, c] = value

    out = call(
        kernel, "rotate", [*parts, *right] + ([before] if n > 6 else []), [shape(128, 1024)] * 2 if last else [shape(256, 1024)],
        after=after,
    )
    return out if last else out[0]


def turn(core, own, other, second, right):
    def kernel(core_ref, own_ref, other_ref, second_ref, rh, rl, new_ref, keep_ref, give_ref):
        zero = core_ref[0] == 0
        a, b = own_ref[...], other_ref[...]
        g, m = jnp.where(zero, a, b), jnp.where(zero, b, a)
        new = second_decay * second_ref[...] + (1.0 - second_decay) * g * g
        new_ref[...] = new
        rotated = m / (jnp.sqrt(new) + epsilon)
        high, low = split(rotated)
        squares = rotated * rotated
        total = squares[0:8, :]
        for i in range(1, 16):
            total = total + squares[i * 8 : i * 8 + 8, :]
        narrow = total[:, 0:128]
        for i in range(1, 8):
            narrow = narrow + total[:, i * 128 : i * 128 + 128]
        zeros = jnp.zeros((8, 128), f32)
        for out, h in ((give_ref, 1), (keep_ref, 0)):
            for t in range(2):
                r = slice(h * 512 + t * 256, h * 512 + t * 256 + 256)
                out[0:128, t * 256 : t * 256 + 256] = dot3(high, low, rh[r, :], rl[r, :], (((1,), (1,)), ((), ())))
            out[128:136, :] = jnp.concatenate([narrow, zeros, narrow, zeros], axis=1)

    return call(
        kernel, "turn", [core, own, other, second, *right], [shape(128, 1024), shape(136, 512), shape(136, 512)],
        [SCALARS] + [WHOLE] * 5,
    )


def back_project(terms, left, before=None, cut=False, after=(), cost=1):
    arrays = [a for _, group in terms for a in group]
    n = len(arrays)

    def kernel(*refs):
        l_refs = refs[n : n + 4]
        sh, sl = refs[-2:]
        outs = refs[n + 4 + (before is not None) : -2]
        at, index = 0, 0
        extra = refs[n + 4][1024:1032, :] if before is not None else jnp.zeros((8, 256), f32)
        for _, group in terms:
            size = 1024 // len(group)
            for _ in group:
                sh[at : at + size, :], sl[at : at + size, :] = split(refs[index][0:size, :])
                if refs[index].shape[0] > size:
                    extra = extra + refs[index][size : size + 8, :]
                at, index = at + size, index + 1
        for t in range(4):
            r = slice(t * 256, t * 256 + 256)
            value = refs[n + 4][r, :] if before is not None else None
            for i, (d, _) in enumerate(terms):
                for h in range(2):
                    rows = slice(i * 1024 + h * 512, i * 1024 + h * 512 + 512)
                    new = dot3(l_refs[2 * h][d, r, :], l_refs[2 * h + 1][d, r, :], sh[rows, :], sl[rows, :])
                    value = new if value is None else value + new
            if cut:
                outs[0][r, :] = value[:, :128]
                outs[1][r, :] = value[:, 128:]
            else:
                outs[0][r, :] = value
        if cut:
            outs[0][1024:1032, :] = extra[:, :128]
            outs[1][1024:1032, :] = extra[:, :128]
        else:
            outs[0][1024:1032, :] = extra

    out = call(
        kernel, "back_project", [*arrays, *left] + ([] if before is None else [before]),
        [shape(1032, 128)] * 2 if cut else [shape(1032, 256)], None, [pltpu.VMEM((1024 * len(terms), 256), bf16)] * 2, after,
        cost=cost,
    )
    return out if cut else out[0]


def finish(parts):
    def kernel(a, b, c, d, out):
        rows = slice(1024, 1032)
        squares = (a[rows, :] + b[rows, :]) + (c[rows, :] + d[rows, :])
        total = jnp.sum(jnp.sum(squares, axis=0, keepdims=True), axis=1, keepdims=True)
        factor = jnp.minimum(1.0, clip_share * math.sqrt(M * N) / (jnp.sqrt(total) + 1e-06))
        rows = slice(0, 1024)
        out[...] = ((a[rows, :] + b[rows, :]) + (c[rows, :] + d[rows, :])) * factor

    return call(kernel, "finish", list(parts), [shape(1024, 128)])[0]


def pack(keep, other):
    def kernel(keep_ref, other_ref, one, two):
        for out, c in ((one, slice(0, 256)), (two, slice(256, 512))):
            out[0, :, :] = keep_ref[:, c]
            out[1, :, :] = other_ref[:, c]

    return call(kernel, "pack", [keep, other], [jax.ShapeDtypeStruct((2, 136, 256), f32)] * 2)


def lay(shares, after=()):
    def kernel(*refs):
        out = refs[-1]
        extra = jnp.zeros((8, 256), f32)
        for d in range(4):
            for h in range(2):
                out[(h * 4 + d) * 128 : (h * 4 + d) * 128 + 128, :] = refs[d][h, 0:128, :]
                extra = extra + refs[d][h, 128:136, :]
        out[1024:1032, :] = extra

    return call(kernel, "lay", list(shares), [shape(1032, 256)], after=after)[0]


def forward(plus, minus, rows, others, after):
    def kernel(plus_ref, minus_ref, one, two):
        one[...] = plus_ref[rows[0] : rows[1], :]
        two[...] = minus_ref[others[0] : others[1], :]

    columns = plus.shape[1]
    outs = [shape(rows[1] - rows[0], columns), shape(others[1] - others[0], columns)]
    return call(kernel, "forward", [plus, minus], outs, after=after)


def sort(plus, minus, after):
    def kernel(plus_ref, minus_ref, keep, gives):
        keep[...] = plus_ref[0:128, :]
        gives[0:128, :] = plus_ref[128:256, :]
        gives[128:256, :] = minus_ref[128:256, :]

    return call(kernel, "sort", [plus, minus], [shape(128, 1024), shape(256, 1024)], after=after)


def tables():
    left = np.zeros((2, 16, 16), np.int32)
    right = np.zeros((8, 8), np.int32)
    for c in range(2):
        for y in range(4):
            for z in range(4):
                for a in range(4):
                    for b in range(4):
                        p, q = (y + a, z + b) if c == 0 else (y + b, z + a)
                        left[c, y * 4 + z, a * 4 + b] = p % 4 * 4 + q % 4
        for x in range(4):
            for h in range(2):
                for i, d in enumerate(CHIPS):
                    right[2 * x + c, h * 4 + i] = 2 * ((x + d) % 4) + (c + h) % 2
    return left, right


def local(grad, moment, second, left_basis, right_basis):
    row, col = lax.axis_index("row"), lax.axis_index("col")
    core = (row % 2).reshape(1).astype(jnp.int32)
    by_col, by_row = tables()
    order = jnp.asarray(by_col)[row % 2, col]
    order_r = jnp.asarray(by_row)[row]

    left_other = swap(left_basis)
    moment_new, both, give = start(core, grad, moment)
    plus, minus = along_x(both, -1), along_x(both, 1)
    moved = swap(give)
    right, mark = order_right(order_r, right_basis, (give,))
    left = order_left(order, left_basis, (), (mark,))
    left = [*left, *order_left(order, left_other, left)]

    one, two, *mine = project_far([(both, 0, 128), (moved, 0, 128)], left)
    keep, gives = sort(plus, minus, (one,))
    far_keep = along_x(keep, -1)
    others = swap(gives)
    far_moved = along_x(others[128:], 1)

    def own_step(halves, near, after, cost=1):
        q = project_own(halves, left, *near, after, cost)
        return [q[0], second_axis(q[1], 1), second_axis(q[3], -1), second_axis(q[2], 2)]

    one, two = first(one, 1), first(two, -1)
    up, down = project_near(mine, left, one, two, 0, (), LONG)
    near = first(up, 1), first(down, -1)
    blocks = [(plus, 0, 128), (others, 0, 128), (minus, 0, 128), (others, 128, 128)]
    one, two, *beside = project_far(blocks, left, (up,))
    more1 = first(one, 1), first(two, -1)
    parts = own_step(mine, near, (one, far_keep, far_moved), LONG)
    one, two, *opposite = project_far([(far_keep, 0, 128), (far_moved, 0, 128)], left, (parts[0],))
    more2 = first(one, 1), first(two, -1)
    up1, down1 = project_near(beside, left, *more1, 0, (one,))
    part = rotate(parts, right, (0,), after=(up1,))
    up2, down2 = project_near(opposite, left, *more2, 0, (up1, part), LONG)
    near1 = first(up1, 1), first(down1, -1)
    near2 = first(up2, 1), first(down2, -1)
    parts1 = own_step(beside, near1, (up2,))
    parts2 = own_step(opposite, near2, (parts1[0],))
    part = rotate(parts1, right, (1, 3), part)
    part = rotate(parts2, right, (2,), part, last=True)
    own, other = part
    other = swap(other)

    second_new, keep, give = turn(core, own, other, second, right)
    share_a, share_b = pack(keep, swap(give))

    def spread_share(share):
        return [share, second_axis(share, -1), second_axis(share, -2), second_axis(share, 1)]

    block_a = lay(spread_share(share_a))
    shares_b = spread_share(share_b)
    plus_a, minus_a = first(block_a, -1), first(block_a, 1)
    sums_a = back_project([(0, [block_a])], left, after=shares_b[1:])
    far_a1, far_a3 = forward(plus_a, minus_a, (0, 512), (512, 1032), (sums_a,))
    block_b = lay(shares_b, (far_a1,))
    far_a1, far_a3 = first(far_a1, -1), first(far_a3, 1)
    plus_b, minus_b = first(block_b, -1), first(block_b, 1)
    sums_a = back_project([(1, [plus_a]), (3, [minus_a])], left, sums_a, after=(block_b,))
    u1, u3 = back_project([(2, [far_a1, far_a3])], left, sums_a, cut=True)
    sums_b = back_project([(0, [block_b])], left, after=(u1,), cost=LONG)
    far_b1, far_b3 = forward(plus_b, minus_b, (0, 512), (512, 1032), (sums_b,))
    got1, got3 = along_x(u1, 1), along_x(u3, -1)
    sums_b = back_project([(1, [plus_b]), (3, [minus_b])], left, sums_b, after=(far_b1, got1, got3), cost=LONG)
    far_b1, far_b3 = first(far_b1, -1), first(far_b3, 1)
    u2, u0 = back_project([(2, [far_b1, far_b3])], left, sums_b, cut=True)
    update = finish([u0, got1, got3, along_x(u2, 2)])
    return (update, moment_new, second_new)


def solution(mesh):
    return jax.shard_map(
        local,
        mesh=mesh,
        in_specs=(P("col", "row"), P("col", "row"), P(("row", "col"), None), P("col", "row"), P()),
        out_specs=(P("col", "row"), P("col", "row"), P(("row", "col"), None)),
        check_vma=False,
    )
```

```python
import functools
import math

import jax
import jax.numpy as jnp
import numpy as np
from jax import lax
from jax.experimental import pallas as pl
from jax.experimental.pallas import tpu as pltpu
from jax.sharding import PartitionSpec as P

M = 16384
N = 1024

first_decay = 0.9
second_decay = 0.95
epsilon = 1e-08
clip_share = 0.25

f32, bf16 = jnp.float32, jnp.bfloat16
BOTH = ("row", "col")
VMEM_LIMIT = 10 * 1024 * 1024
CHIPS = (1, 3, 2, 0)
LONG = 10**11
WHOLE = pl.BlockSpec(memory_space=pltpu.VMEM)
SCALARS = pl.BlockSpec(memory_space=pltpu.SMEM)
ANYWHERE = pl.BlockSpec(memory_space=pl.ANY)


def call(kernel, name, args, out_shape, specs=None, scratch=(), after=(), hold=(), cost=1):
    n, k = len(args), len(after) + len(hold)

    def body(*refs):
        kernel(*refs[:n], *refs[n + k :])

    return pl.pallas_call(
        body,
        in_specs=(specs or [WHOLE] * n) + [ANYWHERE] * len(after) + [WHOLE] * len(hold),
        out_specs=[WHOLE] * len(out_shape),
        out_shape=out_shape,
        scratch_shapes=list(scratch),
        compiler_params=pltpu.CompilerParams(vmem_limit_bytes=VMEM_LIMIT),
        cost_estimate=pl.CostEstimate(flops=cost, bytes_accessed=cost, transcendentals=0),
        name=name,
    )(*args, *after, *hold)


def shape(rows, columns, dtype=f32):
    return jax.ShapeDtypeStruct((rows, columns), dtype)


def split(value):
    high = value.astype(bf16)
    return high, (value - high.astype(f32)).astype(bf16)


def dot3(a_high, a_low, b_high, b_low, dims=(((1,), (0,)), ((), ()))):
    d = functools.partial(lax.dot_general, dimension_numbers=dims, preferred_element_type=f32)
    return d(a_high, b_high) + (d(a_high, b_low) + d(a_low, b_high))


def move(value, step):
    pairs = []
    for x in range(4):
        for c in range(2):
            for y in range(4):
                for z in range(4):
                    tx, tc, ty, tz = step(x, c, y, z)
                    pairs.append(((2 * x + c) * 16 + 4 * y + z, (2 * (tx % 4) + tc) * 16 + 4 * (ty % 4) + tz % 4))
    return lax.ppermute(value, BOTH, pairs)


def swap(value):
    return move(value, lambda x, c, y, z: (x, 1 - c, y, z))


def along_x(value, d):
    return move(value, lambda x, c, y, z: (x + d, c, y, z))


def first(value, d):
    return move(value, lambda x, c, y, z: (x, c, y + d, z) if c == 0 else (x, c, y, z + d))


def second_axis(value, d):
    return move(value, lambda x, c, y, z: (x, c, y, z + d) if c == 0 else (x, c, y + d, z))


def start(core, grad, moment):
    def kernel(core_ref, grad_ref, moment_ref, new_ref, both_ref, give_ref):
        g = grad_ref[...]
        new = first_decay * moment_ref[...] + (1.0 - first_decay) * g
        new_ref[...] = new
        g, new = g.T, new.T
        zero = core_ref[0] == 0
        both_ref[0:128, :] = jnp.where(zero, g, new)
        give = jnp.where(zero, new, g)
        both_ref[128:256, :] = give
        give_ref[...] = give

    return call(
        kernel, "start", [core, grad, moment], [shape(1024, 128), shape(256, 1024), shape(128, 1024)], [SCALARS, WHOLE, WHOLE]
    )


def order_left(order, left, hold=(), after=()):
    steps, slots = 8, 4

    def kernel(order_ref, left_ref, high_ref, low_ref, held, arrived):
        def copy(i):
            return pltpu.make_async_copy(left_ref.at[pl.ds(i * 128, 128), :], held.at[i % slots], arrived.at[i % slots])

        for i in range(slots):
            copy(i).start()
        for i in range(steps):
            copy(i).wait()
            rows = slice(i * 128, i * 128 + 128)
            for a in range(4):
                for b in range(4):
                    at = pl.multiple_of(order_ref[a * 4 + b] * 128, 128)
                    high, low = split(held[i % slots, :, pl.ds(at, 128)])
                    high_ref[a, rows, b * 128 : b * 128 + 128] = high
                    low_ref[a, rows, b * 128 : b * 128 + 128] = low
            if i + slots < steps:
                copy(i + slots).start()

    return call(
        kernel, "order_left", [order, left], [jax.ShapeDtypeStruct((4, 1024, 512), bf16)] * 2, [SCALARS, pl.BlockSpec(memory_space=pltpu.HBM)],
        [pltpu.VMEM((slots, 128, 2048), f32), pltpu.SemaphoreType.DMA((slots,))], after, hold,
    )


def order_right(order, right, after=()):
    def kernel(order_ref, right_ref, high_ref, low_ref, mark_ref):
        for i in range(8):
            at = pl.multiple_of(order_ref[i] * 128, 128)
            rows = slice(i * 128, i * 128 + 128)
            high_ref[rows, :], low_ref[rows, :] = split(right_ref[pl.ds(at, 128), :])
        mark_ref[...] = jnp.zeros((8, 128), f32)

    outs = [shape(1024, 1024, bf16), shape(1024, 1024, bf16), shape(8, 128)]
    *right, mark = call(kernel, "order_right", [order, right], outs, [SCALARS, WHOLE], after=after)
    return right, mark


def fill(refs, blocks, high, low):
    at = 0
    for ref, (_, begin, size) in zip(refs, blocks):
        high[at : at + size, :], low[at : at + size, :] = split(ref[begin : begin + size, :])
        at += size


def project_far(blocks, left, after=()):
    rows = sum(size for _, _, size in blocks)
    n = len(blocks)

    def kernel(*refs):
        l_refs, outs, gh, gl = refs[n : n + 4], refs[n + 4 : n + 6], refs[n + 6], refs[n + 7]
        fill(refs[:n], blocks, gh, gl)
        for h in range(2):
            for t in range(2):
                c = slice(t * 256, t * 256 + 256)
                outs[h][:, c] = dot3(gh[...], gl[...], l_refs[2 * h][2, :, c], l_refs[2 * h + 1][2, :, c])

    return call(
        kernel, "project_far", [*[b[0] for b in blocks], *left], [shape(rows, 512)] * 2 + [shape(rows, 1024, bf16)] * 2,
        after=after,
    )


def project_near(halves, left, near, far, begin, after=(), cost=1):
    rows = halves[0].shape[0]

    def kernel(*refs):
        (gh, gl), l_refs, more, outs = refs[:2], refs[2:6], refs[6:8], refs[8:]
        for i, d in enumerate((1, 3)):
            for h in range(2):
                for t in range(2):
                    c = slice(t * 256, t * 256 + 256)
                    value = dot3(gh[...], gl[...], l_refs[2 * h][d, :, c], l_refs[2 * h + 1][d, :, c])
                    if h == i:
                        value = value + more[i][begin : begin + rows, c]
                    outs[i][:, h * 512 + t * 256 : h * 512 + t * 256 + 256] = value

    return call(
        kernel, "project_near", [*halves, *left, near, far], [shape(rows, 1024)] * 2,
        after=after, cost=cost,
    )


def project_own(halves, left, up, down, after=(), cost=1):
    rows = halves[0].shape[0]

    def kernel(*refs):
        (gh, gl), l_refs, (up_ref, down_ref), outs = refs[:2], refs[2:6], refs[6:8], refs[8:]
        for d in range(4):
            c = slice(d * 128, d * 128 + 128)
            high = jnp.concatenate([l_refs[0][0, :, c], l_refs[2][0, :, c]], axis=1)
            low = jnp.concatenate([l_refs[1][0, :, c], l_refs[3][0, :, c]], axis=1)
            value = dot3(gh[...], gl[...], high, low)
            for h in range(2):
                e = slice(h * 512 + d * 128, h * 512 + d * 128 + 128)
                outs[d][:, h * 128 : h * 128 + 128] = value[:, h * 128 : h * 128 + 128] + up_ref[:, e] + down_ref[:, e]

    return call(
        kernel, "project_own", [*halves, *left, up, down], [shape(rows, 256)] * 4,
        after=after, cost=cost,
    )


def rotate(parts, right, chips, before=None, last=False, after=()):
    n = 6 + (before is not None)

    def kernel(*refs):
        p, (rh, rl) = refs[:4], refs[4:6]
        total = (p[0][...] + p[1][...]) + (p[2][...] + p[3][...])
        high, low = split(total.T)
        places = [h * 512 + CHIPS.index(d) * 128 for d in chips for h in range(2)]
        for t in range(4):
            c = slice(t * 256, t * 256 + 256)
            r_high = jnp.concatenate([rh[p : p + 128, c] for p in places], axis=0)
            r_low = jnp.concatenate([rl[p : p + 128, c] for p in places], axis=0)
            value = dot3(high, low, r_high, r_low)
            if before is not None:
                value = value + refs[6][:, c]
            if last:
                refs[n][:, c] = value[:128]
                refs[n + 1][:, c] = value[128:]
            else:
                refs[n][:, c] = value

    out = call(
        kernel, "rotate", [*parts, *right] + ([before] if n > 6 else []), [shape(128, 1024)] * 2 if last else [shape(256, 1024)],
        after=after,
    )
    return out if last else out[0]


def turn(core, own, other, second, right):
    def kernel(core_ref, own_ref, other_ref, second_ref, rh, rl, new_ref, keep_ref, give_ref):
        zero = core_ref[0] == 0
        a, b = own_ref[...], other_ref[...]
        g, m = jnp.where(zero, a, b), jnp.where(zero, b, a)
        new = second_decay * second_ref[...] + (1.0 - second_decay) * g * g
        new_ref[...] = new
        rotated = m / (jnp.sqrt(new) + epsilon)
        high, low = split(rotated)
        squares = rotated * rotated
        total = squares[0:8, :]
        for i in range(1, 16):
            total = total + squares[i * 8 : i * 8 + 8, :]
        narrow = total[:, 0:128]
        for i in range(1, 8):
            narrow = narrow + total[:, i * 128 : i * 128 + 128]
        zeros = jnp.zeros((8, 128), f32)
        for out, h in ((give_ref, 1), (keep_ref, 0)):
            for t in range(2):
                r = slice(h * 512 + t * 256, h * 512 + t * 256 + 256)
                out[0:128, t * 256 : t * 256 + 256] = dot3(high, low, rh[r, :], rl[r, :], (((1,), (1,)), ((), ())))
            out[128:136, :] = jnp.concatenate([narrow, zeros, narrow, zeros], axis=1)

    return call(
        kernel, "turn", [core, own, other, second, *right], [shape(128, 1024), shape(136, 512), shape(136, 512)],
        [SCALARS] + [WHOLE] * 5,
    )


def back_project(terms, left, before=None, cut=False, after=(), cost=1):
    arrays = [a for _, group in terms for a in group]
    n = len(arrays)

    def kernel(*refs):
        l_refs = refs[n : n + 4]
        sh, sl = refs[-2:]
        outs = refs[n + 4 + (before is not None) : -2]
        at, index = 0, 0
        extra = refs[n + 4][1024:1032, :] if before is not None else jnp.zeros((8, 256), f32)
        for _, group in terms:
            size = 1024 // len(group)
            for _ in group:
                sh[at : at + size, :], sl[at : at + size, :] = split(refs[index][0:size, :])
                if refs[index].shape[0] > size:
                    extra = extra + refs[index][size : size + 8, :]
                at, index = at + size, index + 1
        for t in range(4):
            r = slice(t * 256, t * 256 + 256)
            value = refs[n + 4][r, :] if before is not None else None
            for i, (d, _) in enumerate(terms):
                for h in range(2):
                    rows = slice(i * 1024 + h * 512, i * 1024 + h * 512 + 512)
                    new = dot3(l_refs[2 * h][d, r, :], l_refs[2 * h + 1][d, r, :], sh[rows, :], sl[rows, :])
                    value = new if value is None else value + new
            if cut:
                outs[0][r, :] = value[:, :128]
                outs[1][r, :] = value[:, 128:]
            else:
                outs[0][r, :] = value
        if cut:
            outs[0][1024:1032, :] = extra[:, :128]
            outs[1][1024:1032, :] = extra[:, :128]
        else:
            outs[0][1024:1032, :] = extra

    out = call(
        kernel, "back_project", [*arrays, *left] + ([] if before is None else [before]),
        [shape(1032, 128)] * 2 if cut else [shape(1032, 256)], None, [pltpu.VMEM((1024 * len(terms), 256), bf16)] * 2, after,
        cost=cost,
    )
    return out if cut else out[0]


def finish(parts):
    def kernel(a, b, c, d, out):
        rows = slice(1024, 1032)
        squares = (a[rows, :] + b[rows, :]) + (c[rows, :] + d[rows, :])
        total = jnp.sum(jnp.sum(squares, axis=0, keepdims=True), axis=1, keepdims=True)
        factor = jnp.minimum(1.0, clip_share * math.sqrt(M * N) / (jnp.sqrt(total) + 1e-06))
        rows = slice(0, 1024)
        out[...] = ((a[rows, :] + b[rows, :]) + (c[rows, :] + d[rows, :])) * factor

    return call(kernel, "finish", list(parts), [shape(1024, 128)])[0]


def pack(keep, other):
    def kernel(keep_ref, other_ref, one, two):
        for out, c in ((one, slice(0, 256)), (two, slice(256, 512))):
            out[0, :, :] = keep_ref[:, c]
            out[1, :, :] = other_ref[:, c]

    return call(kernel, "pack", [keep, other], [jax.ShapeDtypeStruct((2, 136, 256), f32)] * 2)


def lay(shares, after=()):
    def kernel(*refs):
        out = refs[-1]
        extra = jnp.zeros((8, 256), f32)
        for d in range(4):
            for h in range(2):
                out[(h * 4 + d) * 128 : (h * 4 + d) * 128 + 128, :] = refs[d][h, 0:128, :]
                extra = extra + refs[d][h, 128:136, :]
        out[1024:1032, :] = extra

    return call(kernel, "lay", list(shares), [shape(1032, 256)], after=after)[0]


def forward(plus, minus, rows, others, after):
    def kernel(plus_ref, minus_ref, one, two):
        one[...] = plus_ref[rows[0] : rows[1], :]
        two[...] = minus_ref[others[0] : others[1], :]

    columns = plus.shape[1]
    outs = [shape(rows[1] - rows[0], columns), shape(others[1] - others[0], columns)]
    return call(kernel, "forward", [plus, minus], outs, after=after)


def sort(plus, minus, after):
    def kernel(plus_ref, minus_ref, keep, gives):
        keep[...] = plus_ref[0:128, :]
        gives[0:128, :] = plus_ref[128:256, :]
        gives[128:256, :] = minus_ref[128:256, :]

    return call(kernel, "sort", [plus, minus], [shape(128, 1024), shape(256, 1024)], after=after)


def tables():
    left = np.zeros((2, 16, 16), np.int32)
    right = np.zeros((8, 8), np.int32)
    for c in range(2):
        for y in range(4):
            for z in range(4):
                for a in range(4):
                    for b in range(4):
                        p, q = (y + a, z + b) if c == 0 else (y + b, z + a)
                        left[c, y * 4 + z, a * 4 + b] = p % 4 * 4 + q % 4
        for x in range(4):
            for h in range(2):
                for i, d in enumerate(CHIPS):
                    right[2 * x + c, h * 4 + i] = 2 * ((x + d) % 4) + (c + h) % 2
    return left, right


def local(grad, moment, second, left_basis, right_basis):
    row, col = lax.axis_index("row"), lax.axis_index("col")
    core = (row % 2).reshape(1).astype(jnp.int32)
    by_col, by_row = tables()
    order = jnp.asarray(by_col)[row % 2, col]
    order_r = jnp.asarray(by_row)[row]

    left_other = swap(left_basis)
    moment_new, both, give = start(core, grad, moment)
    plus, minus = along_x(both, -1), along_x(both, 1)
    moved = swap(give)
    right, mark = order_right(order_r, right_basis, (give,))
    left = order_left(order, left_basis, (), (mark,))
    left = [*left, *order_left(order, left_other, left)]

    one, two, *mine = project_far([(both, 0, 128), (moved, 0, 128)], left)
    keep, gives = sort(plus, minus, (one,))
    far_keep = along_x(keep, -1)
    others = swap(gives)
    far_moved = along_x(others[128:], 1)

    def own_step(halves, near, after, cost=1):
        q = project_own(halves, left, *near, after, cost)
        return [q[0], second_axis(q[1], 1), second_axis(q[3], -1), second_axis(q[2], 2)]

    one, two = first(one, 1), first(two, -1)
    up, down = project_near(mine, left, one, two, 0, (), LONG)
    near = first(up, 1), first(down, -1)
    blocks = [(plus, 0, 128), (others, 0, 128), (minus, 0, 128), (others, 128, 128)]
    one, two, *beside = project_far(blocks, left, (up,))
    more1 = first(one, 1), first(two, -1)
    parts = own_step(mine, near, (one, far_keep, far_moved), LONG)
    one, two, *opposite = project_far([(far_keep, 0, 128), (far_moved, 0, 128)], left, (parts[0],))
    more2 = first(one, 1), first(two, -1)
    up1, down1 = project_near(beside, left, *more1, 0, (one,))
    up2, down2 = project_near(opposite, left, *more2, 0, (up1,), LONG)
    part = rotate(parts, right, (0,), after=(up2,))
    near1 = first(up1, 1), first(down1, -1)
    near2 = first(up2, 1), first(down2, -1)
    parts1 = own_step(beside, near1, (up2,))
    parts2 = own_step(opposite, near2, (parts1[0],))
    part = rotate(parts1, right, (1, 3), part)
    part = rotate(parts2, right, (2,), part, last=True)
    own, other = part
    other = swap(other)

    second_new, keep, give = turn(core, own, other, second, right)
    share_a, share_b = pack(keep, swap(give))

    def spread_share(share):
        return [share, second_axis(share, -1), second_axis(share, -2), second_axis(share, 1)]

    block_a = lay(spread_share(share_a))
    shares_b = spread_share(share_b)
    plus_a, minus_a = first(block_a, -1), first(block_a, 1)
    sums_a = back_project([(0, [block_a])], left, after=shares_b[1:])
    far_a1, far_a3 = forward(plus_a, minus_a, (0, 512), (512, 1032), (sums_a,))
    block_b = lay(shares_b, (far_a1,))
    far_a1, far_a3 = first(far_a1, -1), first(far_a3, 1)
    plus_b, minus_b = first(block_b, -1), first(block_b, 1)
    sums_a = back_project([(1, [plus_a]), (3, [minus_a])], left, sums_a, after=(block_b,))
    u1, u3 = back_project([(2, [far_a1, far_a3])], left, sums_a, cut=True)
    sums_b = back_project([(0, [block_b])], left, after=(u1,), cost=LONG)
    far_b1, far_b3 = forward(plus_b, minus_b, (0, 512), (512, 1032), (sums_b,))
    got1, got3 = along_x(u1, 1), along_x(u3, -1)
    sums_b = back_project([(1, [plus_b]), (3, [minus_b])], left, sums_b, after=(far_b1, got1, got3), cost=LONG)
    far_b1, far_b3 = first(far_b1, -1), first(far_b3, 1)
    u2, u0 = back_project([(2, [far_b1, far_b3])], left, sums_b, cut=True)
    update = finish([u0, got1, got3, along_x(u2, 2)])
    return (update, moment_new, second_new)


def solution(mesh):
    return jax.shard_map(
        local,
        mesh=mesh,
        in_specs=(P("col", "row"), P("col", "row"), P(("row", "col"), None), P("col", "row"), P()),
        out_specs=(P("col", "row"), P("col", "row"), P(("row", "col"), None)),
        check_vma=False,
    )
```
